32 devices in a mesh: batch: 16 (over z, y, x), tower: 2 (over core).
Axes of the slice: x: 2, y: 2, z: 4, core: 2. Of those that a mesh axis runs over, the one named last changes fastest.
Arguments:
- crop_maps: bfloat16 [512, 2, 13, 13, 384], P(('batch', 'tower')), may hold values from -6 to 6
- cotangent: bfloat16 [512, 2, 4096], P('batch', None, 'tower'), may hold values from -48 to 48
- crop_counts: int32 [256], P('batch'), may hold values from 1 to 2, as said below
- filter_weight: float32 [6912, 256], P(('batch', 'tower')), may hold values from -0.109375 to 0.109375
- filter_first: float32 [6912, 256], P(('batch', 'tower')), may hold values from -640 to 640
- filter_second: float32 [6912, 256], P(('batch', 'tower')), may hold values from 13652.503 to 54610.01
- conv_filter_bias: float32 [512], P(('batch', 'tower')), may hold values from -0.625 to 0.625
- conv_filter_bias_mean: float32 [512], P(('batch', 'tower')), may hold values from -640 to 640
- conv_filter_bias_variance: float32 [512], P(('batch', 'tower')), may hold values from 13652.503 to 54610.01
- pool_stitch: float32 [1024], P(('batch', 'tower')), may hold values from 0.15 to 1
- pool_stitch_first: float32 [1024], P(('batch', 'tower')), may hold values from -1280 to 1280
- pool_stitch_second: float32 [1024], P(('batch', 'tower')), may hold values from 55296 to 221184
- dense_weight: float32 [2, 9216, 4096], P('tower', 'batch'), may hold values from -0.125 to 0.125
- dense_weight_first: float32 [2, 9216, 4096], P('tower', 'batch'), may hold values from -160 to 160
- dense_weight_second: float32 [2, 9216, 4096], P('tower', 'batch'), may hold values from 864 to 3456
- dense_bias: float32 [2, 4096], P('tower'), may hold values from -0.625 to 0.625
- dense_bias_first: float32 [2, 4096], P('tower'), may hold values from -512 to 512
- dense_bias_second: float32 [2, 4096], P('tower'), may hold values from 7104 to 28416
- dense_stitch: float32 [2, 2, 4096], P(None, None, 'tower'), may hold values from 0.15 to 1
- dense_stitch_first: float32 [2, 2, 4096], P(None, None, 'tower'), may hold values from -448 to 448
- dense_stitch_second: float32 [2, 2, 4096], P(None, None, 'tower'), may hold values from 4992 to 19968
Outputs:
- stitched: bfloat16 [512, 2, 4096], P('batch', None, 'tower')
- input_grad: bfloat16 [512, 2, 13, 13, 384], P(('batch', 'tower'))
- new_filter_weight: float32 [6912, 256], P(('batch', 'tower'))
- new_filter_first: float32 [6912, 256], P(('batch', 'tower'))
- new_filter_second: float32 [6912, 256], P(('batch', 'tower'))
- filter_copy: bfloat16 [6912, 256], P(('batch', 'tower'))
- new_filter_bias: float32 [512], P(('batch', 'tower'))
- new_filter_bias_first: float32 [512], P(('batch', 'tower'))
- new_filter_bias_second: float32 [512], P(('batch', 'tower'))
- new_pool_stitch: float32 [1024], P(('batch', 'tower'))
- new_pool_stitch_first: float32 [1024], P(('batch', 'tower'))
- new_pool_stitch_second: float32 [1024], P(('batch', 'tower'))
- new_dense_weight: float32 [2, 9216, 4096], P('tower', 'batch')
- new_dense_first: float32 [2, 9216, 4096], P('tower', 'batch')
- new_dense_second: float32 [2, 9216, 4096], P('tower', 'batch')
- dense_copy: bfloat16 [2, 9216, 4096], P('tower', 'batch')
- new_dense_bias: float32 [2, 4096], P('tower')
- new_dense_bias_first: float32 [2, 4096], P('tower')
- new_dense_bias_second: float32 [2, 4096], P('tower')
- new_dense_stitch: float32 [2, 2, 4096], P(None, None, 'tower')
- new_dense_stitch_first: float32 [2, 2, 4096], P(None, None, 'tower')
- new_dense_stitch_second: float32 [2, 2, 4096], P(None, None, 'tower')
The draws below stay inside these ranges and needn't reach their ends.
Inputs may be any that keep to these rules, and one draw needn't show every extreme that they name: `crop_counts`: block b of 16 crop slots holds the crops of images b * 8 to b * 8 + 7 in order, then empty slots; in every draw some block is full.
All inputs are finite; a program needn't handle non-finite values.
Results may differ from the reference program's by a relative error of at most 0.0093.
Values may be sent and summed in bfloat16 or wider, within the bound.
No kernel may reach another device: no remote copies, remote signals or barrier semaphores. Data moves between devices by JAX's collectives and lax.ppermute only.
A program may use at most 448 MiB of HBM per device.

```python
import math
import jax
import jax.numpy as jnp
from jax import lax

CIN = 384
CO = 256
FC = 4096
SIDE = 13
CROPS_DEV = 16
IMG_DEV = 8
STEP = 10
POOL = 6
FEAT = 9216
MAXC = 2
CROPS = 512
IMAGES = 256
DEVICES = 32


def stitch_table(key, channels):
    values = jax.random.uniform(key, (2, 2, channels), jnp.float32)
    diagonal = jnp.eye(2, dtype=jnp.float32)[:, :, None]
    return diagonal * (0.7 + 0.3 * values) + (1.0 - diagonal) * (0.15 + 0.25 * values)


def draw_crop_counts(key, part):
    key = jax.random.fold_in(key, 11)
    first_key, second_key = jax.random.split(key)
    counts = jax.random.randint(first_key, (IMAGES,), 1, MAXC + 1)
    chosen = jax.random.randint(second_key, (), 0, IMAGES // IMG_DEV)
    blocks = jnp.arange(IMAGES) // IMG_DEV
    return jnp.where(blocks == chosen, MAXC, counts).astype(jnp.int32)


def draw_pool_stitch(key, part):
    key = jax.random.fold_in(key, 12)
    return stitch_table(key, CO).reshape(4 * CO)


def draw_dense_stitch(key, part):
    key = jax.random.fold_in(key, 13)
    return stitch_table(key, FC)


def block_scale(own_key, extent, cuts, smallest, top_value):
    gain, own = 1.0, jax.random.fold_in(own_key, 6)
    for dim, shards_of in cuts:
        heights = jnp.exp(jax.random.uniform(jax.random.fold_in(own, dim), (shards_of,), jnp.float32, smallest / len(cuts), top_value / len(cuts)))
        gain = gain * jnp.repeat(heights, extent[dim] // shards_of).reshape([-1 if axis == dim else 1 for axis in range(len(extent))])
    return gain


def bell_draw(stream_key, extent, scale, limit, cuts=(), kind=jnp.bfloat16):
    factor_of = block_scale(stream_key, extent, cuts, -0.22, 0.18) if cuts else 1.0
    entries = jax.random.normal(stream_key, extent, jnp.float32) * scale * factor_of
    return jnp.minimum(jnp.maximum(entries, -limit), limit).astype(kind)


def setup_inputs(seed: int = 0) -> dict:
    key_list = jax.random.split(jax.random.key(seed), 22)
    crop_maps = bell_draw(key_list[0], (CROPS, 2, SIDE, SIDE, CIN), 1.0, 6.0, ((0, 32),))
    cotangent = bell_draw(key_list[1], (CROPS, 2, FC), 8.0, 48.0, ((0, 16), (2, 2)))
    crop_counts = draw_crop_counts(jax.random.fold_in(key_list[21], 71), 0)
    filter_weight = bell_draw(key_list[3], (18 * CIN, CO), (9 * CIN) ** -0.5, 0.109375, ((0, 32),), jnp.float32)
    filter_first = bell_draw(key_list[4], (18 * CIN, CO), (0.688 * SIDE * FC ** 0.5 * FEAT ** -0.5 * (DEVICES * IMG_DEV * (MAXC + 1) // 2) ** 0.5), 640.0, ((0, 32),), jnp.float32)
    filter_second = jnp.clip(jnp.exp(math.log(54610.01) - 1.3862944 * jax.random.uniform(key_list[5], (18 * CIN, CO), jnp.float32) ** block_scale(key_list[5], (18 * CIN, CO), ((0, 32),), -0.2, 0.2)), 13652.503, 54610.01)
    conv_filter_bias = bell_draw(key_list[6], (2 * CO,), 0.1, 0.625, ((0, 32),), jnp.float32)
    conv_filter_bias_mean = bell_draw(key_list[7], (2 * CO,), (0.688 * SIDE * FC ** 0.5 * FEAT ** -0.5 * (DEVICES * IMG_DEV * (MAXC + 1) // 2) ** 0.5), 640.0, ((0, 32),), jnp.float32)
    conv_filter_bias_variance = jnp.clip(jnp.exp(math.log(54610.01) - 1.3862944 * jax.random.uniform(key_list[8], (2 * CO,), jnp.float32) ** block_scale(key_list[8], (2 * CO,), ((0, 32),), -0.2, 0.2)), 13652.503, 54610.01)
    pool_stitch = draw_pool_stitch(jax.random.fold_in(key_list[21], 71), 0)
    pool_stitch_first = bell_draw(key_list[10], (4 * CO,), (3.0 * POOL * FC ** 0.5 * FEAT ** -0.5 * (DEVICES * IMG_DEV * (MAXC + 1) // 2) ** 0.5), 1280.0, ((0, 32),), jnp.float32)
    pool_stitch_second = jnp.clip(jnp.exp(math.log(221184.0) - 1.3862944 * jax.random.uniform(key_list[11], (4 * CO,), jnp.float32) ** block_scale(key_list[11], (4 * CO,), ((0, 32),), -0.2, 0.2)), 55296.0, 221184.0)
    dense_weight = bell_draw(key_list[12], (2, FEAT, FC), (FEAT // 4) ** -0.5, 0.125, ((0, 2), (1, 16)), jnp.float32)
    dense_weight_first = bell_draw(key_list[13], (2, FEAT, FC), (1.5 * (DEVICES * IMG_DEV * (MAXC + 1) // 2) ** 0.5), 160.0, ((0, 2), (1, 16)), jnp.float32)
    dense_weight_second = jnp.clip(jnp.exp(math.log(3456.0) - 1.3862944 * jax.random.uniform(key_list[14], (2, FEAT, FC), jnp.float32) ** block_scale(key_list[14], (2, FEAT, FC), ((0, 2), (1, 16)), -0.2, 0.2)), 864.0, 3456.0)
    dense_bias = bell_draw(key_list[15], (2, FC), 0.1, 0.625, ((0, 2),), jnp.float32)
    dense_bias_first = bell_draw(key_list[16], (2, FC), (4.3 * (DEVICES * IMG_DEV * (MAXC + 1) // 2) ** 0.5), 512.0, ((0, 2),), jnp.float32)
    dense_bias_second = jnp.clip(jnp.exp(math.log(28416.0) - 1.3862944 * jax.random.uniform(key_list[17], (2, FC), jnp.float32) ** block_scale(key_list[17], (2, FC), ((0, 2),), -0.2, 0.2)), 7104.0, 28416.0)
    dense_stitch = draw_dense_stitch(jax.random.fold_in(key_list[21], 71), 0)
    dense_stitch_first = bell_draw(key_list[19], (2, 2, FC), (3.6 * (DEVICES * IMG_DEV * (MAXC + 1) // 2) ** 0.5), 448.0, ((2, 2),), jnp.float32)
    dense_stitch_second = jnp.clip(jnp.exp(math.log(19968.0) - 1.3862944 * jax.random.uniform(key_list[20], (2, 2, FC), jnp.float32) ** block_scale(key_list[20], (2, 2, FC), ((2, 2),), -0.2, 0.2)), 4992.0, 19968.0)
    return dict(crop_maps=crop_maps, cotangent=cotangent, crop_counts=crop_counts, filter_weight=filter_weight, filter_first=filter_first, filter_second=filter_second, conv_filter_bias=conv_filter_bias, conv_filter_bias_mean=conv_filter_bias_mean, conv_filter_bias_variance=conv_filter_bias_variance, pool_stitch=pool_stitch, pool_stitch_first=pool_stitch_first, pool_stitch_second=pool_stitch_second, dense_weight=dense_weight, dense_weight_first=dense_weight_first, dense_weight_second=dense_weight_second, dense_bias=dense_bias, dense_bias_first=dense_bias_first, dense_bias_second=dense_bias_second, dense_stitch=dense_stitch, dense_stitch_first=dense_stitch_first, dense_stitch_second=dense_stitch_second)


@jax.custom_vjp
def low(v):
    return lax.optimization_barrier(v.astype(jnp.bfloat16)).astype(jnp.float32)

@jax.custom_vjp
def low_back(v):
    return v

def low_keep(v):
    return (low(v), None)

def low_pass(kept, grad):
    return (grad,)

def back_keep(v):
    return (v, None)

def back_low(kept, grad):
    return (low(grad),)
low.defvjp(low_keep, low_pass)
low_back.defvjp(back_keep, back_low)
BETA_ONE = 0.5
BETA_TWO = 0.5
EPSILON = 1e-08
DECAY = 0.01
RATE_FILTER = 0.02
RATE_DENSE = 0.02
BIAS_LEARN_RATE = 0.05
RATE_STITCH = 0.2

def smooth_gate(values):
    return jax.nn.gelu(values, approximate=True)

def stitch_mix(weights, values):
    extra = values.ndim - 3
    shaped = weights.reshape((1, 2, 2) + (1,) * extra + (weights.shape[-1],))
    return lax.optimization_barrier(jnp.sum(shaped * values[:, None], axis=2))

def pool_mean(active):
    pooled_side = (active.shape[2] - 1) // 2
    total = jnp.zeros(active.shape[:2] + (pooled_side, pooled_side, active.shape[4]), jnp.float32)
    for offset in range(9):
        row_start = offset // 3
        col_start = offset % 3
        total = total + active[:, :, row_start:row_start + 2 * pooled_side - 1:2, col_start:col_start + 2 * pooled_side - 1:2, :]
    return total / 9.0

def filter_apply(block, filters, biases):
    padded = jnp.pad(block, ((0, 0), (0, 0), (1, 1), (1, 1), (0, 0)))
    total = jnp.zeros(block.shape[:4] + (CO,), jnp.float32)
    for offset in range(9):
        row_start = offset // 3
        col_start = offset % 3
        window = padded[:, :, row_start:row_start + SIDE, col_start:col_start + SIDE, :]
        total = total + jnp.einsum('ntyxc,tco->ntyxo', window, filters[:, offset], precision=lax.Precision.HIGHEST)
    return total + biases[None, :, None, None, :]

def crop_mask(crop_counts):
    totals = lax.optimization_barrier(jnp.sum(crop_counts.reshape(-1, IMG_DEV), axis=1))
    slots = jnp.arange(CROPS_DEV, dtype=jnp.int32)
    return (slots[None, :] < totals[:, None]).astype(jnp.float32).reshape(-1)

def forward(filter_weight, conv_filter_bias, pool_stitch, dense_weight, dense_bias, dense_stitch, crop_maps, mask):
    filters = low(filter_weight).reshape(2, 9, CIN, CO)
    biases = low(conv_filter_bias).reshape(2, CO)
    pool_low = low(pool_stitch).reshape(2, 2, CO)

    def block_features(block):
        conv = low_back(filter_apply(block, filters, biases))
        pooled = pool_mean(smooth_gate(conv))
        mixed = low(low_back(stitch_mix(pool_low, pooled)))
        return mixed.reshape(block.shape[0], 2, FEAT)
    blocks = crop_maps.reshape(CROPS // CROPS_DEV, CROPS_DEV, 2, SIDE, SIDE, CIN)
    features = lax.map(jax.checkpoint(block_features), blocks).reshape(CROPS, 2, FEAT)
    hidden = jnp.einsum('ntf,tfu->ntu', features, low(dense_weight), precision=lax.Precision.HIGHEST) + dense_bias[None]
    active = low(low_back(smooth_gate(low_back(hidden))))
    return stitch_mix(dense_stitch, active) * mask[:, None, None]

def decoupled_adam_step(master, first, second, grad, rate, decay):
    first_new = BETA_ONE * first + (1.0 - BETA_ONE) * grad
    second_new = BETA_TWO * second + (1.0 - BETA_TWO) * grad * grad
    first_hat = first_new / (1.0 - BETA_ONE ** STEP)
    second_hat = second_new / (1.0 - BETA_TWO ** STEP)
    master_new = master - rate * (first_hat / (jnp.sqrt(second_hat) + EPSILON) + decay * master)
    return (master_new, first_new, second_new)

def reference(crop_maps, cotangent, crop_counts, filter_weight, filter_first, filter_second, conv_filter_bias, conv_filter_bias_mean, conv_filter_bias_variance, pool_stitch, pool_stitch_first, pool_stitch_second, dense_weight, dense_weight_first, dense_weight_second, dense_bias, dense_bias_first, dense_bias_second, dense_stitch, dense_stitch_first, dense_stitch_second):
    mask = crop_mask(crop_counts)

    def closed(filter_arg, bias_arg, pool_arg, dense_arg, dbias_arg, dstitch_arg, maps_arg):
        return forward(filter_arg, bias_arg, pool_arg, dense_arg, dbias_arg, dstitch_arg, maps_arg, mask)
    update_outcome, pullback = jax.vjp(closed, filter_weight, conv_filter_bias, pool_stitch, dense_weight, dense_bias, dense_stitch, crop_maps.astype(jnp.float32))
    gradient_tuple = pullback(cotangent.astype(jnp.float32))
    updated_conv_weight, updated_conv_weight_mean, updated_conv_weight_variance = decoupled_adam_step(filter_weight, filter_first, filter_second, gradient_tuple[0], RATE_FILTER, DECAY)
    updated_conv_bias, updated_conv_bias_mean, updated_conv_bias_variance = decoupled_adam_step(conv_filter_bias, conv_filter_bias_mean, conv_filter_bias_variance, gradient_tuple[1], BIAS_LEARN_RATE, 0.0)
    updated_pooling_stitch, updated_pooling_stitch_mean, updated_pooling_stitch_variance = decoupled_adam_step(pool_stitch, pool_stitch_first, pool_stitch_second, gradient_tuple[2], RATE_STITCH, 0.0)
    updated_dense_weight, updated_dense_weight_mean, updated_dense_weight_variance = decoupled_adam_step(dense_weight, dense_weight_first, dense_weight_second, gradient_tuple[3], RATE_DENSE, DECAY)
    updated_dense_bias, updated_dense_bias_mean, updated_dense_bias_variance = decoupled_adam_step(dense_bias, dense_bias_first, dense_bias_second, gradient_tuple[4], BIAS_LEARN_RATE, 0.0)
    updated_dense_stitch, updated_dense_stitch_mean, updated_dense_stitch_variance = decoupled_adam_step(dense_stitch, dense_stitch_first, dense_stitch_second, gradient_tuple[5], RATE_STITCH, 0.0)
    return (update_outcome.astype(jnp.bfloat16), gradient_tuple[6].astype(jnp.bfloat16), updated_conv_weight, updated_conv_weight_mean, updated_conv_weight_variance, updated_conv_weight.astype(jnp.bfloat16), updated_conv_bias, updated_conv_bias_mean, updated_conv_bias_variance, updated_pooling_stitch, updated_pooling_stitch_mean, updated_pooling_stitch_variance, updated_dense_weight, updated_dense_weight_mean, updated_dense_weight_variance, updated_dense_weight.astype(jnp.bfloat16), updated_dense_bias, updated_dense_bias_mean, updated_dense_bias_variance, updated_dense_stitch, updated_dense_stitch_mean, updated_dense_stitch_variance)
```

```python
import jax
import jax.numpy as jnp
from jax import lax
from jax.sharding import PartitionSpec as P

STEP = 10


BETA_ONE = 0.5
BETA_TWO = 0.5
EPSILON = 1e-08
DECAY = 0.01
RATE_FILTER = 0.02
RATE_DENSE = 0.02
BIAS_LEARN_RATE = 0.05
RATE_STITCH = 0.2


def smooth_gate(values):
    return jax.nn.gelu(values, approximate=True)


def gate_slope(values):
    return jax.vjp(smooth_gate, values)[1](jnp.ones_like(values))[0]


def pool_mean(active):
    pooled_side = (active.shape[1] - 1) // 2
    span = 2 * pooled_side - 1
    total = jnp.zeros((), jnp.float32)
    for row_start in range(3):
        for col_start in range(3):
            total = total + active[:, row_start : row_start + span : 2, col_start : col_start + span : 2]
    return total / 9.0


def pool_spread(gradient, full_side):
    scaled = gradient / 9.0
    for axis in (1, 2):
        even = jnp.concatenate([scaled, jnp.zeros_like(lax.slice_in_dim(scaled, 0, 1, axis=axis))], axis)
        shifted = jnp.concatenate([jnp.zeros_like(lax.slice_in_dim(scaled, 0, 1, axis=axis)), scaled], axis)
        pairs = jnp.stack([even + shifted, even], axis + 1)
        shape = list(scaled.shape)
        shape[axis] = 2 * shape[axis] + 2
        scaled = lax.slice_in_dim(pairs.reshape(shape), 0, full_side, axis=axis)
    return scaled


CUBE = 16


def cube():
    return lax.axis_size("batch") == CUBE


def hop(values, offset):
    return lax.ppermute(values, "batch", [(i, i ^ offset) for i in range(CUBE)])


def core_swap(values):
    return lax.ppermute(values, "tower", [(0, 1), (1, 0)])


def by_core(core, own, other):
    return jnp.where(
        core == 0,
        jnp.concatenate([own, other], axis=-1),
        jnp.concatenate([other, own], axis=-1),
    )


def plane_axes(level):
    return (1, 2) if level % 2 == 0 else (2, 1)


LEVELS = (3, 2, 1, 0)


def block_order(level):
    first, second = plane_axes(level)
    return [4 * level + offset for offset in (first, 3, 0, second)]


def sum_batch(values):
    if not cube():
        return lax.psum(values, "batch")
    for offset in (1, 2, 4, 8):
        values = values + hop(values, offset)
    return values


def gather_blocks(block):
    blocks = {}
    tops = {level: hop(block, 4 * level) if level else block for level in range(4)}
    for level in range(4):
        first, second = plane_axes(level)
        near = hop(tops[level], first)
        blocks[4 * level] = tops[level]
        blocks[4 * level + first] = near
        blocks[4 * level + second] = hop(tops[level], second)
        blocks[4 * level + 3] = hop(near, second)
    return blocks


def gather_packed(packed):
    if not cube():
        return lax.all_gather(packed, ("batch", "tower"), axis=0)
    chip, core = lax.axis_index("batch"), lax.axis_index("tower")
    own = jnp.zeros((CUBE,) + packed.shape, packed.dtype)
    for offset, block in gather_blocks(packed).items():
        own = lax.dynamic_update_slice(own, block[None], (chip ^ offset, 0, 0))
    other = core_swap(own)
    return jnp.where(
        core == 0, jnp.stack([own, other], axis=1), jnp.stack([other, own], axis=1)
    ).reshape((2 * CUBE,) + packed.shape)


def scatter_chunks(chunks, chip):
    if not cube():
        arrived = lax.all_to_all(chunks, "batch", split_axis=0, concat_axis=0, tiled=True)
        return [arrived.reshape(-1, chunks.shape[2])]
    parts = []
    for level in LEVELS:
        arrived = []
        for offset in block_order(level):
            chunk = lax.dynamic_index_in_dim(chunks, chip ^ offset, axis=0, keepdims=False)
            arrived.append(hop(chunk, offset) if offset else chunk)
        parts.append(jnp.concatenate(arrived))
    return parts


def return_chunks(parts, chip, rows):
    if not cube():
        blocks = parts[0].reshape(-1, rows, parts[0].shape[1])
        return lax.all_to_all(blocks, "batch", split_axis=0, concat_axis=0, tiled=True)
    chunks = jnp.zeros((CUBE, rows, parts[0].shape[1]), parts[0].dtype)
    for level, part in zip(LEVELS, parts):
        for place, offset in enumerate(block_order(level)):
            block = part[place * rows : (place + 1) * rows]
            block = hop(block, offset) if offset else block
            chunks = lax.dynamic_update_slice(chunks, block[None], (chip ^ offset, 0, 0))
    return chunks


def reduce_rows(parts, rows):
    if not cube():
        total = lax.psum_scatter(parts[0], "batch", scatter_dimension=0, tiled=True)
        return total.astype(jnp.float32)
    total = 0.0
    for level, part in zip(LEVELS, parts):
        first, second = plane_axes(level)
        kept = part[2 * rows :].astype(jnp.float32) + hop(part[: 2 * rows], first).astype(jnp.float32)
        kept = kept[:rows] + hop(kept[rows:].astype(jnp.bfloat16), second).astype(jnp.float32)
        if level:
            kept = hop(kept.astype(jnp.bfloat16), 4 * level).astype(jnp.float32)
        total = total + kept
    return total


def gather_rows(block):
    if not cube():
        return [lax.all_gather(block, "batch", axis=0, tiled=True)]
    blocks = gather_blocks(block)
    return [
        jnp.concatenate([blocks[offset] for offset in block_order(level)]) for level in LEVELS
    ]


def reduce_filters(grads, chip, core):
    own = lax.dynamic_index_in_dim(grads, core, axis=1, keepdims=False).astype(jnp.float32)
    other = lax.dynamic_index_in_dim(grads, 1 - core, axis=1, keepdims=False)
    pair = own + core_swap(other).astype(jnp.float32)
    rows = pair.shape[1]
    if not cube():
        return lax.psum_scatter(pair, "batch", scatter_dimension=0, tiled=True)[0]
    parts = [
        jnp.concatenate(
            [
                lax.dynamic_index_in_dim(pair, chip ^ offset, axis=0, keepdims=False)
                for offset in block_order(level)
            ]
        ).astype(jnp.bfloat16)
        for level in LEVELS
    ]
    return reduce_rows(parts, rows)


def decoupled_adam_step(master, first, second, grad, rate, decay):
    first_new = BETA_ONE * first + (1.0 - BETA_ONE) * grad
    second_new = BETA_TWO * second + (1.0 - BETA_TWO) * grad * grad
    first_hat = first_new / (1.0 - BETA_ONE**STEP)
    second_hat = second_new / (1.0 - BETA_TWO**STEP)
    master_new = master - rate * (first_hat / (jnp.sqrt(second_hat) + EPSILON) + decay * master)
    return (master_new, first_new, second_new)


def local(
    crop_maps,
    cotangent,
    crop_counts,
    filter_weight,
    filter_first,
    filter_second,
    conv_filter_bias,
    conv_filter_bias_mean,
    conv_filter_bias_variance,
    pool_stitch,
    pool_stitch_first,
    pool_stitch_second,
    dense_weight,
    dense_weight_first,
    dense_weight_second,
    dense_bias,
    dense_bias_first,
    dense_bias_second,
    dense_stitch,
    dense_stitch_first,
    dense_stitch_second,
):
    block_rows = crop_maps.shape[0]
    side = crop_maps.shape[2]
    in_width = crop_maps.shape[4]
    filter_rows, out_width = filter_weight.shape
    chips = lax.axis_size("batch")
    chip = lax.axis_index("batch")
    core = lax.axis_index("tower")
    totals = jnp.sum(crop_counts.reshape(2, -1), axis=1)
    slots = jnp.arange(block_rows, dtype=jnp.int32)
    mask = (slots[None, :] < totals[:, None]).astype(jnp.float32).reshape(-1)
    pair_rows = 2 * block_rows
    dense_rows, unit_width = dense_weight.shape[1:]
    half_width = unit_width // 2
    bias_width = conv_filter_bias.shape[0]
    small_width = bias_width + pool_stitch.shape[0]
    pack_rows = -(-(filter_rows + 1) // 16) * 16
    small = jnp.concatenate([conv_filter_bias, pool_stitch])
    small = jnp.pad(small, (0, (pack_rows - filter_rows) * out_width - small_width))
    packed = jnp.concatenate([filter_weight, small.reshape(-1, out_width)]).astype(jnp.bfloat16)
    gathered = gather_packed(packed)
    filters = gathered[:, :filter_rows].reshape(2, 3, 3, in_width, out_width)
    small_full = gathered[:, filter_rows, :small_width].astype(jnp.float32)
    biases = small_full[:, :bias_width].reshape(2, out_width)
    pool_low = small_full[:, bias_width:].reshape(2, 2, out_width)
    maps = jnp.transpose(crop_maps, (1, 2, 3, 0, 4))
    grad_out = cotangent.astype(jnp.float32) * mask[:, None, None]
    own_stitch = lax.dynamic_index_in_dim(dense_stitch, core, axis=1, keepdims=False)
    other_stitch = lax.dynamic_index_in_dim(dense_stitch, 1 - core, axis=1, keepdims=False)
    own_grad = jnp.sum(own_stitch * grad_out, axis=1).astype(jnp.bfloat16)
    other_grad = core_swap(jnp.sum(other_stitch * grad_out, axis=1).astype(jnp.bfloat16))
    grad_active = by_core(core, own_grad, other_grad)
    dense_low = dense_weight[0].astype(jnp.bfloat16)
    conv = jnp.stack(
        [
            lax.conv_general_dilated(
                maps[tower],
                filters[tower],
                (1, 1),
                ((1, 1), (1, 1)),
                dimension_numbers=("HWNC", "HWIO", "HWNC"),
                preferred_element_type=jnp.float32,
            )
            for tower in range(2)
        ]
    )
    conv = conv + biases[:, None, None, None, :]
    pooled = pool_mean(smooth_gate(conv))
    pooled_side = pooled.shape[1]
    mixed = jnp.sum(pool_low[:, :, None, None, None, :] * pooled[None], axis=1).astype(jnp.bfloat16)
    mixed = jnp.transpose(mixed, (0, 3, 1, 2, 4)).reshape(2, block_rows, chips, dense_rows)
    mixed = jnp.transpose(mixed, (0, 2, 1, 3))
    own_mixed = lax.dynamic_index_in_dim(mixed, core, axis=0, keepdims=False)
    other_mixed = core_swap(lax.dynamic_index_in_dim(mixed, 1 - core, axis=0, keepdims=False))
    features = jnp.where(
        core == 0,
        jnp.concatenate([own_mixed, other_mixed], axis=1),
        jnp.concatenate([other_mixed, own_mixed], axis=1),
    )
    columns = scatter_chunks(features, chip)
    partial = [
        jnp.dot(part, dense_low, preferred_element_type=jnp.float32).astype(jnp.bfloat16)
        for part in columns
    ]
    hidden = reduce_rows(partial, pair_rows) + dense_bias
    grad_hidden = (grad_active.astype(jnp.float32) * gate_slope(hidden)).astype(jnp.bfloat16)
    grad_full = gather_rows(grad_hidden)
    active = smooth_gate(hidden).astype(jnp.bfloat16)
    own_active = lax.dynamic_slice_in_dim(active, core * half_width, half_width, axis=1)
    other_active = core_swap(
        lax.dynamic_slice_in_dim(active, (1 - core) * half_width, half_width, axis=1)
    )
    own_active = own_active.astype(jnp.float32)[:, None]
    other_active = other_active.astype(jnp.float32)[:, None]
    stitched = own_stitch * own_active + other_stitch * other_active
    stitched = (stitched * mask[:, None, None]).astype(jnp.bfloat16)
    grad_own_stitch = jnp.sum(grad_out * own_active, axis=0)
    grad_other_stitch = jnp.sum(grad_out * other_active, axis=0)
    grad_dense_stitch = sum_batch(
        jnp.where(
            core == 0,
            jnp.stack([grad_own_stitch, grad_other_stitch], axis=1),
            jnp.stack([grad_other_stitch, grad_own_stitch], axis=1),
        )
    )
    grad_columns = [
        lax.dot_general(
            part, dense_low, (((1,), (1,)), ((), ())), preferred_element_type=jnp.float32
        ).astype(jnp.bfloat16)
        for part in grad_full
    ]
    returned = return_chunks(grad_columns, chip, pair_rows)
    columns = jnp.concatenate(columns)
    grad_full = jnp.concatenate(grad_full)
    grad_dense_bias = jnp.sum(grad_full.astype(jnp.float32), axis=0)
    grad_dense_weight = lax.dot_general(
        columns, grad_full, (((0,), (0,)), ((), ())), preferred_element_type=jnp.float32
    )
    halves = returned.reshape(chips, 2, block_rows, dense_rows)
    own_mixed = lax.dynamic_index_in_dim(halves, core, axis=1, keepdims=False)
    other_mixed = core_swap(lax.dynamic_index_in_dim(halves, 1 - core, axis=1, keepdims=False))
    grad_mixed = jnp.where(
        core == 0, jnp.stack([own_mixed, other_mixed]), jnp.stack([other_mixed, own_mixed])
    )
    grad_mixed = jnp.transpose(grad_mixed, (0, 2, 1, 3)).reshape(
        2, block_rows, pooled_side, pooled_side, out_width
    )
    grad_mixed = jnp.transpose(grad_mixed, (0, 2, 3, 1, 4)).astype(jnp.float32)
    grad_pool_stitch = jnp.sum(grad_mixed[:, None] * pooled[None], axis=(2, 3, 4))
    grad_pooled = jnp.sum(pool_low[:, :, None, None, None, :] * grad_mixed[:, None], axis=0)
    grad_conv = (pool_spread(grad_pooled, side) * gate_slope(conv)).astype(jnp.bfloat16)
    grad_filter_bias = jnp.sum(grad_conv.astype(jnp.float32), axis=(1, 2, 3))
    weight_dims = lax.ConvDimensionNumbers((3, 2, 0, 1), (3, 2, 0, 1), (2, 3, 0, 1))
    grad_filter_weight = jnp.stack(
        [
            lax.conv_general_dilated(
                maps[tower],
                grad_conv[tower],
                (1, 1),
                ((1, 1), (1, 1)),
                dimension_numbers=weight_dims,
                preferred_element_type=jnp.float32,
            ).astype(jnp.bfloat16)
            for tower in range(2)
        ]
    )
    filter_sums = reduce_filters(
        grad_filter_weight.reshape(chips, 2, filter_rows, out_width), chip, core
    )
    small_grad = jnp.concatenate(
        [grad_filter_bias.reshape(2 * chips, -1), grad_pool_stitch.reshape(2 * chips, -1)], axis=1
    )
    small_grad = sum_batch(small_grad + core_swap(small_grad))
    small_grad = lax.dynamic_index_in_dim(small_grad, chip * 2 + core, axis=0, keepdims=False)
    filter_bias_sums = small_grad[:bias_width]
    pool_sums = small_grad[bias_width:]
    input_grad = jnp.stack(
        [
            lax.conv_general_dilated(
                grad_conv[tower],
                filters[tower][::-1, ::-1],
                (1, 1),
                ((1, 1), (1, 1)),
                dimension_numbers=("HWNC", "HWOI", "HWNC"),
                preferred_element_type=jnp.float32,
            ).astype(jnp.bfloat16)
            for tower in range(2)
        ]
    )
    input_grad = jnp.transpose(input_grad, (3, 0, 1, 2, 4))
    updated_conv_weight, updated_conv_weight_mean, updated_conv_weight_variance = (
        decoupled_adam_step(
            filter_weight, filter_first, filter_second, filter_sums, RATE_FILTER, DECAY
        )
    )
    updated_conv_bias, updated_conv_bias_mean, updated_conv_bias_variance = decoupled_adam_step(
        conv_filter_bias,
        conv_filter_bias_mean,
        conv_filter_bias_variance,
        filter_bias_sums,
        BIAS_LEARN_RATE,
        0.0,
    )
    updated_pooling_stitch, updated_pooling_stitch_mean, updated_pooling_stitch_variance = (
        decoupled_adam_step(
            pool_stitch, pool_stitch_first, pool_stitch_second, pool_sums, RATE_STITCH, 0.0
        )
    )
    updated_dense_weight, updated_dense_weight_mean, updated_dense_weight_variance = (
        decoupled_adam_step(
            dense_weight,
            dense_weight_first,
            dense_weight_second,
            grad_dense_weight[None],
            RATE_DENSE,
            DECAY,
        )
    )
    updated_dense_bias, updated_dense_bias_mean, updated_dense_bias_variance = decoupled_adam_step(
        dense_bias, dense_bias_first, dense_bias_second, grad_dense_bias[None], BIAS_LEARN_RATE, 0.0
    )
    updated_dense_stitch, updated_dense_stitch_mean, updated_dense_stitch_variance = (
        decoupled_adam_step(
            dense_stitch,
            dense_stitch_first,
            dense_stitch_second,
            grad_dense_stitch,
            RATE_STITCH,
            0.0,
        )
    )
    return (
        stitched,
        input_grad,
        updated_conv_weight,
        updated_conv_weight_mean,
        updated_conv_weight_variance,
        updated_conv_weight.astype(jnp.bfloat16),
        updated_conv_bias,
        updated_conv_bias_mean,
        updated_conv_bias_variance,
        updated_pooling_stitch,
        updated_pooling_stitch_mean,
        updated_pooling_stitch_variance,
        updated_dense_weight,
        updated_dense_weight_mean,
        updated_dense_weight_variance,
        updated_dense_weight.astype(jnp.bfloat16),
        updated_dense_bias,
        updated_dense_bias_mean,
        updated_dense_bias_variance,
        updated_dense_stitch,
        updated_dense_stitch_mean,
        updated_dense_stitch_variance,
    )


def solution(mesh):
    in_specs = (
        P(("batch", "tower"), None, None, None, None),
        P("batch", None, "tower"),
        P("batch"),
        P(("batch", "tower"), None),
        P(("batch", "tower"), None),
        P(("batch", "tower"), None),
        P(("batch", "tower")),
        P(("batch", "tower")),
        P(("batch", "tower")),
        P(("batch", "tower")),
        P(("batch", "tower")),
        P(("batch", "tower")),
        P("tower", "batch", None),
        P("tower", "batch", None),
        P("tower", "batch", None),
        P("tower", None),
        P("tower", None),
        P("tower", None),
        P(None, None, "tower"),
        P(None, None, "tower"),
        P(None, None, "tower"),
    )
    out_specs = (
        P("batch", None, "tower"),
        P(("batch", "tower"), None, None, None, None),
        P(("batch", "tower"), None),
        P(("batch", "tower"), None),
        P(("batch", "tower"), None),
        P(("batch", "tower"), None),
        P(("batch", "tower")),
        P(("batch", "tower")),
        P(("batch", "tower")),
        P(("batch", "tower")),
        P(("batch", "tower")),
        P(("batch", "tower")),
        P("tower", "batch", None),
        P("tower", "batch", None),
        P("tower", "batch", None),
        P("tower", "batch", None),
        P("tower", None),
        P("tower", None),
        P("tower", None),
        P(None, None, "tower"),
        P(None, None, "tower"),
        P(None, None, "tower"),
    )
    return jax.shard_map(local, mesh=mesh, in_specs=in_specs, out_specs=out_specs, check_vma=False)
```

```python
import jax
import jax.numpy as jnp
from jax import lax
from jax.experimental import pallas as pl
from jax.experimental.pallas import tpu as pltpu
from jax.sharding import PartitionSpec as P

STEP = 10


BETA_ONE = 0.5
BETA_TWO = 0.5
EPSILON = 1e-08
DECAY = 0.01
RATE_FILTER = 0.02
RATE_DENSE = 0.02
BIAS_LEARN_RATE = 0.05
RATE_STITCH = 0.2


def smooth_gate(values):
    return jax.nn.gelu(values, approximate=True)


def gate_slope(values):
    return jax.vjp(smooth_gate, values)[1](jnp.ones_like(values))[0]


def pool_mean(active):
    pooled_side = (active.shape[1] - 1) // 2
    span = 2 * pooled_side - 1
    total = jnp.zeros((), jnp.float32)
    for row_start in range(3):
        for col_start in range(3):
            total = total + active[:, row_start : row_start + span : 2, col_start : col_start + span : 2]
    return total / 9.0


def pool_spread(gradient, full_side):
    scaled = gradient / 9.0
    for axis in (1, 2):
        even = jnp.concatenate([scaled, jnp.zeros_like(lax.slice_in_dim(scaled, 0, 1, axis=axis))], axis)
        shifted = jnp.concatenate([jnp.zeros_like(lax.slice_in_dim(scaled, 0, 1, axis=axis)), scaled], axis)
        pairs = jnp.stack([even + shifted, even], axis + 1)
        shape = list(scaled.shape)
        shape[axis] = 2 * shape[axis] + 2
        scaled = lax.slice_in_dim(pairs.reshape(shape), 0, full_side, axis=axis)
    return scaled


def decoupled_adam_step(master, first, second, grad, rate, decay):
    first_new = BETA_ONE * first + (1.0 - BETA_ONE) * grad
    second_new = BETA_TWO * second + (1.0 - BETA_TWO) * grad * grad
    first_hat = first_new / (1.0 - BETA_ONE**STEP)
    second_hat = second_new / (1.0 - BETA_TWO**STEP)
    master_new = master - rate * (first_hat / (jnp.sqrt(second_hat) + EPSILON) + decay * master)
    return (master_new, first_new, second_new)


def core_swap(values):
    return lax.ppermute(values, "tower", [(0, 1), (1, 0)])


def by_core(core, own, other):
    return jnp.where(
        core == 0,
        jnp.concatenate([own, other], axis=-1),
        jnp.concatenate([other, own], axis=-1),
    )


def gradients_any(
    crop_maps,
    cotangent,
    crop_counts,
    filter_weight,
    conv_filter_bias,
    pool_stitch,
    dense_weight,
    dense_weight_first,
    dense_weight_second,
    dense_bias,
    dense_stitch,
):
    block_rows = crop_maps.shape[0]
    side = crop_maps.shape[2]
    in_width = crop_maps.shape[4]
    filter_rows, out_width = filter_weight.shape
    chips = lax.axis_size("batch")
    chip = lax.axis_index("batch")
    core = lax.axis_index("tower")
    totals = jnp.sum(crop_counts.reshape(2, -1), axis=1)
    slots = jnp.arange(block_rows, dtype=jnp.int32)
    mask = (slots[None, :] < totals[:, None]).astype(jnp.float32).reshape(-1)
    pair_rows = 2 * block_rows
    dense_rows, unit_width = dense_weight.shape[1:]
    half_width = unit_width // 2
    bias_width = conv_filter_bias.shape[0]
    small_width = bias_width + pool_stitch.shape[0]
    pack_rows = -(-(filter_rows + 1) // 16) * 16
    small = jnp.concatenate([conv_filter_bias, pool_stitch])
    small = jnp.pad(small, (0, (pack_rows - filter_rows) * out_width - small_width))
    packed = jnp.concatenate([filter_weight, small.reshape(-1, out_width)]).astype(jnp.bfloat16)
    gathered = lax.all_gather(packed, ("batch", "tower"), axis=0)
    filters = gathered[:, :filter_rows].reshape(2, 3, 3, in_width, out_width)
    small_full = gathered[:, filter_rows, :small_width].astype(jnp.float32)
    biases = small_full[:, :bias_width].reshape(2, out_width)
    pool_low = small_full[:, bias_width:].reshape(2, 2, out_width)
    maps = jnp.transpose(crop_maps, (1, 2, 3, 0, 4))
    grad_out = cotangent.astype(jnp.float32) * mask[:, None, None]
    own_stitch = lax.dynamic_index_in_dim(dense_stitch, core, axis=1, keepdims=False)
    other_stitch = lax.dynamic_index_in_dim(dense_stitch, 1 - core, axis=1, keepdims=False)
    own_grad = jnp.sum(own_stitch * grad_out, axis=1).astype(jnp.bfloat16)
    other_grad = core_swap(jnp.sum(other_stitch * grad_out, axis=1).astype(jnp.bfloat16))
    grad_active = by_core(core, own_grad, other_grad)
    dense_low = dense_weight[0].astype(jnp.bfloat16)
    conv = jnp.stack(
        [
            lax.conv_general_dilated(
                maps[tower],
                filters[tower],
                (1, 1),
                ((1, 1), (1, 1)),
                dimension_numbers=("HWNC", "HWIO", "HWNC"),
                preferred_element_type=jnp.float32,
            )
            for tower in range(2)
        ]
    )
    conv = conv + biases[:, None, None, None, :]
    pooled = pool_mean(smooth_gate(conv))
    pooled_side = pooled.shape[1]
    mixed = jnp.sum(pool_low[:, :, None, None, None, :] * pooled[None], axis=1).astype(jnp.bfloat16)
    mixed = jnp.transpose(mixed, (0, 3, 1, 2, 4)).reshape(2, block_rows, chips, dense_rows)
    mixed = jnp.transpose(mixed, (0, 2, 1, 3))
    own_mixed = lax.dynamic_index_in_dim(mixed, core, axis=0, keepdims=False)
    other_mixed = core_swap(lax.dynamic_index_in_dim(mixed, 1 - core, axis=0, keepdims=False))
    features = jnp.where(
        core == 0,
        jnp.concatenate([own_mixed, other_mixed], axis=1),
        jnp.concatenate([other_mixed, own_mixed], axis=1),
    )
    columns = lax.all_to_all(features, "batch", split_axis=0, concat_axis=0, tiled=True)
    columns = columns.reshape(-1, dense_rows)
    partial = jnp.dot(columns, dense_low, preferred_element_type=jnp.float32)
    hidden = lax.psum_scatter(partial, "batch", scatter_dimension=0, tiled=True) + dense_bias
    grad_hidden = (grad_active.astype(jnp.float32) * gate_slope(hidden)).astype(jnp.bfloat16)
    grad_full = lax.all_gather(grad_hidden, "batch", axis=0, tiled=True)
    active = smooth_gate(hidden).astype(jnp.bfloat16)
    own_active = lax.dynamic_slice_in_dim(active, core * half_width, half_width, axis=1)
    other_active = core_swap(
        lax.dynamic_slice_in_dim(active, (1 - core) * half_width, half_width, axis=1)
    )
    own_active = own_active.astype(jnp.float32)[:, None]
    other_active = other_active.astype(jnp.float32)[:, None]
    stitched = own_stitch * own_active + other_stitch * other_active
    stitched = (stitched * mask[:, None, None]).astype(jnp.bfloat16)
    grad_own_stitch = jnp.sum(grad_out * own_active, axis=0)
    grad_other_stitch = jnp.sum(grad_out * other_active, axis=0)
    grad_dense_stitch = lax.psum(
        jnp.where(
            core == 0,
            jnp.stack([grad_own_stitch, grad_other_stitch], axis=1),
            jnp.stack([grad_other_stitch, grad_own_stitch], axis=1),
        ),
        "batch",
    )
    grad_columns = lax.dot_general(
        grad_full, dense_low, (((1,), (1,)), ((), ())), preferred_element_type=jnp.float32
    ).astype(jnp.bfloat16)
    grad_columns = grad_columns.reshape(chips, pair_rows, dense_rows)
    returned = lax.all_to_all(grad_columns, "batch", split_axis=0, concat_axis=0, tiled=True)
    grad_dense_bias = jnp.sum(grad_full.astype(jnp.float32), axis=0)
    grad_dense_weight = lax.dot_general(
        columns, grad_full, (((0,), (0,)), ((), ())), preferred_element_type=jnp.float32
    )
    halves = returned.reshape(chips, 2, block_rows, dense_rows)
    own_mixed = lax.dynamic_index_in_dim(halves, core, axis=1, keepdims=False)
    other_mixed = core_swap(lax.dynamic_index_in_dim(halves, 1 - core, axis=1, keepdims=False))
    grad_mixed = jnp.where(
        core == 0, jnp.stack([own_mixed, other_mixed]), jnp.stack([other_mixed, own_mixed])
    )
    grad_mixed = jnp.transpose(grad_mixed, (0, 2, 1, 3)).reshape(
        2, block_rows, pooled_side, pooled_side, out_width
    )
    grad_mixed = jnp.transpose(grad_mixed, (0, 2, 3, 1, 4)).astype(jnp.float32)
    grad_pool_stitch = jnp.sum(grad_mixed[:, None] * pooled[None], axis=(2, 3, 4))
    grad_pooled = jnp.sum(pool_low[:, :, None, None, None, :] * grad_mixed[:, None], axis=0)
    grad_conv = (pool_spread(grad_pooled, side) * gate_slope(conv)).astype(jnp.bfloat16)
    grad_filter_bias = jnp.sum(grad_conv.astype(jnp.float32), axis=(1, 2, 3))
    weight_dims = lax.ConvDimensionNumbers((3, 2, 0, 1), (3, 2, 0, 1), (2, 3, 0, 1))
    grad_filter_weight = jnp.stack(
        [
            lax.conv_general_dilated(
                maps[tower],
                grad_conv[tower],
                (1, 1),
                ((1, 1), (1, 1)),
                dimension_numbers=weight_dims,
                preferred_element_type=jnp.float32,
            )
            for tower in range(2)
        ]
    )
    filter_sums = lax.psum_scatter(
        grad_filter_weight.reshape(-1, out_width),
        ("batch", "tower"),
        scatter_dimension=0,
        tiled=True,
    )
    small_grad = jnp.concatenate(
        [grad_filter_bias.reshape(2 * chips, -1), grad_pool_stitch.reshape(2 * chips, -1)], axis=1
    )
    small_grad = lax.psum(small_grad, ("batch", "tower"))
    small_grad = lax.dynamic_index_in_dim(small_grad, chip * 2 + core, axis=0, keepdims=False)
    filter_bias_sums = small_grad[:bias_width]
    pool_sums = small_grad[bias_width:]
    input_grad = jnp.stack(
        [
            lax.conv_general_dilated(
                grad_conv[tower],
                filters[tower][::-1, ::-1],
                (1, 1),
                ((1, 1), (1, 1)),
                dimension_numbers=("HWNC", "HWOI", "HWNC"),
                preferred_element_type=jnp.float32,
            ).astype(jnp.bfloat16)
            for tower in range(2)
        ]
    )
    input_grad = jnp.transpose(input_grad, (3, 0, 1, 2, 4))
    update = decoupled_adam_step(
        dense_weight, dense_weight_first, dense_weight_second, grad_dense_weight[None], RATE_DENSE, DECAY
    )
    return (
        stitched,
        input_grad,
        filter_sums,
        filter_bias_sums,
        pool_sums,
        (*update, update[0].astype(jnp.bfloat16)),
        grad_dense_bias,
        grad_dense_stitch,
    )


CUBE = 16
LANES = 128
VMEM_ASKED = 8 << 20
GELU_SCALE = 0.7978845608028654
GELU_CUBIC = 0.044715


def hop(values, level):
    return lax.ppermute(values, "batch", [(i, i ^ (4 * level)) for i in range(CUBE)])


def plane_hop(values, offset):
    return lax.ppermute(values, "batch", [(i, i ^ offset) for i in range(CUBE)])


SIDES = ((0, 1, 2, 3), (0, 2, 1, 3))


def zero_of(values):
    last = values[(-1,) * values.ndim]
    return (last != last).astype(jnp.int32)


def held(values, *others):
    zero = sum(zero_of(other) for other in others)
    return jnp.where(zero == 0, values, jnp.zeros((), values.dtype))


def gather_levels(block):
    return [hop(block, level) if level else block for level in range(4)]


def gather_plane(tops):
    groups = []
    for group in range(2):
        own = jnp.stack(tops[2 * group : 2 * group + 2])
        half = jnp.stack([own, plane_hop(own, SIDES[group][1])])
        groups.append(jnp.concatenate([half, plane_hop(half, SIDES[group][2])]))
    return groups


def reduce_first(parts, group):
    sent = plane_hop(parts[2:], SIDES[group][2])
    return parts[:2].astype(jnp.float32) + sent.astype(jnp.float32)


def reduce_second(kept, group):
    sent = plane_hop(kept[1].astype(jnp.bfloat16), SIDES[group][1])
    return kept[0] + sent.astype(jnp.float32)


def reduce_levels(groups):
    total = groups[0][0]
    for level in (1, 2, 3):
        part = hop(groups[level // 2][level % 2].astype(jnp.bfloat16), level)
        total = total + part.astype(jnp.float32)
    return total


def sum_pairs(parts):
    parts = [part.astype(jnp.float32) for part in parts]
    return (parts[0] + parts[1]) + (parts[2] + parts[3])


def on_chip():
    return pl.BlockSpec(memory_space=pltpu.VMEM)


def turn(values):
    return pltpu.roll(values, LANES // 2, axis=1)


def mix_kernel(
    place,
    maps_a,
    maps_b,
    small,
    slope_a,
    slope_b,
    pooled,
    sent,
    row_sums,
    means,
):
    side, width, crops, channels = maps_a.shape
    count = (width - 1) // 2

    def gate_row(y, carry):
        for tower, (maps, slopes) in enumerate(((maps_a, slope_a), (maps_b, slope_b))):
            bias = small[tower][None]
            running = [None] * count
            for x in range(width):
                value = maps[y, x] + bias
                square = value * value
                bend = jnp.tanh(GELU_SCALE * value * (1.0 + GELU_CUBIC * square))
                half = 0.5 + 0.5 * bend
                rise = GELU_SCALE * (1.0 + 3.0 * GELU_CUBIC * square)
                slope = half + 0.5 * value * (1.0 - bend * bend) * rise
                slopes[y, x] = slope.astype(jnp.bfloat16)
                gate = value * half
                for place_x in range(max(0, (x - 1) // 2), min(count - 1, x // 2) + 1):
                    old = running[place_x]
                    running[place_x] = gate if old is None else old + gate
            for place_x in range(count):
                row_sums[tower, y, place_x] = running[place_x]
        return carry

    lax.fori_loop(0, side, gate_row, 0)

    def mean_row(row, carry):
        for tower in range(2):
            for place_x in range(count):
                mean = (
                    row_sums[tower, 2 * row, place_x]
                    + row_sums[tower, 2 * row + 1, place_x]
                    + row_sums[tower, 2 * row + 2, place_x]
                ) * (1.0 / 9.0)
                means[tower, row * count + place_x] = mean
                pooled[tower, row * count + place_x] = mean.astype(jnp.bfloat16)
        return carry

    lax.fori_loop(0, count, mean_row, 0)
    low_lanes = lax.broadcasted_iota(jnp.int32, (crops, LANES), 1) < LANES // 2
    own_plane, core = place[1], place[2]
    halves = small.shape[1] // LANES
    for pair in range(CUBE // 2):
        for tower in range(2):
            tiles = []
            for tile in range(9 * pair, 9 * pair + 9):
                cell, first = tile // halves, tile % halves * LANES
                lanes = slice(first, first + LANES)
                tiles.append(
                    small[2 + 2 * tower, lanes][None] * means[0, cell, :, lanes]
                    + small[3 + 2 * tower, lanes][None] * means[1, cell, :, lanes]
                )
            turned = [turn(tile) for tile in tiles[4:]]
            blank = jnp.zeros_like(tiles[0])
            even = tiles[:4] + [jnp.where(low_lanes, tiles[4], blank)]
            odd = [jnp.where(low_lanes, turned[q], turned[q + 1]) for q in range(4)]
            odd.append(jnp.where(low_lanes, turned[4], blank))
            for chunk, pieces in ((2 * pair, even), (2 * pair + 1, odd)):
                target = (tower ^ core, (chunk % 4) ^ own_plane, chunk // 4)
                for q, piece in enumerate(pieces):
                    lanes = slice(q * LANES, (q + 1) * LANES)
                    sent[(*target, slice(None), lanes)] = piece.astype(jnp.bfloat16)


def mix(place, conv, small, wide):
    side, _, crops, width = conv[0].shape
    count = (side - 1) // 2
    cells = count * count
    slope = jax.ShapeDtypeStruct(conv[0].shape, jnp.bfloat16)
    pooled = jax.ShapeDtypeStruct((2, cells, crops, width), jnp.bfloat16)
    sent = jax.ShapeDtypeStruct((2, 4, 4, crops, wide), jnp.bfloat16)
    return pl.pallas_call(
        mix_kernel,
        out_shape=(slope, slope, pooled, sent),
        in_specs=[pl.BlockSpec(memory_space=pltpu.SMEM)] + [on_chip()] * 3,
        out_specs=(on_chip(),) * 4,
        scratch_shapes=[
            pltpu.VMEM((2, side, count, crops, width), jnp.float32),
            pltpu.VMEM((2, cells, crops, width), jnp.float32),
        ],
        compiler_params=pltpu.CompilerParams(vmem_limit_bytes=VMEM_ASKED),
        cost_estimate=pl.CostEstimate(
            flops=60 * conv[0].size,
            bytes_accessed=12 * conv[0].size,
            transcendentals=2 * conv[0].size,
        ),
        name="gate_pool_mix",
    )(place, conv[0], conv[1], small)


def back_kernel(
    place,
    returned,
    pooled,
    small,
    slope_a,
    slope_b,
    grad_a,
    grad_b,
    grad_small,
    mixed,
    spread,
):
    side, width, crops, channels = slope_a.shape
    count = (width - 1) // 2
    halves = channels // LANES
    low_lanes = lax.broadcasted_iota(jnp.int32, (crops, LANES), 1) < LANES // 2
    own_level, own_plane, core = place[0], place[1], place[2]
    for pair in range(CUBE // 2):
        for tower in range(2):
            loaded = []
            for chunk in (2 * pair, 2 * pair + 1):
                source = (tower ^ core, (chunk % 4) ^ own_plane, (chunk // 4) ^ own_level)
                pieces = []
                for q in range(5):
                    lanes = slice(q * LANES, (q + 1) * LANES)
                    pieces.append(returned[(*source, slice(None), lanes)].astype(jnp.float32))
                loaded.append(pieces)
            even, odd = loaded
            turned = [turn(tile) for tile in odd]
            tiles = even[:4] + [jnp.where(low_lanes, even[4], turned[0])]
            tiles += [jnp.where(low_lanes, turned[q], turned[q + 1]) for q in range(4)]
            for q, tile in enumerate(tiles):
                first = (9 * pair + q) % halves * LANES
                mixed[tower, (9 * pair + q) // halves, :, first : first + LANES] = tile
    blank = jnp.zeros((crops, channels), jnp.float32)
    for tower in range(2):
        for place_x in range(count):
            spread[tower, 0, place_x] = blank
            spread[tower, count + 1, place_x] = blank

    def unmix(row, totals):
        totals = list(totals)
        for place_x in range(count):
            cell = row * count + place_x
            grads = [mixed[tower, cell] for tower in range(2)]
            values = [pooled[tower, cell].astype(jnp.float32) for tower in range(2)]
            for i in range(2):
                for j in range(2):
                    totals[2 * i + j] = totals[2 * i + j] + grads[i] * values[j]
            for j in range(2):
                spread[j, row + 1, place_x] = (
                    small[2 + j][None] * grads[0] + small[4 + j][None] * grads[1]
                ) * (1.0 / 9.0)
        return tuple(totals)

    totals = lax.fori_loop(0, count, unmix, (blank,) * 4)
    for which in range(4):
        grad_small[2 + which] = jnp.sum(totals[which], axis=0)

    def spread_row(y, totals):
        totals = list(totals)
        row = y // 2
        both = (1 - y % 2).astype(jnp.float32)
        for tower, (slopes, grads) in enumerate(((slope_a, grad_a), (slope_b, grad_b))):
            line = [
                spread[tower, row + 1, place_x] + both * spread[tower, row, place_x]
                for place_x in range(count)
            ]
            for x in range(width):
                near = [line[q] for q in range(max(0, (x - 1) // 2), min(count - 1, x // 2) + 1)]
                value = near[0] if len(near) == 1 else near[0] + near[1]
                value = (value * slopes[y, x].astype(jnp.float32)).astype(jnp.bfloat16)
                grads[y, x] = value
                totals[tower] = totals[tower] + value.astype(jnp.float32)
        return tuple(totals)

    totals = lax.fori_loop(0, side, spread_row, (blank,) * 2)
    for tower in range(2):
        grad_small[tower] = jnp.sum(totals[tower], axis=0)


def back(place, returned, pooled, small, slopes):
    side, _, crops, width = slopes[0].shape
    count = (side - 1) // 2
    grad = jax.ShapeDtypeStruct(slopes[0].shape, jnp.bfloat16)
    return pl.pallas_call(
        back_kernel,
        out_shape=(grad, grad, jax.ShapeDtypeStruct((6, width), jnp.float32)),
        in_specs=[pl.BlockSpec(memory_space=pltpu.SMEM)] + [on_chip()] * 5,
        out_specs=(on_chip(),) * 3,
        scratch_shapes=[
            pltpu.VMEM((2, count * count, crops, width), jnp.float32),
            pltpu.VMEM((2, count + 2, count, crops, width), jnp.float32),
        ],
        compiler_params=pltpu.CompilerParams(vmem_limit_bytes=VMEM_ASKED),
        cost_estimate=pl.CostEstimate(
            flops=20 * slopes[0].size, bytes_accessed=8 * slopes[0].size, transcendentals=0
        ),
        name="pool_gradient",
    )(place, returned, pooled, small, slopes[0], slopes[1])


def pair_kernel(place, own, other, blocks_a, blocks_b):
    chip = 4 * place[0] + place[1]
    for group, blocks in enumerate((blocks_a, blocks_b)):
        for side in range(4):
            for level in range(2):
                source = chip ^ (4 * (2 * group + level) + SIDES[group][side])
                total = own[source].astype(jnp.float32) + other[source].astype(jnp.float32)
                blocks[side, level] = total.astype(jnp.bfloat16)


def pair_blocks(place, own, other):
    blocks = jax.ShapeDtypeStruct((4, 2) + own.shape[1:], own.dtype)
    return pl.pallas_call(
        pair_kernel,
        out_shape=(blocks, blocks),
        in_specs=[pl.BlockSpec(memory_space=pltpu.SMEM), on_chip(), on_chip()],
        out_specs=(on_chip(), on_chip()),
        compiler_params=pltpu.CompilerParams(vmem_limit_bytes=VMEM_ASKED),
        cost_estimate=pl.CostEstimate(
            flops=own.size, bytes_accessed=6 * own.size, transcendentals=0
        ),
        name="pair_blocks",
    )(place, own, other)


def dense_kernel(order, columns, grads_a, grads_b, weight, first, second, *outs):
    new_weight, new_first, new_second, copy, grad_bias = outs[-5:]
    rows = grads_a.shape[0]
    grad = jnp.dot(columns[:, :rows], grads_a[...], preferred_element_type=jnp.float32)
    grad += jnp.dot(columns[:, rows:], grads_b[...], preferred_element_type=jnp.float32)
    updated, mean, square = decoupled_adam_step(
        weight[0], first[0], second[0], grad[: weight.shape[1]], RATE_DENSE, DECAY
    )
    new_weight[0] = updated
    new_first[0] = mean
    new_second[0] = square
    copy[0] = updated.astype(jnp.bfloat16)
    grad_bias[...] = jnp.sum(
        grads_a[...].astype(jnp.float32) + grads_b[...].astype(jnp.float32), axis=0, keepdims=True
    )


def dense_update(order, columns, grads, weight, first, second, part, parts, old):
    tile = 1024
    _, rows, units = weight.shape
    steps = units // tile // parts
    state = pl.BlockSpec((1, rows, tile), lambda step: (0, 0, part * steps + step))
    grad = pl.BlockSpec((grads[0].shape[0], tile), lambda step: (0, step))
    outs = [jax.ShapeDtypeStruct(weight.shape, jnp.float32)] * 3
    outs += [
        jax.ShapeDtypeStruct(weight.shape, jnp.bfloat16),
        jax.ShapeDtypeStruct((1, units), jnp.float32),
    ]
    return pl.pallas_call(
        dense_kernel,
        grid=(steps,),
        out_shape=outs,
        in_specs=[
            pl.BlockSpec(memory_space=pltpu.SMEM),
            pl.BlockSpec(columns.shape, lambda step: (0, 0)),
            grad,
            grad,
            state,
            state,
            state,
            *[pl.BlockSpec(memory_space=pl.ANY)] * len(old),
        ],
        out_specs=[state] * 4 + [pl.BlockSpec((1, tile), lambda step: (0, part * steps + step))],
        input_output_aliases={7 + i: i for i in range(len(old))},
        compiler_params=pltpu.CompilerParams(vmem_limit_bytes=48 << 20),
        cost_estimate=pl.CostEstimate(
            flops=2 * columns.size * units // parts,
            bytes_accessed=26 * weight.size // parts,
            transcendentals=weight.size // parts,
        ),
        name="dense_update",
    )(order, columns, *grads, weight, first, second, *old)


def gradients_cube(
    crop_maps,
    cotangent,
    crop_counts,
    filter_weight,
    conv_filter_bias,
    pool_stitch,
    dense_weight,
    dense_weight_first,
    dense_weight_second,
    dense_bias,
    dense_stitch,
):
    crops = crop_maps.shape[0]
    in_width = crop_maps.shape[4]
    filter_rows, out_width = filter_weight.shape
    chip, core = lax.axis_index("batch"), lax.axis_index("tower")
    own_level, own_plane = chip // 4, chip % 4
    place = jnp.stack([own_level, own_plane, core]).astype(jnp.int32)
    totals = jnp.sum(crop_counts.reshape(2, -1), axis=1)
    slots = jnp.arange(crops, dtype=jnp.int32)
    mask = (slots[None, :] < totals[:, None]).astype(jnp.float32).reshape(-1)
    rows = 2 * crops
    dense_rows, unit_width = dense_weight.shape[1:]
    half_width = unit_width // 2
    wide = -(-dense_rows // LANES) * LANES
    bias_width = conv_filter_bias.shape[0]
    small_width = bias_width + pool_stitch.shape[0]
    pack_rows = -(-(filter_rows + 1) // 16) * 16
    small = jnp.concatenate([conv_filter_bias, pool_stitch])
    small = jnp.pad(small, (0, (pack_rows - filter_rows) * out_width - small_width))
    packed = jnp.concatenate([filter_weight, small.reshape(-1, out_width)]).astype(jnp.bfloat16)
    maps = jnp.transpose(crop_maps, (1, 2, 3, 0, 4))
    own_packed = jnp.zeros((CUBE,) + packed.shape, packed.dtype)
    for group, blocks in enumerate(gather_plane(gather_levels(packed))):
        for side in range(4):
            for level in range(2):
                owner = chip ^ (4 * (2 * group + level) + SIDES[group][side])
                own_packed = lax.dynamic_update_slice(
                    own_packed, blocks[side, level][None], (owner, 0, 0)
                )
    other_packed = core_swap(own_packed)
    gathered = jnp.where(
        core == 0,
        jnp.stack([own_packed, other_packed], axis=1),
        jnp.stack([other_packed, own_packed], axis=1),
    ).reshape(2 * CUBE, pack_rows, out_width)
    filters = gathered[:, :filter_rows].reshape(2, 3, 3, in_width, out_width)
    small_full = gathered[:, filter_rows, :small_width].astype(jnp.float32)
    smalls = jnp.concatenate(
        [
            small_full[:, :bias_width].reshape(2, out_width),
            small_full[:, bias_width:].reshape(4, out_width),
        ]
    )
    conv = [
        lax.conv_general_dilated(
            maps[tower],
            filters[tower],
            (1, 1),
            ((1, 1), (1, 1)),
            dimension_numbers=("HWNC", "HWIO", "HWNC"),
            preferred_element_type=jnp.float32,
        )
        for tower in range(2)
    ]
    slope_a, slope_b, pooled, sent = mix(place, conv, smalls, wide)
    own_sent = sent[0]
    other_sent = core_swap(sent[1])
    near = []
    for offset in range(4):
        block = jnp.where(
            core == 0,
            jnp.concatenate([own_sent[offset], other_sent[offset]], axis=1),
            jnp.concatenate([other_sent[offset], own_sent[offset]], axis=1),
        )
        near.append(plane_hop(block, offset) if offset else block)
    grad_out = held(cotangent, near[1]).astype(jnp.float32) * mask[:, None, None]
    own_stitch = lax.dynamic_index_in_dim(dense_stitch, core, axis=1, keepdims=False)
    other_stitch = lax.dynamic_index_in_dim(dense_stitch, 1 - core, axis=1, keepdims=False)
    own_grad = jnp.sum(own_stitch * grad_out, axis=1).astype(jnp.bfloat16)
    other_grad = core_swap(jnp.sum(other_stitch * grad_out, axis=1).astype(jnp.bfloat16))
    grad_active = [jnp.where(core == part, own_grad, other_grad) for part in range(2)]
    dense_low = [
        jnp.pad(
            held(dense_weight[0], near[1])[:, part * half_width : (part + 1) * half_width],
            ((0, wide - dense_rows), (0, 0)),
        ).astype(jnp.bfloat16)
        for part in range(2)
    ]
    arrived = []
    for level in range(4):
        block = jnp.stack(
            [
                lax.dynamic_index_in_dim(near[offset], own_level ^ level, axis=0, keepdims=False)
                for offset in SIDES[level // 2]
            ]
        )
        arrived.append(hop(block, level) if level else block)
    columns = [
        jnp.stack(arrived[2 * group : 2 * group + 2], axis=1).reshape(8 * rows, wide)
        for group in range(2)
    ]
    kept, sums = [], [[], []]
    for part in range(2):
        for group in range(2):
            partial = jnp.dot(columns[group], dense_low[part], preferred_element_type=jnp.float32)
            if part:
                partial = held(partial, kept[group])
            partial = partial.astype(jnp.bfloat16).reshape(4, 2, rows, half_width)
            first_sum = reduce_first(partial, group)
            kept.append(first_sum)
            sums[part].append(reduce_second(first_sum, group))
    hidden, grad_full = [], []
    for part in range(2):
        units = slice(part * half_width, (part + 1) * half_width)
        if part:
            sums[1] = [held(group, hidden[0]) for group in sums[1]]
        total = reduce_levels(sums[part]) + dense_bias[:, units]
        if part:
            total = held(total, tops[1])
        hidden.append(total)
        grad_hidden = grad_active[part].astype(jnp.float32) * gate_slope(total)
        tops = gather_levels(grad_hidden.astype(jnp.bfloat16))
        grad_full.append(
            [group.reshape(8 * rows, half_width) for group in gather_plane(tops)]
        )
    active = [smooth_gate(half).astype(jnp.bfloat16) for half in hidden]
    own_active = jnp.where(core == 0, active[0], active[1])
    other_active = core_swap(jnp.where(core == 0, active[1], active[0]))
    own_active = own_active.astype(jnp.float32)[:, None]
    other_active = other_active.astype(jnp.float32)[:, None]
    stitched = own_stitch * own_active + other_stitch * other_active
    stitched = (stitched * mask[:, None, None]).astype(jnp.bfloat16)
    grad_own_stitch = jnp.sum(grad_out * own_active, axis=0)
    grad_other_stitch = jnp.sum(grad_out * other_active, axis=0)
    grad_dense_stitch = jnp.where(
        core == 0,
        jnp.stack([grad_own_stitch, grad_other_stitch], axis=1),
        jnp.stack([grad_other_stitch, grad_own_stitch], axis=1),
    )
    share_rows = -(-grad_dense_stitch.size // (16 * wide)) * 16
    share = jnp.pad(grad_dense_stitch.reshape(-1), (0, share_rows * wide - grad_dense_stitch.size))
    shares = [share.reshape(share_rows, wide).astype(jnp.bfloat16)]
    all_columns = jnp.concatenate(columns).T
    states = (dense_weight, dense_weight_first, dense_weight_second)
    update = dense_update(place, all_columns, grad_full[0], *states, 0, 2, ())
    far = []
    for group in range(2):
        block = sum(
            lax.dot_general(
                grad_full[part][group],
                dense_low[part],
                (((1,), (1,)), ((), ())),
                preferred_element_type=jnp.float32,
            )
            for part in range(2)
        )
        if group:
            block = held(block, update[4])
        block = block.astype(jnp.bfloat16).reshape(4, 2, rows, wide)
        for which in range(2):
            level = 2 * group + which
            part = block[:, which].reshape(4 * rows, wide)
            if level:
                part = hop(jnp.concatenate([part, shares[0]]), level)
                shares.append(part[4 * rows :])
            far.append(part[: 4 * rows].reshape(4, rows, wide))
    shares = [sum_pairs(shares).astype(jnp.bfloat16)]
    update = dense_update(place, all_columns, grad_full[1], *states, 1, 2, update)
    returned = []
    for offset in range(4):
        block = jnp.concatenate([far[level][SIDES[level // 2].index(offset)] for level in range(4)])
        if offset:
            block = plane_hop(held(jnp.concatenate([block, shares[0]]), update[4]), offset)
            shares.append(block[4 * rows :])
        returned.append(block[: 4 * rows])
    grad_dense_stitch = (
        sum_pairs(shares).reshape(-1)[: grad_dense_stitch.size].reshape(grad_dense_stitch.shape)
    )
    returned = jnp.stack(returned).reshape(4, 4, 2, crops, wide)
    own_returned = lax.dynamic_index_in_dim(returned, core, axis=2, keepdims=False)
    other_returned = core_swap(
        lax.dynamic_index_in_dim(returned, 1 - core, axis=2, keepdims=False)
    )
    grad_a, grad_b, grad_small = back(
        place, jnp.stack([own_returned, other_returned]), pooled, smalls, (slope_a, slope_b)
    )
    grad_conv = (grad_a, grad_b)
    weight_dims = lax.ConvDimensionNumbers((3, 2, 0, 1), (3, 2, 0, 1), (2, 3, 0, 1))
    grad_filter_weight = [
        lax.conv_general_dilated(
            maps[tower],
            grad_conv[tower],
            (1, 1),
            ((1, 1), (1, 1)),
            dimension_numbers=weight_dims,
            preferred_element_type=jnp.float32,
        )
        .astype(jnp.bfloat16)
        .reshape(CUBE // 2, 2, filter_rows, out_width)
        for tower in range(2)
    ]
    small_grad = jnp.concatenate(
        [grad_small[:2].reshape(2 * CUBE, -1), grad_small[2:].reshape(2 * CUBE, -1)], axis=1
    )
    scales = 1.0 + jnp.arange(8, dtype=jnp.float32)[:, None] / 8.0
    small_grad = jnp.pad(small_grad[:, None] * scales, ((0, 0), (0, 0), (0, out_width - small_width)))
    small_grad = small_grad.astype(jnp.bfloat16).reshape(CUBE, 2, 8, out_width)
    own_filters, other_filters = (
        jnp.concatenate(
            [
                jnp.concatenate(
                    [
                        lax.dynamic_index_in_dim(
                            grad_filter_weight[tower], which, axis=1, keepdims=False
                        )
                        for tower in range(2)
                    ]
                ),
                lax.dynamic_index_in_dim(small_grad, which, axis=1, keepdims=False),
            ],
            axis=1,
        )
        for which in (core, 1 - core)
    )
    blocks = pair_blocks(place, own_filters, core_swap(other_filters))
    firsts = [reduce_first(blocks[group], group) for group in range(2)]
    groups = [reduce_second(firsts[group], group) for group in range(2)]
    block_sums = reduce_levels(groups)
    filter_sums = block_sums[:filter_rows]
    small_sums = jnp.mean(block_sums[filter_rows:] / scales, axis=0)
    input_grad = jnp.stack(
        [
            held(
                lax.conv_general_dilated(
                    grad_conv[tower],
                    filters[tower][::-1, ::-1],
                    (1, 1),
                    ((1, 1), (1, 1)),
                    dimension_numbers=("HWNC", "HWOI", "HWNC"),
                    preferred_element_type=jnp.float32,
                ),
                (blocks[1] if tower == 0 else firsts[1]),
            ).astype(jnp.bfloat16)
            for tower in range(2)
        ]
    )
    input_grad = jnp.transpose(input_grad, (3, 0, 1, 2, 4))
    return (
        stitched,
        input_grad,
        filter_sums,
        small_sums[:bias_width],
        small_sums[bias_width:small_width],
        update[:4],
        update[4][0],
        grad_dense_stitch,
    )


def local(
    crop_maps,
    cotangent,
    crop_counts,
    filter_weight,
    filter_first,
    filter_second,
    conv_filter_bias,
    conv_filter_bias_mean,
    conv_filter_bias_variance,
    pool_stitch,
    pool_stitch_first,
    pool_stitch_second,
    dense_weight,
    dense_weight_first,
    dense_weight_second,
    dense_bias,
    dense_bias_first,
    dense_bias_second,
    dense_stitch,
    dense_stitch_first,
    dense_stitch_second,
):
    gradients = gradients_cube if lax.axis_size("batch") == CUBE else gradients_any
    (
        stitched,
        input_grad,
        filter_sums,
        filter_bias_sums,
        pool_sums,
        dense_update_outs,
        grad_dense_bias,
        grad_dense_stitch,
    ) = gradients(
        crop_maps,
        cotangent,
        crop_counts,
        filter_weight,
        conv_filter_bias,
        pool_stitch,
        dense_weight,
        dense_weight_first,
        dense_weight_second,
        dense_bias,
        dense_stitch,
    )
    updated_conv_weight, updated_conv_weight_mean, updated_conv_weight_variance = (
        decoupled_adam_step(
            filter_weight, filter_first, filter_second, filter_sums, RATE_FILTER, DECAY
        )
    )
    updated_conv_bias, updated_conv_bias_mean, updated_conv_bias_variance = decoupled_adam_step(
        conv_filter_bias,
        conv_filter_bias_mean,
        conv_filter_bias_variance,
        filter_bias_sums,
        BIAS_LEARN_RATE,
        0.0,
    )
    updated_pooling_stitch, updated_pooling_stitch_mean, updated_pooling_stitch_variance = (
        decoupled_adam_step(
            pool_stitch, pool_stitch_first, pool_stitch_second, pool_sums, RATE_STITCH, 0.0
        )
    )
    updated_dense_bias, updated_dense_bias_mean, updated_dense_bias_variance = decoupled_adam_step(
        dense_bias, dense_bias_first, dense_bias_second, grad_dense_bias[None], BIAS_LEARN_RATE, 0.0
    )
    updated_dense_stitch, updated_dense_stitch_mean, updated_dense_stitch_variance = (
        decoupled_adam_step(
            dense_stitch,
            dense_stitch_first,
            dense_stitch_second,
            grad_dense_stitch,
            RATE_STITCH,
            0.0,
        )
    )
    return (
        stitched,
        input_grad,
        updated_conv_weight,
        updated_conv_weight_mean,
        updated_conv_weight_variance,
        updated_conv_weight.astype(jnp.bfloat16),
        updated_conv_bias,
        updated_conv_bias_mean,
        updated_conv_bias_variance,
        updated_pooling_stitch,
        updated_pooling_stitch_mean,
        updated_pooling_stitch_variance,
        *dense_update_outs,
        updated_dense_bias,
        updated_dense_bias_mean,
        updated_dense_bias_variance,
        updated_dense_stitch,
        updated_dense_stitch_mean,
        updated_dense_stitch_variance,
    )


def solution(mesh):
    in_specs = (
        P(("batch", "tower"), None, None, None, None),
        P("batch", None, "tower"),
        P("batch"),
        P(("batch", "tower"), None),
        P(("batch", "tower"), None),
        P(("batch", "tower"), None),
        P(("batch", "tower")),
        P(("batch", "tower")),
        P(("batch", "tower")),
        P(("batch", "tower")),
        P(("batch", "tower")),
        P(("batch", "tower")),
        P("tower", "batch", None),
        P("tower", "batch", None),
        P("tower", "batch", None),
        P("tower", None),
        P("tower", None),
        P("tower", None),
        P(None, None, "tower"),
        P(None, None, "tower"),
        P(None, None, "tower"),
    )
    out_specs = (
        P("batch", None, "tower"),
        P(("batch", "tower"), None, None, None, None),
        P(("batch", "tower"), None),
        P(("batch", "tower"), None),
        P(("batch", "tower"), None),
        P(("batch", "tower"), None),
        P(("batch", "tower")),
        P(("batch", "tower")),
        P(("batch", "tower")),
        P(("batch", "tower")),
        P(("batch", "tower")),
        P(("batch", "tower")),
        P("tower", "batch", None),
        P("tower", "batch", None),
        P("tower", "batch", None),
        P("tower", "batch", None),
        P("tower", None),
        P("tower", None),
        P("tower", None),
        P(None, None, "tower"),
        P(None, None, "tower"),
        P(None, None, "tower"),
    )
    return jax.shard_map(local, mesh=mesh, in_specs=in_specs, out_specs=out_specs, check_vma=False)
```

```python
import functools

import jax
import jax.numpy as jnp
from jax import lax
from jax.experimental import pallas as pl
from jax.experimental.pallas import tpu as pltpu
from jax.sharding import PartitionSpec as P

STEP = 10


BETA_ONE = 0.5
BETA_TWO = 0.5
EPSILON = 1e-08
DECAY = 0.01
RATE_FILTER = 0.02
RATE_DENSE = 0.02
BIAS_LEARN_RATE = 0.05
RATE_STITCH = 0.2


def smooth_gate(values):
    return jax.nn.gelu(values, approximate=True)


def gate_slope(values):
    return jax.vjp(smooth_gate, values)[1](jnp.ones_like(values))[0]


def pool_mean(active):
    pooled_side = (active.shape[1] - 1) // 2
    span = 2 * pooled_side - 1
    total = jnp.zeros((), jnp.float32)
    for row_start in range(3):
        for col_start in range(3):
            total = total + active[:, row_start : row_start + span : 2, col_start : col_start + span : 2]
    return total / 9.0


def pool_spread(gradient, full_side):
    scaled = gradient / 9.0
    for axis in (1, 2):
        even = jnp.concatenate([scaled, jnp.zeros_like(lax.slice_in_dim(scaled, 0, 1, axis=axis))], axis)
        shifted = jnp.concatenate([jnp.zeros_like(lax.slice_in_dim(scaled, 0, 1, axis=axis)), scaled], axis)
        pairs = jnp.stack([even + shifted, even], axis + 1)
        shape = list(scaled.shape)
        shape[axis] = 2 * shape[axis] + 2
        scaled = lax.slice_in_dim(pairs.reshape(shape), 0, full_side, axis=axis)
    return scaled


def decoupled_adam_step(master, first, second, grad, rate, decay):
    first_new = BETA_ONE * first + (1.0 - BETA_ONE) * grad
    second_new = BETA_TWO * second + (1.0 - BETA_TWO) * grad * grad
    first_hat = first_new / (1.0 - BETA_ONE**STEP)
    second_hat = second_new / (1.0 - BETA_TWO**STEP)
    master_new = master - rate * (first_hat / (jnp.sqrt(second_hat) + EPSILON) + decay * master)
    return (master_new, first_new, second_new)


def core_swap(values):
    return lax.ppermute(values, "tower", [(0, 1), (1, 0)])


def by_core(core, own, other):
    return jnp.where(
        core == 0,
        jnp.concatenate([own, other], axis=-1),
        jnp.concatenate([other, own], axis=-1),
    )


def gradients_any(
    crop_maps,
    cotangent,
    crop_counts,
    filter_weight,
    conv_filter_bias,
    pool_stitch,
    dense_weight,
    dense_weight_first,
    dense_weight_second,
    dense_bias,
    dense_stitch,
):
    block_rows = crop_maps.shape[0]
    side = crop_maps.shape[2]
    in_width = crop_maps.shape[4]
    filter_rows, out_width = filter_weight.shape
    chips = lax.axis_size("batch")
    chip = lax.axis_index("batch")
    core = lax.axis_index("tower")
    totals = jnp.sum(crop_counts.reshape(2, -1), axis=1)
    slots = jnp.arange(block_rows, dtype=jnp.int32)
    mask = (slots[None, :] < totals[:, None]).astype(jnp.float32).reshape(-1)
    pair_rows = 2 * block_rows
    dense_rows, unit_width = dense_weight.shape[1:]
    half_width = unit_width // 2
    bias_width = conv_filter_bias.shape[0]
    small_width = bias_width + pool_stitch.shape[0]
    pack_rows = -(-(filter_rows + 1) // 16) * 16
    small = jnp.concatenate([conv_filter_bias, pool_stitch])
    small = jnp.pad(small, (0, (pack_rows - filter_rows) * out_width - small_width))
    packed = jnp.concatenate([filter_weight, small.reshape(-1, out_width)]).astype(jnp.bfloat16)
    gathered = lax.all_gather(packed, ("batch", "tower"), axis=0)
    filters = gathered[:, :filter_rows].reshape(2, 3, 3, in_width, out_width)
    small_full = gathered[:, filter_rows, :small_width].astype(jnp.float32)
    biases = small_full[:, :bias_width].reshape(2, out_width)
    pool_low = small_full[:, bias_width:].reshape(2, 2, out_width)
    maps = jnp.transpose(crop_maps, (1, 2, 3, 0, 4))
    grad_out = cotangent.astype(jnp.float32) * mask[:, None, None]
    own_stitch = lax.dynamic_index_in_dim(dense_stitch, core, axis=1, keepdims=False)
    other_stitch = lax.dynamic_index_in_dim(dense_stitch, 1 - core, axis=1, keepdims=False)
    own_grad = jnp.sum(own_stitch * grad_out, axis=1).astype(jnp.bfloat16)
    other_grad = core_swap(jnp.sum(other_stitch * grad_out, axis=1).astype(jnp.bfloat16))
    grad_active = by_core(core, own_grad, other_grad)
    dense_low = dense_weight[0].astype(jnp.bfloat16)
    conv = jnp.stack(
        [
            lax.conv_general_dilated(
                maps[tower],
                filters[tower],
                (1, 1),
                ((1, 1), (1, 1)),
                dimension_numbers=("HWNC", "HWIO", "HWNC"),
                preferred_element_type=jnp.float32,
            )
            for tower in range(2)
        ]
    )
    conv = conv + biases[:, None, None, None, :]
    pooled = pool_mean(smooth_gate(conv))
    pooled_side = pooled.shape[1]
    mixed = jnp.sum(pool_low[:, :, None, None, None, :] * pooled[None], axis=1).astype(jnp.bfloat16)
    mixed = jnp.transpose(mixed, (0, 3, 1, 2, 4)).reshape(2, block_rows, chips, dense_rows)
    mixed = jnp.transpose(mixed, (0, 2, 1, 3))
    own_mixed = lax.dynamic_index_in_dim(mixed, core, axis=0, keepdims=False)
    other_mixed = core_swap(lax.dynamic_index_in_dim(mixed, 1 - core, axis=0, keepdims=False))
    features = jnp.where(
        core == 0,
        jnp.concatenate([own_mixed, other_mixed], axis=1),
        jnp.concatenate([other_mixed, own_mixed], axis=1),
    )
    columns = lax.all_to_all(features, "batch", split_axis=0, concat_axis=0, tiled=True)
    columns = columns.reshape(-1, dense_rows)
    partial = jnp.dot(columns, dense_low, preferred_element_type=jnp.float32)
    hidden = lax.psum_scatter(partial, "batch", scatter_dimension=0, tiled=True) + dense_bias
    grad_hidden = (grad_active.astype(jnp.float32) * gate_slope(hidden)).astype(jnp.bfloat16)
    grad_full = lax.all_gather(grad_hidden, "batch", axis=0, tiled=True)
    active = smooth_gate(hidden).astype(jnp.bfloat16)
    own_active = lax.dynamic_slice_in_dim(active, core * half_width, half_width, axis=1)
    other_active = core_swap(
        lax.dynamic_slice_in_dim(active, (1 - core) * half_width, half_width, axis=1)
    )
    own_active = own_active.astype(jnp.float32)[:, None]
    other_active = other_active.astype(jnp.float32)[:, None]
    stitched = own_stitch * own_active + other_stitch * other_active
    stitched = (stitched * mask[:, None, None]).astype(jnp.bfloat16)
    grad_own_stitch = jnp.sum(grad_out * own_active, axis=0)
    grad_other_stitch = jnp.sum(grad_out * other_active, axis=0)
    grad_dense_stitch = lax.psum(
        jnp.where(
            core == 0,
            jnp.stack([grad_own_stitch, grad_other_stitch], axis=1),
            jnp.stack([grad_other_stitch, grad_own_stitch], axis=1),
        ),
        "batch",
    )
    grad_columns = lax.dot_general(
        grad_full, dense_low, (((1,), (1,)), ((), ())), preferred_element_type=jnp.float32
    ).astype(jnp.bfloat16)
    grad_columns = grad_columns.reshape(chips, pair_rows, dense_rows)
    returned = lax.all_to_all(grad_columns, "batch", split_axis=0, concat_axis=0, tiled=True)
    grad_dense_bias = jnp.sum(grad_full.astype(jnp.float32), axis=0)
    grad_dense_weight = lax.dot_general(
        columns, grad_full, (((0,), (0,)), ((), ())), preferred_element_type=jnp.float32
    )
    halves = returned.reshape(chips, 2, block_rows, dense_rows)
    own_mixed = lax.dynamic_index_in_dim(halves, core, axis=1, keepdims=False)
    other_mixed = core_swap(lax.dynamic_index_in_dim(halves, 1 - core, axis=1, keepdims=False))
    grad_mixed = jnp.where(
        core == 0, jnp.stack([own_mixed, other_mixed]), jnp.stack([other_mixed, own_mixed])
    )
    grad_mixed = jnp.transpose(grad_mixed, (0, 2, 1, 3)).reshape(
        2, block_rows, pooled_side, pooled_side, out_width
    )
    grad_mixed = jnp.transpose(grad_mixed, (0, 2, 3, 1, 4)).astype(jnp.float32)
    grad_pool_stitch = jnp.sum(grad_mixed[:, None] * pooled[None], axis=(2, 3, 4))
    grad_pooled = jnp.sum(pool_low[:, :, None, None, None, :] * grad_mixed[:, None], axis=0)
    grad_conv = (pool_spread(grad_pooled, side) * gate_slope(conv)).astype(jnp.bfloat16)
    grad_filter_bias = jnp.sum(grad_conv.astype(jnp.float32), axis=(1, 2, 3))
    weight_dims = lax.ConvDimensionNumbers((3, 2, 0, 1), (3, 2, 0, 1), (2, 3, 0, 1))
    grad_filter_weight = jnp.stack(
        [
            lax.conv_general_dilated(
                maps[tower],
                grad_conv[tower],
                (1, 1),
                ((1, 1), (1, 1)),
                dimension_numbers=weight_dims,
                preferred_element_type=jnp.float32,
            )
            for tower in range(2)
        ]
    )
    filter_sums = lax.psum_scatter(
        grad_filter_weight.reshape(-1, out_width),
        ("batch", "tower"),
        scatter_dimension=0,
        tiled=True,
    )
    small_grad = jnp.concatenate(
        [grad_filter_bias.reshape(2 * chips, -1), grad_pool_stitch.reshape(2 * chips, -1)], axis=1
    )
    small_grad = lax.psum(small_grad, ("batch", "tower"))
    small_grad = lax.dynamic_index_in_dim(small_grad, chip * 2 + core, axis=0, keepdims=False)
    filter_bias_sums = small_grad[:bias_width]
    pool_sums = small_grad[bias_width:]
    input_grad = jnp.stack(
        [
            lax.conv_general_dilated(
                grad_conv[tower],
                filters[tower][::-1, ::-1],
                (1, 1),
                ((1, 1), (1, 1)),
                dimension_numbers=("HWNC", "HWOI", "HWNC"),
                preferred_element_type=jnp.float32,
            ).astype(jnp.bfloat16)
            for tower in range(2)
        ]
    )
    input_grad = jnp.transpose(input_grad, (3, 0, 1, 2, 4))
    update = decoupled_adam_step(
        dense_weight, dense_weight_first, dense_weight_second, grad_dense_weight[None], RATE_DENSE, DECAY
    )
    return (
        stitched,
        input_grad,
        filter_sums,
        filter_bias_sums,
        pool_sums,
        (*update, update[0].astype(jnp.bfloat16)),
        grad_dense_bias,
        grad_dense_stitch,
    )


CUBE = 16
LANES = 128
VMEM_ASKED = 8 << 20
GELU_SCALE = 0.7978845608028654
GELU_CUBIC = 0.044715


def hop(values, level):
    return lax.ppermute(values, "batch", [(i, i ^ (4 * level)) for i in range(CUBE)])


def plane_hop(values, offset):
    return lax.ppermute(values, "batch", [(i, i ^ offset) for i in range(CUBE)])


SIDES = ((0, 1, 2, 3), (0, 2, 1, 3))


def zero_of(values):
    first = values[(0,) * values.ndim]
    return (first != first).astype(jnp.int32)


def held(values, *others):
    zero = sum(zero_of(other) for other in others)
    return jnp.where(zero == 0, values, jnp.zeros((), values.dtype))


def gather_levels(block):
    return [hop(block, level) if level else block for level in range(4)]


def gather_plane(tops, *others):
    groups, halves = [], []
    for group in range(2):
        own = jnp.stack(tops[2 * group : 2 * group + 2])
        if group and others:
            own = held(own, *others)
        half = jnp.stack([own, plane_hop(own, SIDES[group][1])])
        halves.append(half)
        groups.append(jnp.concatenate([half, plane_hop(half, SIDES[group][2])]))
    return groups, halves


def reduce_first(parts, group):
    sent = plane_hop(parts[2:], SIDES[group][2])
    return parts[:2].astype(jnp.float32) + sent.astype(jnp.float32)


def reduce_second(kept, group):
    sent = plane_hop(kept[1].astype(jnp.bfloat16), SIDES[group][1])
    return kept[0] + sent.astype(jnp.float32)


def reduce_levels(groups):
    total = groups[0][0]
    for level in (1, 2, 3):
        part = hop(groups[level // 2][level % 2].astype(jnp.bfloat16), level)
        total = total + part.astype(jnp.float32)
    return total


def on_chip():
    return pl.BlockSpec(memory_space=pltpu.VMEM)


def turn(values):
    return pltpu.roll(values, LANES // 2, axis=1)


def mix_kernel(
    maps_a,
    maps_b,
    small,
    slope_a,
    slope_b,
    pooled,
    sent,
    row_sums,
    means,
):
    side, width, crops, channels = maps_a.shape
    count = (width - 1) // 2

    def gate_row(y, carry):
        for tower, (maps, slopes) in enumerate(((maps_a, slope_a), (maps_b, slope_b))):
            bias = small[tower][None]
            running = [None] * count
            for x in range(width):
                value = maps[y, x] + bias
                square = value * value
                bend = jnp.tanh(GELU_SCALE * value * (1.0 + GELU_CUBIC * square))
                half = 0.5 + 0.5 * bend
                rise = GELU_SCALE * (1.0 + 3.0 * GELU_CUBIC * square)
                slope = half + 0.5 * value * (1.0 - bend * bend) * rise
                slopes[y, x] = slope.astype(jnp.bfloat16)
                gate = value * half
                for place_x in range(max(0, (x - 1) // 2), min(count - 1, x // 2) + 1):
                    old = running[place_x]
                    running[place_x] = gate if old is None else old + gate
            for place_x in range(count):
                row_sums[tower, y, place_x] = running[place_x]
        return carry

    lax.fori_loop(0, side, gate_row, 0)

    def mean_row(row, carry):
        for tower in range(2):
            for place_x in range(count):
                mean = (
                    row_sums[tower, 2 * row, place_x]
                    + row_sums[tower, 2 * row + 1, place_x]
                    + row_sums[tower, 2 * row + 2, place_x]
                ) * (1.0 / 9.0)
                means[tower, row * count + place_x] = mean
                pooled[tower, row * count + place_x] = mean.astype(jnp.bfloat16)
        return carry

    lax.fori_loop(0, count, mean_row, 0)
    low_lanes = lax.broadcasted_iota(jnp.int32, (crops, LANES), 1) < LANES // 2
    halves = small.shape[1] // LANES
    for pair in range(CUBE // 2):
        for tower in range(2):
            tiles = []
            for tile in range(9 * pair, 9 * pair + 9):
                cell, first = tile // halves, tile % halves * LANES
                lanes = slice(first, first + LANES)
                tiles.append(
                    small[2 + 2 * tower, lanes][None] * means[0, cell, :, lanes]
                    + small[3 + 2 * tower, lanes][None] * means[1, cell, :, lanes]
                )
            turned = [turn(tile) for tile in tiles[4:]]
            blank = jnp.zeros_like(tiles[0])
            even = tiles[:4] + [jnp.where(low_lanes, tiles[4], blank)]
            odd = [jnp.where(low_lanes, turned[q], turned[q + 1]) for q in range(4)]
            odd.append(jnp.where(low_lanes, turned[4], blank))
            for chunk, pieces in ((2 * pair, even), (2 * pair + 1, odd)):
                for q, piece in enumerate(pieces):
                    lanes = slice(q * LANES, (q + 1) * LANES)
                    sent[2 * chunk + tower, :, lanes] = piece.astype(jnp.bfloat16)


def mix(conv, small, wide):
    side, _, crops, width = conv[0].shape
    count = (side - 1) // 2
    cells = count * count
    slope = jax.ShapeDtypeStruct(conv[0].shape, jnp.bfloat16)
    pooled = jax.ShapeDtypeStruct((2, cells, crops, width), jnp.bfloat16)
    sent = jax.ShapeDtypeStruct((2 * CUBE, crops, wide), jnp.bfloat16)
    return pl.pallas_call(
        mix_kernel,
        out_shape=(slope, slope, pooled, sent),
        in_specs=[on_chip()] * 3,
        out_specs=(on_chip(),) * 4,
        scratch_shapes=[
            pltpu.VMEM((2, side, count, crops, width), jnp.float32),
            pltpu.VMEM((2, cells, crops, width), jnp.float32),
        ],
        compiler_params=pltpu.CompilerParams(vmem_limit_bytes=VMEM_ASKED),
        cost_estimate=pl.CostEstimate(
            flops=60 * conv[0].size,
            bytes_accessed=12 * conv[0].size,
            transcendentals=2 * conv[0].size,
        ),
        name="gate_pool_mix",
    )(conv[0], conv[1], small)


def back_kernel(
    returned,
    pooled,
    small,
    slope_a,
    slope_b,
    grad_a,
    grad_b,
    grad_small,
    mixed,
    spread,
):
    side, width, crops, channels = slope_a.shape
    count = (width - 1) // 2
    halves = channels // LANES
    low_lanes = lax.broadcasted_iota(jnp.int32, (crops, LANES), 1) < LANES // 2
    for pair in range(CUBE // 2):
        for tower in range(2):
            loaded = []
            for chunk in (2 * pair, 2 * pair + 1):
                source = 2 * chunk + tower
                pieces = []
                for q in range(5):
                    lanes = slice(q * LANES, (q + 1) * LANES)
                    pieces.append(returned[source, :, lanes].astype(jnp.float32))
                loaded.append(pieces)
            even, odd = loaded
            turned = [turn(tile) for tile in odd]
            tiles = even[:4] + [jnp.where(low_lanes, even[4], turned[0])]
            tiles += [jnp.where(low_lanes, turned[q], turned[q + 1]) for q in range(4)]
            for q, tile in enumerate(tiles):
                first = (9 * pair + q) % halves * LANES
                mixed[tower, (9 * pair + q) // halves, :, first : first + LANES] = tile
    blank = jnp.zeros((crops, channels), jnp.float32)
    for tower in range(2):
        for place_x in range(count):
            spread[tower, 0, place_x] = blank
            spread[tower, count + 1, place_x] = blank

    def unmix(row, totals):
        totals = list(totals)
        for place_x in range(count):
            cell = row * count + place_x
            grads = [mixed[tower, cell] for tower in range(2)]
            values = [pooled[tower, cell].astype(jnp.float32) for tower in range(2)]
            for i in range(2):
                for j in range(2):
                    totals[2 * i + j] = totals[2 * i + j] + grads[i] * values[j]
            for j in range(2):
                spread[j, row + 1, place_x] = (
                    small[2 + j][None] * grads[0] + small[4 + j][None] * grads[1]
                ) * (1.0 / 9.0)
        return tuple(totals)

    totals = lax.fori_loop(0, count, unmix, (blank,) * 4)
    for which in range(4):
        grad_small[2 + which] = jnp.sum(totals[which], axis=0)

    def spread_row(y, totals):
        totals = list(totals)
        row = y // 2
        both = (1 - y % 2).astype(jnp.float32)
        for tower, (slopes, grads) in enumerate(((slope_a, grad_a), (slope_b, grad_b))):
            line = [
                spread[tower, row + 1, place_x] + both * spread[tower, row, place_x]
                for place_x in range(count)
            ]
            for x in range(width):
                near = [line[q] for q in range(max(0, (x - 1) // 2), min(count - 1, x // 2) + 1)]
                value = near[0] if len(near) == 1 else near[0] + near[1]
                value = (value * slopes[y, x].astype(jnp.float32)).astype(jnp.bfloat16)
                grads[y, x] = value
                totals[tower] = totals[tower] + value.astype(jnp.float32)
        return tuple(totals)

    totals = lax.fori_loop(0, side, spread_row, (blank,) * 2)
    for tower in range(2):
        grad_small[tower] = jnp.sum(totals[tower], axis=0)


def back(returned, pooled, small, slopes):
    side, _, crops, width = slopes[0].shape
    count = (side - 1) // 2
    grad = jax.ShapeDtypeStruct(slopes[0].shape, jnp.bfloat16)
    return pl.pallas_call(
        back_kernel,
        out_shape=(grad, grad, jax.ShapeDtypeStruct((6, width), jnp.float32)),
        in_specs=[on_chip()] * 5,
        out_specs=(on_chip(),) * 3,
        scratch_shapes=[
            pltpu.VMEM((2, count * count, crops, width), jnp.float32),
            pltpu.VMEM((2, count + 2, count, crops, width), jnp.float32),
        ],
        compiler_params=pltpu.CompilerParams(vmem_limit_bytes=VMEM_ASKED),
        cost_estimate=pl.CostEstimate(
            flops=20 * slopes[0].size, bytes_accessed=8 * slopes[0].size, transcendentals=0
        ),
        name="pool_gradient",
    )(returned, pooled, small, slopes[0], slopes[1])


def order_kernel(place, *refs):
    back = len(refs) == 4
    blocks, groups = (refs[3], refs[:2]) if back else (refs[0], refs[1:])
    chip = 4 * place[0] + place[1]
    rows = blocks.shape[1]
    last = blocks.shape[2] - LANES
    for group in range(2):
        for side in range(4):
            for level in range(2):
                at = chip ^ (4 * (2 * group + level) + SIDES[group][side])
                start = (2 * side + level) * rows
                if back:
                    half = rows // 2
                    for first in (start, start + half):
                        into = pl.ds(first - start, half)
                        blocks[at, into, :last] = groups[group][first : first + half, :last]
                        blocks[at, into, last:] = groups[group][first : first + half, last:] + refs[2][...]
                else:
                    groups[group][start : start + rows] = blocks[at]


def order_rows(place, *arrays):
    if len(arrays) == 1:
        _, rows, width = arrays[0].shape
        outs = [jax.ShapeDtypeStruct((CUBE // 2 * rows, width), arrays[0].dtype)] * 2
    else:
        rows, width = arrays[0].shape
        outs = jax.ShapeDtypeStruct((CUBE, rows // (CUBE // 2), width), arrays[0].dtype)
    size = arrays[0].size * (1 if len(arrays) == 1 else 2)
    return pl.pallas_call(
        order_kernel,
        out_shape=outs,
        in_specs=[pl.BlockSpec(memory_space=pltpu.SMEM)] + [on_chip()] * len(arrays),
        out_specs=[on_chip()] * 2 if len(arrays) == 1 else on_chip(),
        compiler_params=pltpu.CompilerParams(vmem_limit_bytes=VMEM_ASKED),
        cost_estimate=pl.CostEstimate(flops=size, bytes_accessed=4 * size, transcendentals=0),
        name="order_rows",
    )(place, *arrays)


def pair_kernel(place, own, other, blocks_a, blocks_b):
    chip = 4 * place[0] + place[1]
    for group, blocks in enumerate((blocks_a, blocks_b)):
        for side in range(4):
            for level in range(2):
                source = chip ^ (4 * (2 * group + level) + SIDES[group][side])
                total = own[source].astype(jnp.float32) + other[source].astype(jnp.float32)
                blocks[side, level] = total.astype(jnp.bfloat16)


def pair_blocks(place, own, other):
    blocks = jax.ShapeDtypeStruct((4, 2) + own.shape[1:], own.dtype)
    return pl.pallas_call(
        pair_kernel,
        out_shape=(blocks, blocks),
        in_specs=[pl.BlockSpec(memory_space=pltpu.SMEM), on_chip(), on_chip()],
        out_specs=(on_chip(), on_chip()),
        compiler_params=pltpu.CompilerParams(vmem_limit_bytes=VMEM_ASKED),
        cost_estimate=pl.CostEstimate(
            flops=own.size, bytes_accessed=6 * own.size, transcendentals=0
        ),
        name="pair_blocks",
    )(place, own, other)


def dense_kernel(order, columns, grads_a, grads_b, weight, first, second, *outs):
    new_weight, new_first, new_second, copy, grad_bias = outs[-5:]
    rows = grads_a.shape[0]
    grad = jnp.dot(columns[:, :rows], grads_a[...], preferred_element_type=jnp.float32)
    grad += jnp.dot(columns[:, rows:], grads_b[...], preferred_element_type=jnp.float32)
    updated, mean, square = decoupled_adam_step(
        weight[0], first[0], second[0], grad[: weight.shape[1]], RATE_DENSE, DECAY
    )
    new_weight[0] = updated
    new_first[0] = mean
    new_second[0] = square
    copy[0] = updated.astype(jnp.bfloat16)
    grad_bias[...] = jnp.sum(
        grads_a[...].astype(jnp.float32) + grads_b[...].astype(jnp.float32), axis=0, keepdims=True
    )


def dense_update(order, columns, grads, weight, first, second, part, parts, old):
    tile = 1024
    _, rows, units = weight.shape
    steps = units // tile // parts
    state = pl.BlockSpec((1, rows, tile), lambda step: (0, 0, part * steps + step))
    grad = pl.BlockSpec((grads[0].shape[0], tile), lambda step: (0, step))
    outs = [jax.ShapeDtypeStruct(weight.shape, jnp.float32)] * 3
    outs += [
        jax.ShapeDtypeStruct(weight.shape, jnp.bfloat16),
        jax.ShapeDtypeStruct((1, units), jnp.float32),
    ]
    return pl.pallas_call(
        dense_kernel,
        grid=(steps,),
        out_shape=outs,
        in_specs=[
            pl.BlockSpec(memory_space=pltpu.SMEM),
            pl.BlockSpec(columns.shape, lambda step: (0, 0)),
            grad,
            grad,
            state,
            state,
            state,
            *[pl.BlockSpec(memory_space=pl.ANY)] * len(old),
        ],
        out_specs=[state] * 4 + [pl.BlockSpec((1, tile), lambda step: (0, part * steps + step))],
        input_output_aliases={7 + i: i for i in range(len(old))},
        compiler_params=pltpu.CompilerParams(vmem_limit_bytes=48 << 20),
        cost_estimate=pl.CostEstimate(
            flops=2 * columns.size * units // parts,
            bytes_accessed=26 * weight.size // parts,
            transcendentals=weight.size // parts,
        ),
        name="dense_update",
    )(order, columns, *grads, weight, first, second, *old)


def gradients_cube(
    crop_maps,
    cotangent,
    crop_counts,
    filter_weight,
    conv_filter_bias,
    pool_stitch,
    dense_weight,
    dense_weight_first,
    dense_weight_second,
    dense_bias,
    dense_stitch,
):
    crops = crop_maps.shape[0]
    in_width = crop_maps.shape[4]
    filter_rows, out_width = filter_weight.shape
    chip, core = lax.axis_index("batch"), lax.axis_index("tower")
    own_level, own_plane = chip // 4, chip % 4
    place = jnp.stack([own_level, own_plane, core]).astype(jnp.int32)
    totals = jnp.sum(crop_counts.reshape(2, -1), axis=1)
    slots = jnp.arange(crops, dtype=jnp.int32)
    mask = (slots[None, :] < totals[:, None]).astype(jnp.float32).reshape(-1)
    rows = 2 * crops
    dense_rows, unit_width = dense_weight.shape[1:]
    half_width = unit_width // 2
    wide = -(-dense_rows // LANES) * LANES
    bias_width = conv_filter_bias.shape[0]
    small_width = bias_width + pool_stitch.shape[0]
    pack_rows = -(-(filter_rows + 1) // 16) * 16
    small = jnp.concatenate([conv_filter_bias, pool_stitch])
    small = jnp.pad(small, (0, (pack_rows - filter_rows) * out_width - small_width))
    packed = jnp.concatenate([filter_weight, small.reshape(-1, out_width)]).astype(jnp.bfloat16)
    maps = jnp.transpose(crop_maps, (1, 2, 3, 0, 4))
    tops = gather_levels(packed)
    own_packed = jnp.zeros((CUBE,) + packed.shape, packed.dtype)
    for group, blocks in enumerate(gather_plane(tops)[0]):
        for side in range(4):
            for level in range(2):
                owner = chip ^ (4 * (2 * group + level) + SIDES[group][side])
                own_packed = lax.dynamic_update_slice(
                    own_packed, blocks[side, level][None], (owner, 0, 0)
                )
    other_packed = core_swap(own_packed)
    gathered = jnp.where(
        core == 0,
        jnp.stack([own_packed, other_packed], axis=1),
        jnp.stack([other_packed, own_packed], axis=1),
    ).reshape(2 * CUBE, pack_rows, out_width)
    filters = gathered[:, :filter_rows].reshape(2, 3, 3, in_width, out_width)
    small_full = gathered[:, filter_rows, :small_width].astype(jnp.float32)
    smalls = jnp.concatenate(
        [
            small_full[:, :bias_width].reshape(2, out_width),
            small_full[:, bias_width:].reshape(4, out_width),
        ]
    )
    conv = [
        lax.conv_general_dilated(
            maps[tower],
            filters[tower],
            (1, 1),
            ((1, 1), (1, 1)),
            dimension_numbers=("HWNC", "HWIO", "HWNC"),
            preferred_element_type=jnp.float32,
        )
        for tower in range(2)
    ]
    slope_a, slope_b, pooled, sent = mix(conv, smalls, wide)
    arrived = lax.all_to_all(sent, ("batch", "tower"), split_axis=0, concat_axis=0, tiled=True)
    arrived = arrived.reshape(CUBE, rows, wide)
    dense_all = dense_weight[0].astype(jnp.bfloat16)
    dense_low = [
        jnp.pad(
            dense_all[:, part * half_width : (part + 1) * half_width],
            ((0, wide - dense_rows), (0, 0)),
        )
        for part in range(2)
    ]
    columns = order_rows(place, arrived)
    grad_out = cotangent.astype(jnp.float32) * mask[:, None, None]
    own_stitch = lax.dynamic_index_in_dim(dense_stitch, core, axis=1, keepdims=False)
    other_stitch = lax.dynamic_index_in_dim(dense_stitch, 1 - core, axis=1, keepdims=False)
    own_grad = jnp.sum(own_stitch * grad_out, axis=1).astype(jnp.bfloat16)
    other_grad = core_swap(jnp.sum(other_stitch * grad_out, axis=1).astype(jnp.bfloat16))
    grad_active = [jnp.where(core == part, own_grad, other_grad) for part in range(2)]
    kept, sums = [], [[], []]
    for part in range(2):
        for group in range(2):
            partial = jnp.dot(columns[group], dense_low[part], preferred_element_type=jnp.float32)
            if part:
                partial = held(partial, kept[group])
            partial = partial.astype(jnp.bfloat16).reshape(4, 2, rows, half_width)
            first_sum = reduce_first(partial, group)
            kept.append(first_sum)
            sums[part].append(reduce_second(first_sum, group))
    hidden, grad_full = [], []
    for part in range(2):
        units = slice(part * half_width, (part + 1) * half_width)
        if part:
            sums[1] = [held(group, hidden[0]) for group in sums[1]]
        total = reduce_levels(sums[part]) + dense_bias[:, units]
        if part:
            total = held(total, tops[1])
        hidden.append(total)
        grad_hidden = grad_active[part].astype(jnp.float32) * gate_slope(total)
        tops = gather_levels(grad_hidden.astype(jnp.bfloat16))
        gathered, halves = gather_plane(tops)
        grad_full.append([group.reshape(8 * rows, half_width) for group in gathered])
    active = [smooth_gate(half).astype(jnp.bfloat16) for half in hidden]
    own_active = jnp.where(core == 0, active[0], active[1])
    other_active = core_swap(jnp.where(core == 0, active[1], active[0]))
    own_active = own_active.astype(jnp.float32)[:, None]
    other_active = other_active.astype(jnp.float32)[:, None]
    stitched = own_stitch * own_active + other_stitch * other_active
    stitched = (stitched * mask[:, None, None]).astype(jnp.bfloat16)
    grad_own_stitch = jnp.sum(grad_out * own_active, axis=0)
    grad_other_stitch = jnp.sum(grad_out * other_active, axis=0)
    grad_dense_stitch = jnp.where(
        core == 0,
        jnp.stack([grad_own_stitch, grad_other_stitch], axis=1),
        jnp.stack([grad_other_stitch, grad_own_stitch], axis=1),
    )
    share = lax.all_to_all(
        grad_dense_stitch.reshape(CUBE, -1), "batch", split_axis=0, concat_axis=0, tiled=True
    )
    share = jnp.sum(share, axis=0)
    high = lax.reduce_precision(share, 8, 7)
    share = jnp.concatenate([high, share - high]).reshape(crops, -1)
    share = jnp.pad(share, ((0, 0), (LANES - share.shape[1], 0))).astype(jnp.bfloat16)
    sent = [
        sum(
            lax.dot_general(
                grad_full[part][group],
                dense_low[part],
                (((1,), (1,)), ((), ())),
                preferred_element_type=jnp.float32,
            )
            for part in range(2)
        ).astype(jnp.bfloat16)
        for group in range(2)
    ]
    sent = order_rows(place, *sent, share).reshape(2 * CUBE, crops, wide)
    returned = lax.all_to_all(sent, ("batch", "tower"), split_axis=0, concat_axis=0, tiled=True)
    share = returned.reshape(CUBE, 2, crops, wide)[:, :, :, dense_rows:]
    share = jnp.where(core == 0, share[:, 0], share[:, 1]).astype(jnp.float32).reshape(CUBE, 2, -1)
    grad_dense_stitch = (share[:, 0] + share[:, 1]).reshape(grad_dense_stitch.shape)
    all_columns = jnp.concatenate(columns).T
    states = (dense_weight, dense_weight_first, dense_weight_second)
    update = ()
    for part in range(2):
        update = dense_update(place, all_columns, grad_full[part], *states, part, 2, update)
    small_held = held(smalls, update[4][:, half_width:])
    grad_a, grad_b, grad_small = back(returned, pooled, small_held, (slope_a, slope_b))
    grad_conv = (grad_a, grad_b)
    weight_dims = lax.ConvDimensionNumbers((3, 2, 0, 1), (3, 2, 0, 1), (2, 3, 0, 1))
    grad_filter_weight = [
        lax.conv_general_dilated(
            maps[tower],
            grad_conv[tower],
            (1, 1),
            ((1, 1), (1, 1)),
            dimension_numbers=weight_dims,
            preferred_element_type=jnp.float32,
        )
        .astype(jnp.bfloat16)
        .reshape(CUBE // 2, 2, filter_rows, out_width)
        for tower in range(2)
    ]
    small_grad = jnp.concatenate(
        [grad_small[:2].reshape(2 * CUBE, -1), grad_small[2:].reshape(2 * CUBE, -1)], axis=1
    )
    scales = 1.0 + jnp.arange(8, dtype=jnp.float32)[:, None] / 8.0
    small_grad = jnp.pad(small_grad[:, None] * scales, ((0, 0), (0, 0), (0, out_width - small_width)))
    small_grad = small_grad.astype(jnp.bfloat16).reshape(CUBE, 2, 8, out_width)
    own_filters, other_filters = (
        jnp.concatenate(
            [
                jnp.concatenate(
                    [
                        lax.dynamic_index_in_dim(
                            grad_filter_weight[tower], which, axis=1, keepdims=False
                        )
                        for tower in range(2)
                    ]
                ),
                lax.dynamic_index_in_dim(small_grad, which, axis=1, keepdims=False),
            ],
            axis=1,
        )
        for which in (core, 1 - core)
    )
    blocks = pair_blocks(place, own_filters, core_swap(other_filters))
    firsts = [reduce_first(blocks[group], group) for group in range(2)]
    groups = [reduce_second(firsts[group], group) for group in range(2)]
    block_sums = reduce_levels(groups)
    filter_sums = block_sums[:filter_rows]
    small_sums = jnp.mean(block_sums[filter_rows:] / scales, axis=0)
    input_grad = jnp.stack(
        [
            held(
                lax.conv_general_dilated(
                    grad_conv[tower],
                    filters[tower][::-1, ::-1],
                    (1, 1),
                    ((1, 1), (1, 1)),
                    dimension_numbers=("HWNC", "HWOI", "HWNC"),
                    preferred_element_type=jnp.float32,
                ),
                (blocks[1] if tower == 0 else firsts[1]),
            ).astype(jnp.bfloat16)
            for tower in range(2)
        ]
    )
    input_grad = jnp.transpose(input_grad, (3, 0, 1, 2, 4))
    return (
        stitched,
        input_grad,
        filter_sums,
        small_sums[:bias_width],
        small_sums[bias_width:small_width],
        update[:4],
        update[4][0],
        grad_dense_stitch,
    )


def local(
    crop_maps,
    cotangent,
    crop_counts,
    filter_weight,
    filter_first,
    filter_second,
    conv_filter_bias,
    conv_filter_bias_mean,
    conv_filter_bias_variance,
    pool_stitch,
    pool_stitch_first,
    pool_stitch_second,
    dense_weight,
    dense_weight_first,
    dense_weight_second,
    dense_bias,
    dense_bias_first,
    dense_bias_second,
    dense_stitch,
    dense_stitch_first,
    dense_stitch_second,
):
    gradients = gradients_cube if lax.axis_size("batch") == CUBE else gradients_any
    (
        stitched,
        input_grad,
        filter_sums,
        filter_bias_sums,
        pool_sums,
        dense_update_outs,
        grad_dense_bias,
        grad_dense_stitch,
    ) = gradients(
        crop_maps,
        cotangent,
        crop_counts,
        filter_weight,
        conv_filter_bias,
        pool_stitch,
        dense_weight,
        dense_weight_first,
        dense_weight_second,
        dense_bias,
        dense_stitch,
    )
    updated_conv_weight, updated_conv_weight_mean, updated_conv_weight_variance = (
        decoupled_adam_step(
            filter_weight, filter_first, filter_second, filter_sums, RATE_FILTER, DECAY
        )
    )
    updated_conv_bias, updated_conv_bias_mean, updated_conv_bias_variance = decoupled_adam_step(
        conv_filter_bias,
        conv_filter_bias_mean,
        conv_filter_bias_variance,
        filter_bias_sums,
        BIAS_LEARN_RATE,
        0.0,
    )
    updated_pooling_stitch, updated_pooling_stitch_mean, updated_pooling_stitch_variance = (
        decoupled_adam_step(
            pool_stitch, pool_stitch_first, pool_stitch_second, pool_sums, RATE_STITCH, 0.0
        )
    )
    updated_dense_bias, updated_dense_bias_mean, updated_dense_bias_variance = decoupled_adam_step(
        dense_bias, dense_bias_first, dense_bias_second, grad_dense_bias[None], BIAS_LEARN_RATE, 0.0
    )
    updated_dense_stitch, updated_dense_stitch_mean, updated_dense_stitch_variance = (
        decoupled_adam_step(
            dense_stitch,
            dense_stitch_first,
            dense_stitch_second,
            grad_dense_stitch,
            RATE_STITCH,
            0.0,
        )
    )
    return (
        stitched,
        input_grad,
        updated_conv_weight,
        updated_conv_weight_mean,
        updated_conv_weight_variance,
        updated_conv_weight.astype(jnp.bfloat16),
        updated_conv_bias,
        updated_conv_bias_mean,
        updated_conv_bias_variance,
        updated_pooling_stitch,
        updated_pooling_stitch_mean,
        updated_pooling_stitch_variance,
        *dense_update_outs,
        updated_dense_bias,
        updated_dense_bias_mean,
        updated_dense_bias_variance,
        updated_dense_stitch,
        updated_dense_stitch_mean,
        updated_dense_stitch_variance,
    )


def solution(mesh):
    in_specs = (
        P(("batch", "tower"), None, None, None, None),
        P("batch", None, "tower"),
        P("batch"),
        P(("batch", "tower"), None),
        P(("batch", "tower"), None),
        P(("batch", "tower"), None),
        P(("batch", "tower")),
        P(("batch", "tower")),
        P(("batch", "tower")),
        P(("batch", "tower")),
        P(("batch", "tower")),
        P(("batch", "tower")),
        P("tower", "batch", None),
        P("tower", "batch", None),
        P("tower", "batch", None),
        P("tower", None),
        P("tower", None),
        P("tower", None),
        P(None, None, "tower"),
        P(None, None, "tower"),
        P(None, None, "tower"),
    )
    out_specs = (
        P("batch", None, "tower"),
        P(("batch", "tower"), None, None, None, None),
        P(("batch", "tower"), None),
        P(("batch", "tower"), None),
        P(("batch", "tower"), None),
        P(("batch", "tower"), None),
        P(("batch", "tower")),
        P(("batch", "tower")),
        P(("batch", "tower")),
        P(("batch", "tower")),
        P(("batch", "tower")),
        P(("batch", "tower")),
        P("tower", "batch", None),
        P("tower", "batch", None),
        P("tower", "batch", None),
        P("tower", "batch", None),
        P("tower", None),
        P("tower", None),
        P("tower", None),
        P(None, None, "tower"),
        P(None, None, "tower"),
        P(None, None, "tower"),
    )
    return jax.shard_map(local, mesh=mesh, in_specs=in_specs, out_specs=out_specs, check_vma=False)
```

```python
import functools

import jax
import jax.numpy as jnp
from jax import lax
from jax.experimental import pallas as pl
from jax.experimental.pallas import tpu as pltpu
from jax.sharding import PartitionSpec as P

STEP = 10


BETA_ONE = 0.5
BETA_TWO = 0.5
EPSILON = 1e-08
DECAY = 0.01
RATE_FILTER = 0.02
RATE_DENSE = 0.02
BIAS_LEARN_RATE = 0.05
RATE_STITCH = 0.2


def smooth_gate(values):
    return jax.nn.gelu(values, approximate=True)


def gate_slope(values):
    return jax.vjp(smooth_gate, values)[1](jnp.ones_like(values))[0]


def pool_mean(active):
    pooled_side = (active.shape[1] - 1) // 2
    span = 2 * pooled_side - 1
    total = jnp.zeros((), jnp.float32)
    for row_start in range(3):
        for col_start in range(3):
            total = total + active[:, row_start : row_start + span : 2, col_start : col_start + span : 2]
    return total / 9.0


def pool_spread(gradient, full_side):
    scaled = gradient / 9.0
    for axis in (1, 2):
        even = jnp.concatenate([scaled, jnp.zeros_like(lax.slice_in_dim(scaled, 0, 1, axis=axis))], axis)
        shifted = jnp.concatenate([jnp.zeros_like(lax.slice_in_dim(scaled, 0, 1, axis=axis)), scaled], axis)
        pairs = jnp.stack([even + shifted, even], axis + 1)
        shape = list(scaled.shape)
        shape[axis] = 2 * shape[axis] + 2
        scaled = lax.slice_in_dim(pairs.reshape(shape), 0, full_side, axis=axis)
    return scaled


def decoupled_adam_step(master, first, second, grad, rate, decay):
    first_new = BETA_ONE * first + (1.0 - BETA_ONE) * grad
    second_new = BETA_TWO * second + (1.0 - BETA_TWO) * grad * grad
    first_hat = first_new / (1.0 - BETA_ONE**STEP)
    second_hat = second_new / (1.0 - BETA_TWO**STEP)
    master_new = master - rate * (first_hat / (jnp.sqrt(second_hat) + EPSILON) + decay * master)
    return (master_new, first_new, second_new)


def core_swap(values):
    return lax.ppermute(values, "tower", [(0, 1), (1, 0)])


def by_core(core, own, other):
    return jnp.where(
        core == 0,
        jnp.concatenate([own, other], axis=-1),
        jnp.concatenate([other, own], axis=-1),
    )


def gradients_any(
    crop_maps,
    cotangent,
    crop_counts,
    filter_weight,
    conv_filter_bias,
    pool_stitch,
    dense_weight,
    dense_weight_first,
    dense_weight_second,
    dense_bias,
    dense_stitch,
):
    block_rows = crop_maps.shape[0]
    side = crop_maps.shape[2]
    in_width = crop_maps.shape[4]
    filter_rows, out_width = filter_weight.shape
    chips = lax.axis_size("batch")
    chip = lax.axis_index("batch")
    core = lax.axis_index("tower")
    totals = jnp.sum(crop_counts.reshape(2, -1), axis=1)
    slots = jnp.arange(block_rows, dtype=jnp.int32)
    mask = (slots[None, :] < totals[:, None]).astype(jnp.float32).reshape(-1)
    pair_rows = 2 * block_rows
    dense_rows, unit_width = dense_weight.shape[1:]
    half_width = unit_width // 2
    bias_width = conv_filter_bias.shape[0]
    small_width = bias_width + pool_stitch.shape[0]
    pack_rows = -(-(filter_rows + 1) // 16) * 16
    small = jnp.concatenate([conv_filter_bias, pool_stitch])
    small = jnp.pad(small, (0, (pack_rows - filter_rows) * out_width - small_width))
    packed = jnp.concatenate([filter_weight, small.reshape(-1, out_width)]).astype(jnp.bfloat16)
    gathered = lax.all_gather(packed, ("batch", "tower"), axis=0)
    filters = gathered[:, :filter_rows].reshape(2, 3, 3, in_width, out_width)
    small_full = gathered[:, filter_rows, :small_width].astype(jnp.float32)
    biases = small_full[:, :bias_width].reshape(2, out_width)
    pool_low = small_full[:, bias_width:].reshape(2, 2, out_width)
    maps = jnp.transpose(crop_maps, (1, 2, 3, 0, 4))
    grad_out = cotangent.astype(jnp.float32) * mask[:, None, None]
    own_stitch = lax.dynamic_index_in_dim(dense_stitch, core, axis=1, keepdims=False)
    other_stitch = lax.dynamic_index_in_dim(dense_stitch, 1 - core, axis=1, keepdims=False)
    own_grad = jnp.sum(own_stitch * grad_out, axis=1).astype(jnp.bfloat16)
    other_grad = core_swap(jnp.sum(other_stitch * grad_out, axis=1).astype(jnp.bfloat16))
    grad_active = by_core(core, own_grad, other_grad)
    dense_low = dense_weight[0].astype(jnp.bfloat16)
    conv = jnp.stack(
        [
            lax.conv_general_dilated(
                maps[tower],
                filters[tower],
                (1, 1),
                ((1, 1), (1, 1)),
                dimension_numbers=("HWNC", "HWIO", "HWNC"),
                preferred_element_type=jnp.float32,
            )
            for tower in range(2)
        ]
    )
    conv = conv + biases[:, None, None, None, :]
    pooled = pool_mean(smooth_gate(conv))
    pooled_side = pooled.shape[1]
    mixed = jnp.sum(pool_low[:, :, None, None, None, :] * pooled[None], axis=1).astype(jnp.bfloat16)
    mixed = jnp.transpose(mixed, (0, 3, 1, 2, 4)).reshape(2, block_rows, chips, dense_rows)
    mixed = jnp.transpose(mixed, (0, 2, 1, 3))
    own_mixed = lax.dynamic_index_in_dim(mixed, core, axis=0, keepdims=False)
    other_mixed = core_swap(lax.dynamic_index_in_dim(mixed, 1 - core, axis=0, keepdims=False))
    features = jnp.where(
        core == 0,
        jnp.concatenate([own_mixed, other_mixed], axis=1),
        jnp.concatenate([other_mixed, own_mixed], axis=1),
    )
    columns = lax.all_to_all(features, "batch", split_axis=0, concat_axis=0, tiled=True)
    columns = columns.reshape(-1, dense_rows)
    partial = jnp.dot(columns, dense_low, preferred_element_type=jnp.float32)
    hidden = lax.psum_scatter(partial, "batch", scatter_dimension=0, tiled=True) + dense_bias
    grad_hidden = (grad_active.astype(jnp.float32) * gate_slope(hidden)).astype(jnp.bfloat16)
    grad_full = lax.all_gather(grad_hidden, "batch", axis=0, tiled=True)
    active = smooth_gate(hidden).astype(jnp.bfloat16)
    own_active = lax.dynamic_slice_in_dim(active, core * half_width, half_width, axis=1)
    other_active = core_swap(
        lax.dynamic_slice_in_dim(active, (1 - core) * half_width, half_width, axis=1)
    )
    own_active = own_active.astype(jnp.float32)[:, None]
    other_active = other_active.astype(jnp.float32)[:, None]
    stitched = own_stitch * own_active + other_stitch * other_active
    stitched = (stitched * mask[:, None, None]).astype(jnp.bfloat16)
    grad_own_stitch = jnp.sum(grad_out * own_active, axis=0)
    grad_other_stitch = jnp.sum(grad_out * other_active, axis=0)
    grad_dense_stitch = lax.psum(
        jnp.where(
            core == 0,
            jnp.stack([grad_own_stitch, grad_other_stitch], axis=1),
            jnp.stack([grad_other_stitch, grad_own_stitch], axis=1),
        ),
        "batch",
    )
    grad_columns = lax.dot_general(
        grad_full, dense_low, (((1,), (1,)), ((), ())), preferred_element_type=jnp.float32
    ).astype(jnp.bfloat16)
    grad_columns = grad_columns.reshape(chips, pair_rows, dense_rows)
    returned = lax.all_to_all(grad_columns, "batch", split_axis=0, concat_axis=0, tiled=True)
    grad_dense_bias = jnp.sum(grad_full.astype(jnp.float32), axis=0)
    grad_dense_weight = lax.dot_general(
        columns, grad_full, (((0,), (0,)), ((), ())), preferred_element_type=jnp.float32
    )
    halves = returned.reshape(chips, 2, block_rows, dense_rows)
    own_mixed = lax.dynamic_index_in_dim(halves, core, axis=1, keepdims=False)
    other_mixed = core_swap(lax.dynamic_index_in_dim(halves, 1 - core, axis=1, keepdims=False))
    grad_mixed = jnp.where(
        core == 0, jnp.stack([own_mixed, other_mixed]), jnp.stack([other_mixed, own_mixed])
    )
    grad_mixed = jnp.transpose(grad_mixed, (0, 2, 1, 3)).reshape(
        2, block_rows, pooled_side, pooled_side, out_width
    )
    grad_mixed = jnp.transpose(grad_mixed, (0, 2, 3, 1, 4)).astype(jnp.float32)
    grad_pool_stitch = jnp.sum(grad_mixed[:, None] * pooled[None], axis=(2, 3, 4))
    grad_pooled = jnp.sum(pool_low[:, :, None, None, None, :] * grad_mixed[:, None], axis=0)
    grad_conv = (pool_spread(grad_pooled, side) * gate_slope(conv)).astype(jnp.bfloat16)
    grad_filter_bias = jnp.sum(grad_conv.astype(jnp.float32), axis=(1, 2, 3))
    weight_dims = lax.ConvDimensionNumbers((3, 2, 0, 1), (3, 2, 0, 1), (2, 3, 0, 1))
    grad_filter_weight = jnp.stack(
        [
            lax.conv_general_dilated(
                maps[tower],
                grad_conv[tower],
                (1, 1),
                ((1, 1), (1, 1)),
                dimension_numbers=weight_dims,
                preferred_element_type=jnp.float32,
            )
            for tower in range(2)
        ]
    )
    filter_sums = lax.psum_scatter(
        grad_filter_weight.reshape(-1, out_width),
        ("batch", "tower"),
        scatter_dimension=0,
        tiled=True,
    )
    small_grad = jnp.concatenate(
        [grad_filter_bias.reshape(2 * chips, -1), grad_pool_stitch.reshape(2 * chips, -1)], axis=1
    )
    small_grad = lax.psum(small_grad, ("batch", "tower"))
    small_grad = lax.dynamic_index_in_dim(small_grad, chip * 2 + core, axis=0, keepdims=False)
    filter_bias_sums = small_grad[:bias_width]
    pool_sums = small_grad[bias_width:]
    input_grad = jnp.stack(
        [
            lax.conv_general_dilated(
                grad_conv[tower],
                filters[tower][::-1, ::-1],
                (1, 1),
                ((1, 1), (1, 1)),
                dimension_numbers=("HWNC", "HWOI", "HWNC"),
                preferred_element_type=jnp.float32,
            ).astype(jnp.bfloat16)
            for tower in range(2)
        ]
    )
    input_grad = jnp.transpose(input_grad, (3, 0, 1, 2, 4))
    update = decoupled_adam_step(
        dense_weight, dense_weight_first, dense_weight_second, grad_dense_weight[None], RATE_DENSE, DECAY
    )
    return (
        stitched,
        input_grad,
        filter_sums,
        filter_bias_sums,
        pool_sums,
        (*update, update[0].astype(jnp.bfloat16)),
        grad_dense_bias,
        grad_dense_stitch,
    )


CUBE = 16
LANES = 128
VMEM_ASKED = 8 << 20
GELU_SCALE = 0.7978845608028654
GELU_CUBIC = 0.044715


def hop(values, level):
    return lax.ppermute(values, "batch", [(i, i ^ (4 * level)) for i in range(CUBE)])


def plane_hop(values, offset):
    return lax.ppermute(values, "batch", [(i, i ^ offset) for i in range(CUBE)])


SIDES = ((0, 1, 2, 3), (0, 2, 1, 3))


def zero_of(values):
    first = values[(0,) * values.ndim]
    return (first != first).astype(jnp.int32)


def held(values, *others):
    zero = sum(zero_of(other) for other in others)
    return jnp.where(zero == 0, values, jnp.zeros((), values.dtype))


def gather_levels(block):
    return [hop(block, level) if level else block for level in range(4)]


def gather_plane(tops, *others):
    groups, halves = [], []
    for group in range(2):
        own = jnp.stack(tops[2 * group : 2 * group + 2])
        if group and others:
            own = held(own, *others)
        half = jnp.stack([own, plane_hop(own, SIDES[group][1])])
        halves.append(half)
        groups.append(jnp.concatenate([half, plane_hop(half, SIDES[group][2])]))
    return groups, halves


def reduce_first(parts, group):
    sent = plane_hop(parts[2:], SIDES[group][2])
    return parts[:2].astype(jnp.float32) + sent.astype(jnp.float32)


def reduce_second(kept, group):
    sent = plane_hop(kept[1].astype(jnp.bfloat16), SIDES[group][1])
    return kept[0] + sent.astype(jnp.float32)


def reduce_levels(groups):
    total = groups[0][0]
    for level in (1, 2, 3):
        part = hop(groups[level // 2][level % 2].astype(jnp.bfloat16), level)
        total = total + part.astype(jnp.float32)
    return total


def on_chip():
    return pl.BlockSpec(memory_space=pltpu.VMEM)


def turn(values):
    return pltpu.roll(values, LANES // 2, axis=1)


def mix_kernel(
    maps_a,
    maps_b,
    small,
    slope_a,
    slope_b,
    pooled,
    sent,
    row_sums,
    means,
):
    side, width, crops, channels = maps_a.shape
    count = (width - 1) // 2

    def gate_row(y, carry):
        for tower, (maps, slopes) in enumerate(((maps_a, slope_a), (maps_b, slope_b))):
            bias = small[tower][None]
            running = [None] * count
            for x in range(width):
                value = maps[y, x].astype(jnp.float32) + bias
                square = value * value
                bend = jnp.tanh(GELU_SCALE * value * (1.0 + GELU_CUBIC * square))
                half = 0.5 + 0.5 * bend
                rise = GELU_SCALE * (1.0 + 3.0 * GELU_CUBIC * square)
                slope = half + 0.5 * value * (1.0 - bend * bend) * rise
                slopes[y, x] = slope.astype(jnp.bfloat16)
                gate = value * half
                for place_x in range(max(0, (x - 1) // 2), min(count - 1, x // 2) + 1):
                    old = running[place_x]
                    running[place_x] = gate if old is None else old + gate
            for place_x in range(count):
                row_sums[tower, y, place_x] = running[place_x]
        return carry

    lax.fori_loop(0, side, gate_row, 0)

    def mean_row(row, carry):
        for tower in range(2):
            for place_x in range(count):
                mean = (
                    row_sums[tower, 2 * row, place_x]
                    + row_sums[tower, 2 * row + 1, place_x]
                    + row_sums[tower, 2 * row + 2, place_x]
                ) * (1.0 / 9.0)
                means[tower, row * count + place_x] = mean
                pooled[tower, row * count + place_x] = mean.astype(jnp.bfloat16)
        return carry

    lax.fori_loop(0, count, mean_row, 0)
    low_lanes = lax.broadcasted_iota(jnp.int32, (crops, LANES), 1) < LANES // 2
    halves = small.shape[1] // LANES
    for pair in range(CUBE // 2):
        for tower in range(2):
            tiles = []
            for tile in range(9 * pair, 9 * pair + 9):
                cell, first = tile // halves, tile % halves * LANES
                lanes = slice(first, first + LANES)
                tiles.append(
                    small[2 + 2 * tower, lanes][None] * means[0, cell, :, lanes]
                    + small[3 + 2 * tower, lanes][None] * means[1, cell, :, lanes]
                )
            turned = [turn(tile) for tile in tiles[4:]]
            blank = jnp.zeros_like(tiles[0])
            even = tiles[:4] + [jnp.where(low_lanes, tiles[4], blank)]
            odd = [jnp.where(low_lanes, turned[q], turned[q + 1]) for q in range(4)]
            odd.append(jnp.where(low_lanes, turned[4], blank))
            for chunk, pieces in ((2 * pair, even), (2 * pair + 1, odd)):
                for q, piece in enumerate(pieces):
                    lanes = slice(q * LANES, (q + 1) * LANES)
                    sent[2 * chunk + tower, :, lanes] = piece.astype(jnp.bfloat16)


def mix(conv, small, wide):
    side, _, crops, width = conv[0].shape
    count = (side - 1) // 2
    cells = count * count
    slope = jax.ShapeDtypeStruct(conv[0].shape, jnp.bfloat16)
    pooled = jax.ShapeDtypeStruct((2, cells, crops, width), jnp.bfloat16)
    sent = jax.ShapeDtypeStruct((2 * CUBE, crops, wide), jnp.bfloat16)
    return pl.pallas_call(
        mix_kernel,
        out_shape=(slope, slope, pooled, sent),
        in_specs=[on_chip()] * 3,
        out_specs=(on_chip(),) * 4,
        scratch_shapes=[
            pltpu.VMEM((2, side, count, crops, width), jnp.float32),
            pltpu.VMEM((2, cells, crops, width), jnp.float32),
        ],
        compiler_params=pltpu.CompilerParams(vmem_limit_bytes=VMEM_ASKED),
        cost_estimate=pl.CostEstimate(
            flops=60 * conv[0].size,
            bytes_accessed=12 * conv[0].size,
            transcendentals=2 * conv[0].size,
        ),
        name="gate_pool_mix",
    )(conv[0], conv[1], small)


def back_kernel(
    returned,
    pooled,
    small,
    slope_a,
    slope_b,
    grad_a,
    grad_b,
    grad_small,
    mixed,
    spread,
):
    side, width, crops, channels = slope_a.shape
    count = (width - 1) // 2
    halves = channels // LANES
    low_lanes = lax.broadcasted_iota(jnp.int32, (crops, LANES), 1) < LANES // 2
    for pair in range(CUBE // 2):
        for tower in range(2):
            loaded = []
            for chunk in (2 * pair, 2 * pair + 1):
                source = 2 * chunk + tower
                pieces = []
                for q in range(5):
                    lanes = slice(q * LANES, (q + 1) * LANES)
                    pieces.append(returned[source, :, lanes].astype(jnp.float32))
                loaded.append(pieces)
            even, odd = loaded
            turned = [turn(tile) for tile in odd]
            tiles = even[:4] + [jnp.where(low_lanes, even[4], turned[0])]
            tiles += [jnp.where(low_lanes, turned[q], turned[q + 1]) for q in range(4)]
            for q, tile in enumerate(tiles):
                first = (9 * pair + q) % halves * LANES
                mixed[tower, (9 * pair + q) // halves, :, first : first + LANES] = tile
    blank = jnp.zeros((crops, channels), jnp.float32)
    for tower in range(2):
        for place_x in range(count):
            spread[tower, 0, place_x] = blank
            spread[tower, count + 1, place_x] = blank

    def unmix(row, totals):
        totals = list(totals)
        for place_x in range(count):
            cell = row * count + place_x
            grads = [mixed[tower, cell] for tower in range(2)]
            values = [pooled[tower, cell].astype(jnp.float32) for tower in range(2)]
            for i in range(2):
                for j in range(2):
                    totals[2 * i + j] = totals[2 * i + j] + grads[i] * values[j]
            for j in range(2):
                spread[j, row + 1, place_x] = (
                    small[2 + j][None] * grads[0] + small[4 + j][None] * grads[1]
                ) * (1.0 / 9.0)
        return tuple(totals)

    totals = lax.fori_loop(0, count, unmix, (blank,) * 4)
    for which in range(4):
        grad_small[2 + which] = jnp.sum(totals[which], axis=0)

    def spread_row(y, totals):
        totals = list(totals)
        row = y // 2
        both = (1 - y % 2).astype(jnp.float32)
        for tower, (slopes, grads) in enumerate(((slope_a, grad_a), (slope_b, grad_b))):
            line = [
                spread[tower, row + 1, place_x] + both * spread[tower, row, place_x]
                for place_x in range(count)
            ]
            for x in range(width):
                near = [line[q] for q in range(max(0, (x - 1) // 2), min(count - 1, x // 2) + 1)]
                value = near[0] if len(near) == 1 else near[0] + near[1]
                value = (value * slopes[y, x].astype(jnp.float32)).astype(jnp.bfloat16)
                grads[y, x] = value
                totals[tower] = totals[tower] + value.astype(jnp.float32)
        return tuple(totals)

    totals = lax.fori_loop(0, side, spread_row, (blank,) * 2)
    for tower in range(2):
        grad_small[tower] = jnp.sum(totals[tower], axis=0)


def back(returned, pooled, small, slopes):
    side, _, crops, width = slopes[0].shape
    count = (side - 1) // 2
    grad = jax.ShapeDtypeStruct(slopes[0].shape, jnp.bfloat16)
    return pl.pallas_call(
        back_kernel,
        out_shape=(grad, grad, jax.ShapeDtypeStruct((6, width), jnp.float32)),
        in_specs=[on_chip()] * 5,
        out_specs=(on_chip(),) * 3,
        scratch_shapes=[
            pltpu.VMEM((2, count * count, crops, width), jnp.float32),
            pltpu.VMEM((2, count + 2, count, crops, width), jnp.float32),
        ],
        compiler_params=pltpu.CompilerParams(vmem_limit_bytes=VMEM_ASKED),
        cost_estimate=pl.CostEstimate(
            flops=20 * slopes[0].size, bytes_accessed=8 * slopes[0].size, transcendentals=0
        ),
        name="pool_gradient",
    )(returned, pooled, small, slopes[0], slopes[1])


def order_kernel(place, *refs):
    back = len(refs) == 4
    blocks, groups = (refs[3], refs[:2]) if back else (refs[0], refs[1:])
    chip = 4 * place[0] + place[1]
    rows = blocks.shape[1]
    last = blocks.shape[2] - LANES
    for group in range(2):
        for side in range(4):
            for level in range(2):
                at = chip ^ (4 * (2 * group + level) + SIDES[group][side])
                start = (2 * side + level) * rows
                if back:
                    half = rows // 2
                    for first in (start, start + half):
                        into = pl.ds(first - start, half)
                        blocks[at, into, :last] = groups[group][first : first + half, :last]
                        blocks[at, into, last:] = groups[group][first : first + half, last:] + refs[2][...]
                else:
                    groups[group][start : start + rows] = blocks[at]


def order_rows(place, *arrays):
    if len(arrays) == 1:
        _, rows, width = arrays[0].shape
        outs = [jax.ShapeDtypeStruct((CUBE // 2 * rows, width), arrays[0].dtype)] * 2
    else:
        rows, width = arrays[0].shape
        outs = jax.ShapeDtypeStruct((CUBE, rows // (CUBE // 2), width), arrays[0].dtype)
    size = arrays[0].size * (1 if len(arrays) == 1 else 2)
    return pl.pallas_call(
        order_kernel,
        out_shape=outs,
        in_specs=[pl.BlockSpec(memory_space=pltpu.SMEM)] + [on_chip()] * len(arrays),
        out_specs=[on_chip()] * 2 if len(arrays) == 1 else on_chip(),
        compiler_params=pltpu.CompilerParams(vmem_limit_bytes=VMEM_ASKED),
        cost_estimate=pl.CostEstimate(flops=size, bytes_accessed=4 * size, transcendentals=0),
        name="order_rows",
    )(place, *arrays)


def pair_kernel(place, own, other, blocks_a, blocks_b):
    chip = 4 * place[0] + place[1]
    for group, blocks in enumerate((blocks_a, blocks_b)):
        for side in range(4):
            for level in range(2):
                source = chip ^ (4 * (2 * group + level) + SIDES[group][side])
                total = own[source].astype(jnp.float32) + other[source].astype(jnp.float32)
                blocks[side, level] = total.astype(jnp.bfloat16)


def pair_blocks(place, own, other):
    blocks = jax.ShapeDtypeStruct((4, 2) + own.shape[1:], own.dtype)
    return pl.pallas_call(
        pair_kernel,
        out_shape=(blocks, blocks),
        in_specs=[pl.BlockSpec(memory_space=pltpu.SMEM), on_chip(), on_chip()],
        out_specs=(on_chip(), on_chip()),
        compiler_params=pltpu.CompilerParams(vmem_limit_bytes=VMEM_ASKED),
        cost_estimate=pl.CostEstimate(
            flops=own.size, bytes_accessed=6 * own.size, transcendentals=0
        ),
        name="pair_blocks",
    )(place, own, other)


def dense_kernel(columns_a, columns_b, *refs):
    weight, first, second, new_weight, new_first, new_second, copy, grad_bias = refs[4:]
    early = pl.program_id(0) < pl.num_programs(0) // 2
    grads = [jnp.where(early, refs[group][...], refs[2 + group][...]) for group in range(2)]
    grad = sum(
        lax.dot_general(
            columns[...], part, (((0,), (0,)), ((), ())), preferred_element_type=jnp.float32
        )
        for columns, part in zip((columns_a, columns_b), grads)
    )
    updated, mean, square = decoupled_adam_step(
        weight[0], first[0], second[0], grad[: weight.shape[1]], RATE_DENSE, DECAY
    )
    new_weight[0] = updated
    new_first[0] = mean
    new_second[0] = square
    copy[0] = updated.astype(jnp.bfloat16)
    grad_bias[...] = jnp.sum(
        grads[0].astype(jnp.float32) + grads[1].astype(jnp.float32), axis=0, keepdims=True
    )


def dense_update(columns, grads, weight, first, second):
    tile = 1024
    _, rows, units = weight.shape
    steps = units // tile
    half = steps // 2
    state = pl.BlockSpec((1, rows, tile), lambda step: (0, 0, step))
    block = (grads[0][0].shape[0], tile)
    early = pl.BlockSpec(block, lambda step: (0, jnp.minimum(step, half - 1)))
    late = pl.BlockSpec(block, lambda step: (0, jnp.maximum(step - half, 0)))
    outs = [jax.ShapeDtypeStruct(weight.shape, jnp.float32)] * 3
    outs += [
        jax.ShapeDtypeStruct(weight.shape, jnp.bfloat16),
        jax.ShapeDtypeStruct((1, units), jnp.float32),
    ]
    return pl.pallas_call(
        dense_kernel,
        grid=(steps,),
        out_shape=outs,
        in_specs=[
            *[pl.BlockSpec(columns[0].shape, lambda step: (0, 0))] * 2,
            early,
            early,
            late,
            late,
            state,
            state,
            state,
        ],
        out_specs=[state] * 4 + [pl.BlockSpec((1, tile), lambda step: (0, step))],
        compiler_params=pltpu.CompilerParams(vmem_limit_bytes=48 << 20),
        cost_estimate=pl.CostEstimate(
            flops=4 * columns[0].size * units,
            bytes_accessed=26 * weight.size,
            transcendentals=weight.size,
        ),
        name="dense_update",
    )(*columns, *grads[0], *grads[1], weight, first, second)


def gradients_cube(
    crop_maps,
    cotangent,
    crop_counts,
    filter_weight,
    conv_filter_bias,
    pool_stitch,
    dense_weight,
    dense_weight_first,
    dense_weight_second,
    dense_bias,
    dense_stitch,
):
    crops = crop_maps.shape[0]
    in_width = crop_maps.shape[4]
    filter_rows, out_width = filter_weight.shape
    chip, core = lax.axis_index("batch"), lax.axis_index("tower")
    own_level, own_plane = chip // 4, chip % 4
    place = jnp.stack([own_level, own_plane, core]).astype(jnp.int32)
    totals = jnp.sum(crop_counts.reshape(2, -1), axis=1)
    slots = jnp.arange(crops, dtype=jnp.int32)
    mask = (slots[None, :] < totals[:, None]).astype(jnp.float32).reshape(-1)
    rows = 2 * crops
    dense_rows, unit_width = dense_weight.shape[1:]
    half_width = unit_width // 2
    wide = -(-dense_rows // LANES) * LANES
    bias_width = conv_filter_bias.shape[0]
    small_width = bias_width + pool_stitch.shape[0]
    pack_rows = -(-(filter_rows + 1) // 16) * 16
    small = jnp.concatenate([conv_filter_bias, pool_stitch])
    small = jnp.pad(small, (0, (pack_rows - filter_rows) * out_width - small_width))
    packed = jnp.concatenate([filter_weight, small.reshape(-1, out_width)]).astype(jnp.bfloat16)
    maps = jnp.transpose(crop_maps, (1, 2, 3, 0, 4))
    tops = gather_levels(packed)
    own_packed = jnp.zeros((CUBE,) + packed.shape, packed.dtype)
    for group, blocks in enumerate(gather_plane(tops)[0]):
        for side in range(4):
            for level in range(2):
                owner = chip ^ (4 * (2 * group + level) + SIDES[group][side])
                own_packed = lax.dynamic_update_slice(
                    own_packed, blocks[side, level][None], (owner, 0, 0)
                )
    other_packed = core_swap(own_packed)
    gathered = jnp.where(
        core == 0,
        jnp.stack([own_packed, other_packed], axis=1),
        jnp.stack([other_packed, own_packed], axis=1),
    ).reshape(2 * CUBE, pack_rows, out_width)
    filters = gathered[:, :filter_rows].reshape(2, 3, 3, in_width, out_width)
    small_full = gathered[:, filter_rows, :small_width].astype(jnp.float32)
    smalls = jnp.concatenate(
        [
            small_full[:, :bias_width].reshape(2, out_width),
            small_full[:, bias_width:].reshape(4, out_width),
        ]
    )
    conv = [
        lax.conv_general_dilated(
            maps[tower],
            filters[tower],
            (1, 1),
            ((1, 1), (1, 1)),
            dimension_numbers=("HWNC", "HWIO", "HWNC"),
            preferred_element_type=jnp.float32,
        ).astype(jnp.bfloat16)
        for tower in range(2)
    ]
    slope_a, slope_b, pooled, sent = mix(conv, smalls, wide)
    arrived = lax.all_to_all(sent, ("batch", "tower"), split_axis=0, concat_axis=0, tiled=True)
    arrived = arrived.reshape(CUBE, rows, wide)
    dense_all = dense_weight[0].astype(jnp.bfloat16)
    dense_low = [
        jnp.pad(
            dense_all[:, part * half_width : (part + 1) * half_width],
            ((0, wide - dense_rows), (0, 0)),
        )
        for part in range(2)
    ]
    columns = order_rows(place, arrived)
    grad_out = cotangent.astype(jnp.float32) * mask[:, None, None]
    own_stitch = lax.dynamic_index_in_dim(dense_stitch, core, axis=1, keepdims=False)
    other_stitch = lax.dynamic_index_in_dim(dense_stitch, 1 - core, axis=1, keepdims=False)
    own_grad = jnp.sum(own_stitch * grad_out, axis=1).astype(jnp.bfloat16)
    other_grad = core_swap(jnp.sum(other_stitch * grad_out, axis=1).astype(jnp.bfloat16))
    grad_active = [jnp.where(core == part, own_grad, other_grad) for part in range(2)]
    kept, sums = [], [[], []]
    for part in range(2):
        for group in range(2):
            partial = jnp.dot(columns[group], dense_low[part], preferred_element_type=jnp.float32)
            if part:
                partial = held(partial, kept[group])
            partial = partial.astype(jnp.bfloat16).reshape(4, 2, rows, half_width)
            first_sum = reduce_first(partial, group)
            kept.append(first_sum)
            sums[part].append(reduce_second(first_sum, group))
    hidden, grad_full = [], []
    for part in range(2):
        units = slice(part * half_width, (part + 1) * half_width)
        if part:
            sums[1] = [held(group, hidden[0]) for group in sums[1]]
        total = reduce_levels(sums[part]) + dense_bias[:, units]
        if part:
            total = held(total, tops[1])
        hidden.append(total)
        grad_hidden = grad_active[part].astype(jnp.float32) * gate_slope(total)
        tops = gather_levels(grad_hidden.astype(jnp.bfloat16))
        gathered, halves = gather_plane(tops)
        grad_full.append([group.reshape(8 * rows, half_width) for group in gathered])
    active = [smooth_gate(half).astype(jnp.bfloat16) for half in hidden]
    own_active = jnp.where(core == 0, active[0], active[1])
    other_active = core_swap(jnp.where(core == 0, active[1], active[0]))
    own_active = own_active.astype(jnp.float32)[:, None]
    other_active = other_active.astype(jnp.float32)[:, None]
    stitched = own_stitch * own_active + other_stitch * other_active
    stitched = (stitched * mask[:, None, None]).astype(jnp.bfloat16)
    grad_own_stitch = jnp.sum(grad_out * own_active, axis=0)
    grad_other_stitch = jnp.sum(grad_out * other_active, axis=0)
    grad_dense_stitch = jnp.where(
        core == 0,
        jnp.stack([grad_own_stitch, grad_other_stitch], axis=1),
        jnp.stack([grad_other_stitch, grad_own_stitch], axis=1),
    )
    share = lax.all_to_all(
        grad_dense_stitch.reshape(CUBE, -1), "batch", split_axis=0, concat_axis=0, tiled=True
    )
    share = jnp.sum(share, axis=0)
    high = lax.reduce_precision(share, 8, 7)
    share = jnp.concatenate([high, share - high]).reshape(crops, -1)
    share = jnp.pad(share, ((0, 0), (LANES - share.shape[1], 0))).astype(jnp.bfloat16)
    sent = [
        sum(
            lax.dot_general(
                grad_full[part][group],
                dense_low[part],
                (((1,), (1,)), ((), ())),
                preferred_element_type=jnp.float32,
            )
            for part in range(2)
        ).astype(jnp.bfloat16)
        for group in range(2)
    ]
    sent = order_rows(place, *sent, share).reshape(2 * CUBE, crops, wide)
    returned = lax.all_to_all(sent, ("batch", "tower"), split_axis=0, concat_axis=0, tiled=True)
    share = returned.reshape(CUBE, 2, crops, wide)[:, :, :, dense_rows:]
    share = jnp.where(core == 0, share[:, 0], share[:, 1]).astype(jnp.float32).reshape(CUBE, 2, -1)
    grad_dense_stitch = (share[:, 0] + share[:, 1]).reshape(grad_dense_stitch.shape)
    update = dense_update(
        columns, grad_full, dense_weight, dense_weight_first, dense_weight_second
    )
    small_held = held(smalls, update[4])
    grad_a, grad_b, grad_small = back(returned, pooled, small_held, (slope_a, slope_b))
    grad_conv = (grad_a, grad_b)
    weight_dims = lax.ConvDimensionNumbers((3, 2, 0, 1), (3, 2, 0, 1), (2, 3, 0, 1))
    grad_filter_weight = [
        lax.conv_general_dilated(
            maps[tower],
            grad_conv[tower],
            (1, 1),
            ((1, 1), (1, 1)),
            dimension_numbers=weight_dims,
            preferred_element_type=jnp.float32,
        )
        .astype(jnp.bfloat16)
        .reshape(CUBE // 2, 2, filter_rows, out_width)
        for tower in range(2)
    ]
    small_grad = jnp.concatenate(
        [grad_small[:2].reshape(2 * CUBE, -1), grad_small[2:].reshape(2 * CUBE, -1)], axis=1
    )
    scales = 1.0 + jnp.arange(8, dtype=jnp.float32)[:, None] / 8.0
    small_grad = jnp.pad(small_grad[:, None] * scales, ((0, 0), (0, 0), (0, out_width - small_width)))
    small_grad = small_grad.astype(jnp.bfloat16).reshape(CUBE, 2, 8, out_width)
    own_filters, other_filters = (
        jnp.concatenate(
            [
                jnp.concatenate(
                    [
                        lax.dynamic_index_in_dim(
                            grad_filter_weight[tower], which, axis=1, keepdims=False
                        )
                        for tower in range(2)
                    ]
                ),
                lax.dynamic_index_in_dim(small_grad, which, axis=1, keepdims=False),
            ],
            axis=1,
        )
        for which in (core, 1 - core)
    )
    blocks = pair_blocks(place, own_filters, core_swap(other_filters))
    firsts = [reduce_first(blocks[group], group) for group in range(2)]
    groups = [reduce_second(firsts[group], group) for group in range(2)]
    block_sums = reduce_levels(groups)
    filter_sums = block_sums[:filter_rows]
    small_sums = jnp.mean(block_sums[filter_rows:] / scales, axis=0)
    input_grad = jnp.stack(
        [
            held(
                lax.conv_general_dilated(
                    grad_conv[tower],
                    filters[tower][::-1, ::-1],
                    (1, 1),
                    ((1, 1), (1, 1)),
                    dimension_numbers=("HWNC", "HWOI", "HWNC"),
                    preferred_element_type=jnp.float32,
                ),
                (blocks[1] if tower == 0 else firsts[1]),
            ).astype(jnp.bfloat16)
            for tower in range(2)
        ]
    )
    input_grad = jnp.transpose(input_grad, (3, 0, 1, 2, 4))
    return (
        stitched,
        input_grad,
        filter_sums,
        small_sums[:bias_width],
        small_sums[bias_width:small_width],
        update[:4],
        update[4][0],
        grad_dense_stitch,
    )


def local(
    crop_maps,
    cotangent,
    crop_counts,
    filter_weight,
    filter_first,
    filter_second,
    conv_filter_bias,
    conv_filter_bias_mean,
    conv_filter_bias_variance,
    pool_stitch,
    pool_stitch_first,
    pool_stitch_second,
    dense_weight,
    dense_weight_first,
    dense_weight_second,
    dense_bias,
    dense_bias_first,
    dense_bias_second,
    dense_stitch,
    dense_stitch_first,
    dense_stitch_second,
):
    gradients = gradients_cube if lax.axis_size("batch") == CUBE else gradients_any
    (
        stitched,
        input_grad,
        filter_sums,
        filter_bias_sums,
        pool_sums,
        dense_update_outs,
        grad_dense_bias,
        grad_dense_stitch,
    ) = gradients(
        crop_maps,
        cotangent,
        crop_counts,
        filter_weight,
        conv_filter_bias,
        pool_stitch,
        dense_weight,
        dense_weight_first,
        dense_weight_second,
        dense_bias,
        dense_stitch,
    )
    updated_conv_weight, updated_conv_weight_mean, updated_conv_weight_variance = (
        decoupled_adam_step(
            filter_weight, filter_first, filter_second, filter_sums, RATE_FILTER, DECAY
        )
    )
    updated_conv_bias, updated_conv_bias_mean, updated_conv_bias_variance = decoupled_adam_step(
        conv_filter_bias,
        conv_filter_bias_mean,
        conv_filter_bias_variance,
        filter_bias_sums,
        BIAS_LEARN_RATE,
        0.0,
    )
    updated_pooling_stitch, updated_pooling_stitch_mean, updated_pooling_stitch_variance = (
        decoupled_adam_step(
            pool_stitch, pool_stitch_first, pool_stitch_second, pool_sums, RATE_STITCH, 0.0
        )
    )
    updated_dense_bias, updated_dense_bias_mean, updated_dense_bias_variance = decoupled_adam_step(
        dense_bias, dense_bias_first, dense_bias_second, grad_dense_bias[None], BIAS_LEARN_RATE, 0.0
    )
    updated_dense_stitch, updated_dense_stitch_mean, updated_dense_stitch_variance = (
        decoupled_adam_step(
            dense_stitch,
            dense_stitch_first,
            dense_stitch_second,
            grad_dense_stitch,
            RATE_STITCH,
            0.0,
        )
    )
    return (
        stitched,
        input_grad,
        updated_conv_weight,
        updated_conv_weight_mean,
        updated_conv_weight_variance,
        updated_conv_weight.astype(jnp.bfloat16),
        updated_conv_bias,
        updated_conv_bias_mean,
        updated_conv_bias_variance,
        updated_pooling_stitch,
        updated_pooling_stitch_mean,
        updated_pooling_stitch_variance,
        *dense_update_outs,
        updated_dense_bias,
        updated_dense_bias_mean,
        updated_dense_bias_variance,
        updated_dense_stitch,
        updated_dense_stitch_mean,
        updated_dense_stitch_variance,
    )


def solution(mesh):
    in_specs = (
        P(("batch", "tower"), None, None, None, None),
        P("batch", None, "tower"),
        P("batch"),
        P(("batch", "tower"), None),
        P(("batch", "tower"), None),
        P(("batch", "tower"), None),
        P(("batch", "tower")),
        P(("batch", "tower")),
        P(("batch", "tower")),
        P(("batch", "tower")),
        P(("batch", "tower")),
        P(("batch", "tower")),
        P("tower", "batch", None),
        P("tower", "batch", None),
        P("tower", "batch", None),
        P("tower", None),
        P("tower", None),
        P("tower", None),
        P(None, None, "tower"),
        P(None, None, "tower"),
        P(None, None, "tower"),
    )
    out_specs = (
        P("batch", None, "tower"),
        P(("batch", "tower"), None, None, None, None),
        P(("batch", "tower"), None),
        P(("batch", "tower"), None),
        P(("batch", "tower"), None),
        P(("batch", "tower"), None),
        P(("batch", "tower")),
        P(("batch", "tower")),
        P(("batch", "tower")),
        P(("batch", "tower")),
        P(("batch", "tower")),
        P(("batch", "tower")),
        P("tower", "batch", None),
        P("tower", "batch", None),
        P("tower", "batch", None),
        P("tower", "batch", None),
        P("tower", None),
        P("tower", None),
        P("tower", None),
        P(None, None, "tower"),
        P(None, None, "tower"),
        P(None, None, "tower"),
    )
    return jax.shard_map(local, mesh=mesh, in_specs=in_specs, out_specs=out_specs, check_vma=False)
```

```python
import functools

import jax
import jax.numpy as jnp
from jax import lax
from jax.experimental import pallas as pl
from jax.experimental.pallas import tpu as pltpu
from jax.sharding import PartitionSpec as P

STEP = 10


BETA_ONE = 0.5
BETA_TWO = 0.5
EPSILON = 1e-08
DECAY = 0.01
RATE_FILTER = 0.02
RATE_DENSE = 0.02
BIAS_LEARN_RATE = 0.05
RATE_STITCH = 0.2


def smooth_gate(values):
    return jax.nn.gelu(values, approximate=True)


def gate_slope(values):
    return jax.vjp(smooth_gate, values)[1](jnp.ones_like(values))[0]


def pool_mean(active):
    pooled_side = (active.shape[1] - 1) // 2
    span = 2 * pooled_side - 1
    total = jnp.zeros((), jnp.float32)
    for row_start in range(3):
        for col_start in range(3):
            total = total + active[:, row_start : row_start + span : 2, col_start : col_start + span : 2]
    return total / 9.0


def pool_spread(gradient, full_side):
    scaled = gradient / 9.0
    for axis in (1, 2):
        even = jnp.concatenate([scaled, jnp.zeros_like(lax.slice_in_dim(scaled, 0, 1, axis=axis))], axis)
        shifted = jnp.concatenate([jnp.zeros_like(lax.slice_in_dim(scaled, 0, 1, axis=axis)), scaled], axis)
        pairs = jnp.stack([even + shifted, even], axis + 1)
        shape = list(scaled.shape)
        shape[axis] = 2 * shape[axis] + 2
        scaled = lax.slice_in_dim(pairs.reshape(shape), 0, full_side, axis=axis)
    return scaled


def decoupled_adam_step(master, first, second, grad, rate, decay):
    first_new = BETA_ONE * first + (1.0 - BETA_ONE) * grad
    second_new = BETA_TWO * second + (1.0 - BETA_TWO) * grad * grad
    first_hat = first_new / (1.0 - BETA_ONE**STEP)
    second_hat = second_new / (1.0 - BETA_TWO**STEP)
    master_new = master - rate * (first_hat / (jnp.sqrt(second_hat) + EPSILON) + decay * master)
    return (master_new, first_new, second_new)


def core_swap(values):
    return lax.ppermute(values, "tower", [(0, 1), (1, 0)])


def by_core(core, own, other):
    return jnp.where(
        core == 0,
        jnp.concatenate([own, other], axis=-1),
        jnp.concatenate([other, own], axis=-1),
    )


def gradients_any(
    crop_maps,
    cotangent,
    crop_counts,
    filter_weight,
    conv_filter_bias,
    pool_stitch,
    dense_weight,
    dense_weight_first,
    dense_weight_second,
    dense_bias,
    dense_stitch,
):
    block_rows = crop_maps.shape[0]
    side = crop_maps.shape[2]
    in_width = crop_maps.shape[4]
    filter_rows, out_width = filter_weight.shape
    chips = lax.axis_size("batch")
    chip = lax.axis_index("batch")
    core = lax.axis_index("tower")
    totals = jnp.sum(crop_counts.reshape(2, -1), axis=1)
    slots = jnp.arange(block_rows, dtype=jnp.int32)
    mask = (slots[None, :] < totals[:, None]).astype(jnp.float32).reshape(-1)
    pair_rows = 2 * block_rows
    dense_rows, unit_width = dense_weight.shape[1:]
    half_width = unit_width // 2
    bias_width = conv_filter_bias.shape[0]
    small_width = bias_width + pool_stitch.shape[0]
    pack_rows = -(-(filter_rows + 1) // 16) * 16
    small = jnp.concatenate([conv_filter_bias, pool_stitch])
    small = jnp.pad(small, (0, (pack_rows - filter_rows) * out_width - small_width))
    packed = jnp.concatenate([filter_weight, small.reshape(-1, out_width)]).astype(jnp.bfloat16)
    gathered = lax.all_gather(packed, ("batch", "tower"), axis=0)
    filters = gathered[:, :filter_rows].reshape(2, 3, 3, in_width, out_width)
    small_full = gathered[:, filter_rows, :small_width].astype(jnp.float32)
    biases = small_full[:, :bias_width].reshape(2, out_width)
    pool_low = small_full[:, bias_width:].reshape(2, 2, out_width)
    maps = jnp.transpose(crop_maps, (1, 2, 3, 0, 4))
    grad_out = cotangent.astype(jnp.float32) * mask[:, None, None]
    own_stitch = lax.dynamic_index_in_dim(dense_stitch, core, axis=1, keepdims=False)
    other_stitch = lax.dynamic_index_in_dim(dense_stitch, 1 - core, axis=1, keepdims=False)
    own_grad = jnp.sum(own_stitch * grad_out, axis=1).astype(jnp.bfloat16)
    other_grad = core_swap(jnp.sum(other_stitch * grad_out, axis=1).astype(jnp.bfloat16))
    grad_active = by_core(core, own_grad, other_grad)
    dense_low = dense_weight[0].astype(jnp.bfloat16)
    conv = jnp.stack(
        [
            lax.conv_general_dilated(
                maps[tower],
                filters[tower],
                (1, 1),
                ((1, 1), (1, 1)),
                dimension_numbers=("HWNC", "HWIO", "HWNC"),
                preferred_element_type=jnp.float32,
            )
            for tower in range(2)
        ]
    )
    conv = conv + biases[:, None, None, None, :]
    pooled = pool_mean(smooth_gate(conv))
    pooled_side = pooled.shape[1]
    mixed = jnp.sum(pool_low[:, :, None, None, None, :] * pooled[None], axis=1).astype(jnp.bfloat16)
    mixed = jnp.transpose(mixed, (0, 3, 1, 2, 4)).reshape(2, block_rows, chips, dense_rows)
    mixed = jnp.transpose(mixed, (0, 2, 1, 3))
    own_mixed = lax.dynamic_index_in_dim(mixed, core, axis=0, keepdims=False)
    other_mixed = core_swap(lax.dynamic_index_in_dim(mixed, 1 - core, axis=0, keepdims=False))
    features = jnp.where(
        core == 0,
        jnp.concatenate([own_mixed, other_mixed], axis=1),
        jnp.concatenate([other_mixed, own_mixed], axis=1),
    )
    columns = lax.all_to_all(features, "batch", split_axis=0, concat_axis=0, tiled=True)
    columns = columns.reshape(-1, dense_rows)
    partial = jnp.dot(columns, dense_low, preferred_element_type=jnp.float32)
    hidden = lax.psum_scatter(partial, "batch", scatter_dimension=0, tiled=True) + dense_bias
    grad_hidden = (grad_active.astype(jnp.float32) * gate_slope(hidden)).astype(jnp.bfloat16)
    grad_full = lax.all_gather(grad_hidden, "batch", axis=0, tiled=True)
    active = smooth_gate(hidden).astype(jnp.bfloat16)
    own_active = lax.dynamic_slice_in_dim(active, core * half_width, half_width, axis=1)
    other_active = core_swap(
        lax.dynamic_slice_in_dim(active, (1 - core) * half_width, half_width, axis=1)
    )
    own_active = own_active.astype(jnp.float32)[:, None]
    other_active = other_active.astype(jnp.float32)[:, None]
    stitched = own_stitch * own_active + other_stitch * other_active
    stitched = (stitched * mask[:, None, None]).astype(jnp.bfloat16)
    grad_own_stitch = jnp.sum(grad_out * own_active, axis=0)
    grad_other_stitch = jnp.sum(grad_out * other_active, axis=0)
    grad_dense_stitch = lax.psum(
        jnp.where(
            core == 0,
            jnp.stack([grad_own_stitch, grad_other_stitch], axis=1),
            jnp.stack([grad_other_stitch, grad_own_stitch], axis=1),
        ),
        "batch",
    )
    grad_columns = lax.dot_general(
        grad_full, dense_low, (((1,), (1,)), ((), ())), preferred_element_type=jnp.float32
    ).astype(jnp.bfloat16)
    grad_columns = grad_columns.reshape(chips, pair_rows, dense_rows)
    returned = lax.all_to_all(grad_columns, "batch", split_axis=0, concat_axis=0, tiled=True)
    grad_dense_bias = jnp.sum(grad_full.astype(jnp.float32), axis=0)
    grad_dense_weight = lax.dot_general(
        columns, grad_full, (((0,), (0,)), ((), ())), preferred_element_type=jnp.float32
    )
    halves = returned.reshape(chips, 2, block_rows, dense_rows)
    own_mixed = lax.dynamic_index_in_dim(halves, core, axis=1, keepdims=False)
    other_mixed = core_swap(lax.dynamic_index_in_dim(halves, 1 - core, axis=1, keepdims=False))
    grad_mixed = jnp.where(
        core == 0, jnp.stack([own_mixed, other_mixed]), jnp.stack([other_mixed, own_mixed])
    )
    grad_mixed = jnp.transpose(grad_mixed, (0, 2, 1, 3)).reshape(
        2, block_rows, pooled_side, pooled_side, out_width
    )
    grad_mixed = jnp.transpose(grad_mixed, (0, 2, 3, 1, 4)).astype(jnp.float32)
    grad_pool_stitch = jnp.sum(grad_mixed[:, None] * pooled[None], axis=(2, 3, 4))
    grad_pooled = jnp.sum(pool_low[:, :, None, None, None, :] * grad_mixed[:, None], axis=0)
    grad_conv = (pool_spread(grad_pooled, side) * gate_slope(conv)).astype(jnp.bfloat16)
    grad_filter_bias = jnp.sum(grad_conv.astype(jnp.float32), axis=(1, 2, 3))
    weight_dims = lax.ConvDimensionNumbers((3, 2, 0, 1), (3, 2, 0, 1), (2, 3, 0, 1))
    grad_filter_weight = jnp.stack(
        [
            lax.conv_general_dilated(
                maps[tower],
                grad_conv[tower],
                (1, 1),
                ((1, 1), (1, 1)),
                dimension_numbers=weight_dims,
                preferred_element_type=jnp.float32,
            )
            for tower in range(2)
        ]
    )
    filter_sums = lax.psum_scatter(
        grad_filter_weight.reshape(-1, out_width),
        ("batch", "tower"),
        scatter_dimension=0,
        tiled=True,
    )
    small_grad = jnp.concatenate(
        [grad_filter_bias.reshape(2 * chips, -1), grad_pool_stitch.reshape(2 * chips, -1)], axis=1
    )
    small_grad = lax.psum(small_grad, ("batch", "tower"))
    small_grad = lax.dynamic_index_in_dim(small_grad, chip * 2 + core, axis=0, keepdims=False)
    filter_bias_sums = small_grad[:bias_width]
    pool_sums = small_grad[bias_width:]
    input_grad = jnp.stack(
        [
            lax.conv_general_dilated(
                grad_conv[tower],
                filters[tower][::-1, ::-1],
                (1, 1),
                ((1, 1), (1, 1)),
                dimension_numbers=("HWNC", "HWOI", "HWNC"),
                preferred_element_type=jnp.float32,
            ).astype(jnp.bfloat16)
            for tower in range(2)
        ]
    )
    input_grad = jnp.transpose(input_grad, (3, 0, 1, 2, 4))
    update = decoupled_adam_step(
        dense_weight, dense_weight_first, dense_weight_second, grad_dense_weight[None], RATE_DENSE, DECAY
    )
    return (
        stitched,
        input_grad,
        filter_sums,
        filter_bias_sums,
        pool_sums,
        (*update, update[0].astype(jnp.bfloat16)),
        grad_dense_bias,
        grad_dense_stitch,
    )


CUBE = 16
LANES = 128
VMEM_ASKED = 8 << 20
GELU_SCALE = 0.7978845608028654
GELU_CUBIC = 0.044715


def hop(values, level):
    return lax.ppermute(values, "batch", [(i, i ^ (4 * level)) for i in range(CUBE)])


def plane_hop(values, offset):
    return lax.ppermute(values, "batch", [(i, i ^ offset) for i in range(CUBE)])


SIDES = ((0, 1, 2, 3), (0, 2, 1, 3))


def zero_of(values):
    first = values[(0,) * values.ndim]
    return (first != first).astype(jnp.int32)


def held(values, *others):
    zero = sum(zero_of(other) for other in others)
    return jnp.where(zero == 0, values, jnp.zeros((), values.dtype))


def gather_levels(block):
    return [hop(block, level) if level else block for level in range(4)]


def gather_plane(tops, *others):
    groups, halves = [], []
    for group in range(2):
        own = jnp.stack(tops[2 * group : 2 * group + 2])
        if group and others:
            own = held(own, *others)
        half = jnp.stack([own, plane_hop(own, SIDES[group][1])])
        halves.append(half)
        groups.append(jnp.concatenate([half, plane_hop(half, SIDES[group][2])]))
    return groups, halves


def reduce_first(parts, group):
    sent = plane_hop(parts[2:], SIDES[group][2])
    return parts[:2].astype(jnp.float32) + sent.astype(jnp.float32)


def reduce_second(kept, group):
    sent = plane_hop(kept[1].astype(jnp.bfloat16), SIDES[group][1])
    return kept[0] + sent.astype(jnp.float32)


def reduce_levels(groups):
    total = groups[0][0]
    for level in (1, 2, 3):
        part = hop(groups[level // 2][level % 2].astype(jnp.bfloat16), level)
        total = total + part.astype(jnp.float32)
    return total


def on_chip():
    return pl.BlockSpec(memory_space=pltpu.VMEM)


def turn(values):
    return pltpu.roll(values, LANES // 2, axis=1)


def mix_kernel(
    maps_a,
    maps_b,
    small,
    pooled,
    sent,
    row_sums,
    means,
):
    side, width, crops, channels = maps_a.shape
    count = (width - 1) // 2

    def gate_row(y, carry):
        for tower, maps in enumerate((maps_a, maps_b)):
            bias = small[tower][None]
            running = [None] * count
            for x in range(width):
                value = maps[y, x].astype(jnp.float32) + bias
                square = value * value
                bend = jnp.tanh(GELU_SCALE * value * (1.0 + GELU_CUBIC * square))
                half = 0.5 + 0.5 * bend
                gate = value * half
                for place_x in range(max(0, (x - 1) // 2), min(count - 1, x // 2) + 1):
                    old = running[place_x]
                    running[place_x] = gate if old is None else old + gate
            for place_x in range(count):
                row_sums[tower, y, place_x] = running[place_x]
        return carry

    lax.fori_loop(0, side, gate_row, 0)

    def mean_row(row, carry):
        for tower in range(2):
            for place_x in range(count):
                mean = (
                    row_sums[tower, 2 * row, place_x]
                    + row_sums[tower, 2 * row + 1, place_x]
                    + row_sums[tower, 2 * row + 2, place_x]
                ) * (1.0 / 9.0)
                means[tower, row * count + place_x] = mean
                pooled[tower, row * count + place_x] = mean.astype(jnp.bfloat16)
        return carry

    lax.fori_loop(0, count, mean_row, 0)
    low_lanes = lax.broadcasted_iota(jnp.int32, (crops, LANES), 1) < LANES // 2
    halves = small.shape[1] // LANES
    for pair in range(CUBE // 2):
        for tower in range(2):
            tiles = []
            for tile in range(9 * pair, 9 * pair + 9):
                cell, first = tile // halves, tile % halves * LANES
                lanes = slice(first, first + LANES)
                tiles.append(
                    small[2 + 2 * tower, lanes][None] * means[0, cell, :, lanes]
                    + small[3 + 2 * tower, lanes][None] * means[1, cell, :, lanes]
                )
            turned = [turn(tile) for tile in tiles[4:]]
            blank = jnp.zeros_like(tiles[0])
            even = tiles[:4] + [jnp.where(low_lanes, tiles[4], blank)]
            odd = [jnp.where(low_lanes, turned[q], turned[q + 1]) for q in range(4)]
            odd.append(jnp.where(low_lanes, turned[4], blank))
            for chunk, pieces in ((2 * pair, even), (2 * pair + 1, odd)):
                for q, piece in enumerate(pieces):
                    lanes = slice(q * LANES, (q + 1) * LANES)
                    sent[2 * chunk + tower, :, lanes] = piece.astype(jnp.bfloat16)


def mix(conv, small, wide):
    side, _, crops, width = conv[0].shape
    count = (side - 1) // 2
    cells = count * count
    pooled = jax.ShapeDtypeStruct((2, cells, crops, width), jnp.bfloat16)
    sent = jax.ShapeDtypeStruct((2 * CUBE, crops, wide), jnp.bfloat16)
    return pl.pallas_call(
        mix_kernel,
        out_shape=(pooled, sent),
        in_specs=[on_chip()] * 3,
        out_specs=(on_chip(),) * 2,
        scratch_shapes=[
            pltpu.VMEM((2, side, count, crops, width), jnp.float32),
            pltpu.VMEM((2, cells, crops, width), jnp.float32),
        ],
        compiler_params=pltpu.CompilerParams(vmem_limit_bytes=VMEM_ASKED),
        cost_estimate=pl.CostEstimate(
            flops=60 * conv[0].size,
            bytes_accessed=12 * conv[0].size,
            transcendentals=2 * conv[0].size,
        ),
        name="gate_pool_mix",
    )(conv[0], conv[1], small)


def slope_kernel(maps_a, maps_b, small, slope_a, slope_b):
    side, width = maps_a.shape[:2]

    def row(y, carry):
        for tower, (maps, slopes) in enumerate(((maps_a, slope_a), (maps_b, slope_b))):
            bias = small[tower][None]
            for x in range(width):
                value = maps[y, x].astype(jnp.float32) + bias
                square = value * value
                bend = jnp.tanh(GELU_SCALE * value * (1.0 + GELU_CUBIC * square))
                rise = GELU_SCALE * (1.0 + 3.0 * GELU_CUBIC * square)
                slope = 0.5 + 0.5 * bend + 0.5 * value * (1.0 - bend * bend) * rise
                slopes[y, x] = slope.astype(jnp.bfloat16)
        return carry

    lax.fori_loop(0, side, row, 0)


def gate_slopes(conv, small):
    slope = jax.ShapeDtypeStruct(conv[0].shape, jnp.bfloat16)
    return pl.pallas_call(
        slope_kernel,
        out_shape=(slope, slope),
        in_specs=[on_chip()] * 3,
        out_specs=(on_chip(),) * 2,
        compiler_params=pltpu.CompilerParams(vmem_limit_bytes=VMEM_ASKED),
        cost_estimate=pl.CostEstimate(
            flops=40 * conv[0].size, bytes_accessed=8 * conv[0].size, transcendentals=2 * conv[0].size
        ),
        name="gate_slope",
    )(conv[0], conv[1], small)


def back_kernel(
    returned,
    pooled,
    small,
    slope_a,
    slope_b,
    grad_a,
    grad_b,
    grad_small,
    mixed,
    spread,
):
    side, width, crops, channels = slope_a.shape
    count = (width - 1) // 2
    halves = channels // LANES
    low_lanes = lax.broadcasted_iota(jnp.int32, (crops, LANES), 1) < LANES // 2
    for pair in range(CUBE // 2):
        for tower in range(2):
            loaded = []
            for chunk in (2 * pair, 2 * pair + 1):
                source = 2 * chunk + tower
                pieces = []
                for q in range(5):
                    lanes = slice(q * LANES, (q + 1) * LANES)
                    pieces.append(returned[source, :, lanes].astype(jnp.float32))
                loaded.append(pieces)
            even, odd = loaded
            turned = [turn(tile) for tile in odd]
            tiles = even[:4] + [jnp.where(low_lanes, even[4], turned[0])]
            tiles += [jnp.where(low_lanes, turned[q], turned[q + 1]) for q in range(4)]
            for q, tile in enumerate(tiles):
                first = (9 * pair + q) % halves * LANES
                mixed[tower, (9 * pair + q) // halves, :, first : first + LANES] = tile
    blank = jnp.zeros((crops, channels), jnp.float32)
    for tower in range(2):
        for place_x in range(count):
            spread[tower, 0, place_x] = blank
            spread[tower, count + 1, place_x] = blank

    def unmix(row, totals):
        totals = list(totals)
        for place_x in range(count):
            cell = row * count + place_x
            grads = [mixed[tower, cell] for tower in range(2)]
            values = [pooled[tower, cell].astype(jnp.float32) for tower in range(2)]
            for i in range(2):
                for j in range(2):
                    totals[2 * i + j] = totals[2 * i + j] + grads[i] * values[j]
            for j in range(2):
                spread[j, row + 1, place_x] = (
                    small[2 + j][None] * grads[0] + small[4 + j][None] * grads[1]
                ) * (1.0 / 9.0)
        return tuple(totals)

    totals = lax.fori_loop(0, count, unmix, (blank,) * 4)
    for which in range(4):
        grad_small[2 + which] = jnp.sum(totals[which], axis=0)

    def spread_row(y, totals):
        totals = list(totals)
        row = y // 2
        both = (1 - y % 2).astype(jnp.float32)
        for tower, (slopes, grads) in enumerate(((slope_a, grad_a), (slope_b, grad_b))):
            line = [
                spread[tower, row + 1, place_x] + both * spread[tower, row, place_x]
                for place_x in range(count)
            ]
            for x in range(width):
                near = [line[q] for q in range(max(0, (x - 1) // 2), min(count - 1, x // 2) + 1)]
                value = near[0] if len(near) == 1 else near[0] + near[1]
                value = (value * slopes[y, x].astype(jnp.float32)).astype(jnp.bfloat16)
                grads[y, x] = value
                totals[tower] = totals[tower] + value.astype(jnp.float32)
        return tuple(totals)

    totals = lax.fori_loop(0, side, spread_row, (blank,) * 2)
    for tower in range(2):
        grad_small[tower] = jnp.sum(totals[tower], axis=0)


def back(returned, pooled, small, slopes):
    side, _, crops, width = slopes[0].shape
    count = (side - 1) // 2
    grad = jax.ShapeDtypeStruct(slopes[0].shape, jnp.bfloat16)
    return pl.pallas_call(
        back_kernel,
        out_shape=(grad, grad, jax.ShapeDtypeStruct((6, width), jnp.float32)),
        in_specs=[on_chip()] * 5,
        out_specs=(on_chip(),) * 3,
        scratch_shapes=[
            pltpu.VMEM((2, count * count, crops, width), jnp.float32),
            pltpu.VMEM((2, count + 2, count, crops, width), jnp.float32),
        ],
        compiler_params=pltpu.CompilerParams(vmem_limit_bytes=VMEM_ASKED),
        cost_estimate=pl.CostEstimate(
            flops=20 * slopes[0].size, bytes_accessed=8 * slopes[0].size, transcendentals=0
        ),
        name="pool_gradient",
    )(returned, pooled, small, slopes[0], slopes[1])


def low_kernel(weight, low):
    rows = weight.shape[1]
    low[:rows] = weight[0].astype(jnp.bfloat16)
    low[rows:] = jnp.zeros((low.shape[0] - rows, low.shape[1]), jnp.bfloat16)


def low_half(weight, part, wide):
    tile = 1024
    _, rows, units = weight.shape
    steps = units // 2 // tile
    return pl.pallas_call(
        low_kernel,
        grid=(steps,),
        out_shape=jax.ShapeDtypeStruct((wide, units // 2), jnp.bfloat16),
        in_specs=[pl.BlockSpec((1, rows, tile), lambda step: (0, 0, part * steps + step))],
        out_specs=pl.BlockSpec((wide, tile), lambda step: (0, step)),
        compiler_params=pltpu.CompilerParams(vmem_limit_bytes=16 << 20),
        cost_estimate=pl.CostEstimate(
            flops=rows * units // 2, bytes_accessed=3 * rows * units, transcendentals=0
        ),
        name="low_half",
    )(weight)


def order_kernel(place, *refs):
    back = len(refs) == 4
    blocks, groups = (refs[3], refs[:2]) if back else (refs[0], refs[1:])
    chip = 4 * place[0] + place[1]
    rows = blocks.shape[1]
    last = blocks.shape[2] - LANES
    for group in range(2):
        for side in range(4):
            for level in range(2):
                at = chip ^ (4 * (2 * group + level) + SIDES[group][side])
                start = (2 * side + level) * rows
                if back:
                    half = rows // 2
                    for first in (start, start + half):
                        into = pl.ds(first - start, half)
                        blocks[at, into, :last] = groups[group][first : first + half, :last]
                        blocks[at, into, last:] = groups[group][first : first + half, last:] + refs[2][...]
                else:
                    groups[group][start : start + rows] = blocks[at]


def order_rows(place, *arrays):
    if len(arrays) == 1:
        _, rows, width = arrays[0].shape
        outs = [jax.ShapeDtypeStruct((CUBE // 2 * rows, width), arrays[0].dtype)] * 2
    else:
        rows, width = arrays[0].shape
        outs = jax.ShapeDtypeStruct((CUBE, rows // (CUBE // 2), width), arrays[0].dtype)
    size = arrays[0].size * (1 if len(arrays) == 1 else 2)
    return pl.pallas_call(
        order_kernel,
        out_shape=outs,
        in_specs=[pl.BlockSpec(memory_space=pltpu.SMEM)] + [on_chip()] * len(arrays),
        out_specs=[on_chip()] * 2 if len(arrays) == 1 else on_chip(),
        compiler_params=pltpu.CompilerParams(vmem_limit_bytes=VMEM_ASKED),
        cost_estimate=pl.CostEstimate(flops=size, bytes_accessed=4 * size, transcendentals=0),
        name="order_rows",
    )(place, *arrays)


def pair_kernel(place, own, other, blocks_a, blocks_b):
    chip = 4 * place[0] + place[1]
    for group, blocks in enumerate((blocks_a, blocks_b)):
        for side in range(4):
            for level in range(2):
                source = chip ^ (4 * (2 * group + level) + SIDES[group][side])
                total = own[source].astype(jnp.float32) + other[source].astype(jnp.float32)
                blocks[side, level] = total.astype(jnp.bfloat16)


def pair_blocks(place, own, other):
    blocks = jax.ShapeDtypeStruct((4, 2) + own.shape[1:], own.dtype)
    return pl.pallas_call(
        pair_kernel,
        out_shape=(blocks, blocks),
        in_specs=[pl.BlockSpec(memory_space=pltpu.SMEM), on_chip(), on_chip()],
        out_specs=(on_chip(), on_chip()),
        compiler_params=pltpu.CompilerParams(vmem_limit_bytes=VMEM_ASKED),
        cost_estimate=pl.CostEstimate(
            flops=own.size, bytes_accessed=6 * own.size, transcendentals=0
        ),
        name="pair_blocks",
    )(place, own, other)


def dense_kernel(columns_a, columns_b, *refs):
    weight, first, second, new_weight, new_first, new_second, copy, grad_bias = refs[4:]
    early = pl.program_id(0) < pl.num_programs(0) // 2
    grads = [jnp.where(early, refs[group][...], refs[2 + group][...]) for group in range(2)]
    grad = sum(
        lax.dot_general(
            columns[...], part, (((0,), (0,)), ((), ())), preferred_element_type=jnp.float32
        )
        for columns, part in zip((columns_a, columns_b), grads)
    )
    updated, mean, square = decoupled_adam_step(
        weight[0], first[0], second[0], grad[: weight.shape[1]], RATE_DENSE, DECAY
    )
    new_weight[0] = updated
    new_first[0] = mean
    new_second[0] = square
    copy[0] = updated.astype(jnp.bfloat16)
    grad_bias[...] = jnp.sum(
        grads[0].astype(jnp.float32) + grads[1].astype(jnp.float32), axis=0, keepdims=True
    )


def dense_update(columns, grads, weight, first, second):
    tile = 1024
    _, rows, units = weight.shape
    steps = units // tile
    half = steps // 2
    state = pl.BlockSpec((1, rows, tile), lambda step: (0, 0, step))
    block = (grads[0][0].shape[0], tile)
    early = pl.BlockSpec(block, lambda step: (0, jnp.minimum(step, half - 1)))
    late = pl.BlockSpec(block, lambda step: (0, jnp.maximum(step - half, 0)))
    outs = [jax.ShapeDtypeStruct(weight.shape, jnp.float32)] * 3
    outs += [
        jax.ShapeDtypeStruct(weight.shape, jnp.bfloat16),
        jax.ShapeDtypeStruct((1, units), jnp.float32),
    ]
    return pl.pallas_call(
        dense_kernel,
        grid=(steps,),
        out_shape=outs,
        in_specs=[
            *[pl.BlockSpec(columns[0].shape, lambda step: (0, 0))] * 2,
            early,
            early,
            late,
            late,
            state,
            state,
            state,
        ],
        out_specs=[state] * 4 + [pl.BlockSpec((1, tile), lambda step: (0, step))],
        compiler_params=pltpu.CompilerParams(vmem_limit_bytes=48 << 20),
        cost_estimate=pl.CostEstimate(
            flops=4 * columns[0].size * units,
            bytes_accessed=26 * weight.size,
            transcendentals=weight.size,
        ),
        name="dense_update",
    )(*columns, *grads[0], *grads[1], weight, first, second)


def gradients_cube(
    crop_maps,
    cotangent,
    crop_counts,
    filter_weight,
    conv_filter_bias,
    pool_stitch,
    dense_weight,
    dense_weight_first,
    dense_weight_second,
    dense_bias,
    dense_stitch,
):
    crops = crop_maps.shape[0]
    in_width = crop_maps.shape[4]
    filter_rows, out_width = filter_weight.shape
    chip, core = lax.axis_index("batch"), lax.axis_index("tower")
    own_level, own_plane = chip // 4, chip % 4
    place = jnp.stack([own_level, own_plane, core]).astype(jnp.int32)
    totals = jnp.sum(crop_counts.reshape(2, -1), axis=1)
    slots = jnp.arange(crops, dtype=jnp.int32)
    mask = (slots[None, :] < totals[:, None]).astype(jnp.float32).reshape(-1)
    rows = 2 * crops
    dense_rows, unit_width = dense_weight.shape[1:]
    half_width = unit_width // 2
    wide = -(-dense_rows // LANES) * LANES
    bias_width = conv_filter_bias.shape[0]
    small_width = bias_width + pool_stitch.shape[0]
    pack_rows = -(-(filter_rows + 1) // 16) * 16
    small = jnp.concatenate([conv_filter_bias, pool_stitch])
    small = jnp.pad(small, (0, (pack_rows - filter_rows) * out_width - small_width))
    packed = jnp.concatenate([filter_weight, small.reshape(-1, out_width)]).astype(jnp.bfloat16)
    maps = jnp.transpose(crop_maps, (1, 2, 3, 0, 4))
    tops = gather_levels(packed)
    own_packed = jnp.zeros((CUBE,) + packed.shape, packed.dtype)
    for group, blocks in enumerate(gather_plane(tops)[0]):
        for side in range(4):
            for level in range(2):
                owner = chip ^ (4 * (2 * group + level) + SIDES[group][side])
                own_packed = lax.dynamic_update_slice(
                    own_packed, blocks[side, level][None], (owner, 0, 0)
                )
    other_packed = core_swap(own_packed)
    gathered = jnp.where(
        core == 0,
        jnp.stack([own_packed, other_packed], axis=1),
        jnp.stack([other_packed, own_packed], axis=1),
    ).reshape(2 * CUBE, pack_rows, out_width)
    filters = gathered[:, :filter_rows].reshape(2, 3, 3, in_width, out_width)
    small_full = gathered[:, filter_rows, :small_width].astype(jnp.float32)
    smalls = jnp.concatenate(
        [
            small_full[:, :bias_width].reshape(2, out_width),
            small_full[:, bias_width:].reshape(4, out_width),
        ]
    )
    conv = [
        lax.conv_general_dilated(
            maps[tower],
            filters[tower],
            (1, 1),
            ((1, 1), (1, 1)),
            dimension_numbers=("HWNC", "HWIO", "HWNC"),
            preferred_element_type=jnp.float32,
        ).astype(jnp.bfloat16)
        for tower in range(2)
    ]
    pooled, sent = mix(conv, smalls, wide)
    slope_a, slope_b = gate_slopes(conv, smalls)
    arrived = lax.all_to_all(sent, ("batch", "tower"), split_axis=0, concat_axis=0, tiled=True)
    arrived = arrived.reshape(CUBE, rows, wide)
    dense_low = [low_half(dense_weight, part, wide) for part in range(2)]
    columns = order_rows(held(place, slope_a), arrived)
    grad_out = cotangent.astype(jnp.float32) * mask[:, None, None]
    own_stitch = lax.dynamic_index_in_dim(dense_stitch, core, axis=1, keepdims=False)
    other_stitch = lax.dynamic_index_in_dim(dense_stitch, 1 - core, axis=1, keepdims=False)
    own_grad = jnp.sum(own_stitch * grad_out, axis=1).astype(jnp.bfloat16)
    other_grad = core_swap(jnp.sum(other_stitch * grad_out, axis=1).astype(jnp.bfloat16))
    grad_active = [jnp.where(core == part, own_grad, other_grad) for part in range(2)]
    kept, sums = [], [[], []]
    for part in range(2):
        for group in range(2):
            partial = jnp.dot(columns[group], dense_low[part], preferred_element_type=jnp.float32)
            if part:
                partial = held(partial, kept[group])
            partial = partial.astype(jnp.bfloat16).reshape(4, 2, rows, half_width)
            first_sum = reduce_first(partial, group)
            kept.append(first_sum)
            sums[part].append(reduce_second(first_sum, group))
    hidden, grad_full = [], []
    for part in range(2):
        units = slice(part * half_width, (part + 1) * half_width)
        if part:
            sums[1] = [held(group, hidden[0]) for group in sums[1]]
        total = reduce_levels(sums[part]) + dense_bias[:, units]
        if part:
            total = held(total, tops[1])
        hidden.append(total)
        grad_hidden = grad_active[part].astype(jnp.float32) * gate_slope(total)
        tops = gather_levels(grad_hidden.astype(jnp.bfloat16))
        gathered, halves = gather_plane(tops)
        grad_full.append([group.reshape(8 * rows, half_width) for group in gathered])
    active = [smooth_gate(half).astype(jnp.bfloat16) for half in hidden]
    own_active = jnp.where(core == 0, active[0], active[1])
    other_active = core_swap(jnp.where(core == 0, active[1], active[0]))
    own_active = own_active.astype(jnp.float32)[:, None]
    other_active = other_active.astype(jnp.float32)[:, None]
    stitched = own_stitch * own_active + other_stitch * other_active
    stitched = (stitched * mask[:, None, None]).astype(jnp.bfloat16)
    grad_own_stitch = jnp.sum(grad_out * own_active, axis=0)
    grad_other_stitch = jnp.sum(grad_out * other_active, axis=0)
    grad_dense_stitch = jnp.where(
        core == 0,
        jnp.stack([grad_own_stitch, grad_other_stitch], axis=1),
        jnp.stack([grad_other_stitch, grad_own_stitch], axis=1),
    )
    share = lax.all_to_all(
        grad_dense_stitch.reshape(CUBE, -1), "batch", split_axis=0, concat_axis=0, tiled=True
    )
    share = jnp.sum(share, axis=0)
    high = lax.reduce_precision(share, 8, 7)
    share = jnp.concatenate([high, share - high]).reshape(crops, -1)
    share = jnp.pad(share, ((0, 0), (LANES - share.shape[1], 0))).astype(jnp.bfloat16)
    sent = [
        sum(
            lax.dot_general(
                grad_full[part][group],
                dense_low[part],
                (((1,), (1,)), ((), ())),
                preferred_element_type=jnp.float32,
            )
            for part in range(2)
        ).astype(jnp.bfloat16)
        for group in range(2)
    ]
    sent = order_rows(place, *sent, share).reshape(2 * CUBE, crops, wide)
    returned = lax.all_to_all(sent, ("batch", "tower"), split_axis=0, concat_axis=0, tiled=True)
    share = returned.reshape(CUBE, 2, crops, wide)[:, :, :, dense_rows:]
    share = jnp.where(core == 0, share[:, 0], share[:, 1]).astype(jnp.float32).reshape(CUBE, 2, -1)
    grad_dense_stitch = (share[:, 0] + share[:, 1]).reshape(grad_dense_stitch.shape)
    update = dense_update(
        columns, grad_full, dense_weight, dense_weight_first, dense_weight_second
    )
    small_held = held(smalls, update[4])
    grad_a, grad_b, grad_small = back(returned, pooled, small_held, (slope_a, slope_b))
    grad_conv = (grad_a, grad_b)
    weight_dims = lax.ConvDimensionNumbers((3, 2, 0, 1), (3, 2, 0, 1), (2, 3, 0, 1))
    grad_filter_weight = [
        lax.conv_general_dilated(
            maps[tower],
            grad_conv[tower],
            (1, 1),
            ((1, 1), (1, 1)),
            dimension_numbers=weight_dims,
            preferred_element_type=jnp.float32,
        )
        .astype(jnp.bfloat16)
        .reshape(CUBE // 2, 2, filter_rows, out_width)
        for tower in range(2)
    ]
    small_grad = jnp.concatenate(
        [grad_small[:2].reshape(2 * CUBE, -1), grad_small[2:].reshape(2 * CUBE, -1)], axis=1
    )
    scales = 1.0 + jnp.arange(8, dtype=jnp.float32)[:, None] / 8.0
    small_grad = jnp.pad(small_grad[:, None] * scales, ((0, 0), (0, 0), (0, out_width - small_width)))
    small_grad = small_grad.astype(jnp.bfloat16).reshape(CUBE, 2, 8, out_width)
    own_filters, other_filters = (
        jnp.concatenate(
            [
                jnp.concatenate(
                    [
                        lax.dynamic_index_in_dim(
                            grad_filter_weight[tower], which, axis=1, keepdims=False
                        )
                        for tower in range(2)
                    ]
                ),
                lax.dynamic_index_in_dim(small_grad, which, axis=1, keepdims=False),
            ],
            axis=1,
        )
        for which in (core, 1 - core)
    )
    blocks = pair_blocks(place, own_filters, core_swap(other_filters))
    firsts = [reduce_first(blocks[group], group) for group in range(2)]
    groups = [reduce_second(firsts[group], group) for group in range(2)]
    block_sums = reduce_levels(groups)
    filter_sums = block_sums[:filter_rows]
    small_sums = jnp.mean(block_sums[filter_rows:] / scales, axis=0)
    input_grad = jnp.stack(
        [
            held(
                lax.conv_general_dilated(
                    grad_conv[tower],
                    filters[tower][::-1, ::-1],
                    (1, 1),
                    ((1, 1), (1, 1)),
                    dimension_numbers=("HWNC", "HWOI", "HWNC"),
                    preferred_element_type=jnp.float32,
                ),
                (blocks[1] if tower == 0 else firsts[1]),
            ).astype(jnp.bfloat16)
            for tower in range(2)
        ]
    )
    input_grad = jnp.transpose(input_grad, (3, 0, 1, 2, 4))
    return (
        stitched,
        input_grad,
        filter_sums,
        small_sums[:bias_width],
        small_sums[bias_width:small_width],
        update[:4],
        update[4][0],
        grad_dense_stitch,
    )


def local(
    crop_maps,
    cotangent,
    crop_counts,
    filter_weight,
    filter_first,
    filter_second,
    conv_filter_bias,
    conv_filter_bias_mean,
    conv_filter_bias_variance,
    pool_stitch,
    pool_stitch_first,
    pool_stitch_second,
    dense_weight,
    dense_weight_first,
    dense_weight_second,
    dense_bias,
    dense_bias_first,
    dense_bias_second,
    dense_stitch,
    dense_stitch_first,
    dense_stitch_second,
):
    gradients = gradients_cube if lax.axis_size("batch") == CUBE else gradients_any
    (
        stitched,
        input_grad,
        filter_sums,
        filter_bias_sums,
        pool_sums,
        dense_update_outs,
        grad_dense_bias,
        grad_dense_stitch,
    ) = gradients(
        crop_maps,
        cotangent,
        crop_counts,
        filter_weight,
        conv_filter_bias,
        pool_stitch,
        dense_weight,
        dense_weight_first,
        dense_weight_second,
        dense_bias,
        dense_stitch,
    )
    updated_conv_weight, updated_conv_weight_mean, updated_conv_weight_variance = (
        decoupled_adam_step(
            filter_weight, filter_first, filter_second, filter_sums, RATE_FILTER, DECAY
        )
    )
    updated_conv_bias, updated_conv_bias_mean, updated_conv_bias_variance = decoupled_adam_step(
        conv_filter_bias,
        conv_filter_bias_mean,
        conv_filter_bias_variance,
        filter_bias_sums,
        BIAS_LEARN_RATE,
        0.0,
    )
    updated_pooling_stitch, updated_pooling_stitch_mean, updated_pooling_stitch_variance = (
        decoupled_adam_step(
            pool_stitch, pool_stitch_first, pool_stitch_second, pool_sums, RATE_STITCH, 0.0
        )
    )
    updated_dense_bias, updated_dense_bias_mean, updated_dense_bias_variance = decoupled_adam_step(
        dense_bias, dense_bias_first, dense_bias_second, grad_dense_bias[None], BIAS_LEARN_RATE, 0.0
    )
    updated_dense_stitch, updated_dense_stitch_mean, updated_dense_stitch_variance = (
        decoupled_adam_step(
            dense_stitch,
            dense_stitch_first,
            dense_stitch_second,
            grad_dense_stitch,
            RATE_STITCH,
            0.0,
        )
    )
    return (
        stitched,
        input_grad,
        updated_conv_weight,
        updated_conv_weight_mean,
        updated_conv_weight_variance,
        updated_conv_weight.astype(jnp.bfloat16),
        updated_conv_bias,
        updated_conv_bias_mean,
        updated_conv_bias_variance,
        updated_pooling_stitch,
        updated_pooling_stitch_mean,
        updated_pooling_stitch_variance,
        *dense_update_outs,
        updated_dense_bias,
        updated_dense_bias_mean,
        updated_dense_bias_variance,
        updated_dense_stitch,
        updated_dense_stitch_mean,
        updated_dense_stitch_variance,
    )


def solution(mesh):
    in_specs = (
        P(("batch", "tower"), None, None, None, None),
        P("batch", None, "tower"),
        P("batch"),
        P(("batch", "tower"), None),
        P(("batch", "tower"), None),
        P(("batch", "tower"), None),
        P(("batch", "tower")),
        P(("batch", "tower")),
        P(("batch", "tower")),
        P(("batch", "tower")),
        P(("batch", "tower")),
        P(("batch", "tower")),
        P("tower", "batch", None),
        P("tower", "batch", None),
        P("tower", "batch", None),
        P("tower", None),
        P("tower", None),
        P("tower", None),
        P(None, None, "tower"),
        P(None, None, "tower"),
        P(None, None, "tower"),
    )
    out_specs = (
        P("batch", None, "tower"),
        P(("batch", "tower"), None, None, None, None),
        P(("batch", "tower"), None),
        P(("batch", "tower"), None),
        P(("batch", "tower"), None),
        P(("batch", "tower"), None),
        P(("batch", "tower")),
        P(("batch", "tower")),
        P(("batch", "tower")),
        P(("batch", "tower")),
        P(("batch", "tower")),
        P(("batch", "tower")),
        P("tower", "batch", None),
        P("tower", "batch", None),
        P("tower", "batch", None),
        P("tower", "batch", None),
        P("tower", None),
        P("tower", None),
        P("tower", None),
        P(None, None, "tower"),
        P(None, None, "tower"),
        P(None, None, "tower"),
    )
    return jax.shard_map(local, mesh=mesh, in_specs=in_specs, out_specs=out_specs, check_vma=False)
```
